32 devices in a mesh: parts: 2 (over y), ep: 16 (over z, x, core), tp: 1.
Axes of the slice: x: 2, y: 2, z: 4, core: 2. Of those that a mesh axis runs over, the one named last changes fastest.
Arguments:
- tokens: bfloat16 [2048, 3584], P(('parts', 'ep'), 'tp'), parts along dimension 0, may hold values from -6 to 6
- expert_ids: int32 [2048, 8], P(('parts', 'ep')), parts along dimension 0, may hold values from 0 to 15, all different within a row; in each aligned block of 64 rows (0 to 63, 64 to 127, ...) at most 48 rows name the same one
- gate_weights: float32 [2048, 8], P(('parts', 'ep')), parts along dimension 0, may hold values from 0.05 to 1
- w_gate: bfloat16 [16, 3584, 1024], P(None, 'ep', 'tp'), may hold values from -0.09375 to 0.09375
- w_up: bfloat16 [16, 3584, 1024], P(None, 'ep', 'tp'), may hold values from -0.09375 to 0.09375
- w_down: bfloat16 [16, 1024, 3584], P(None, 'tp', 'ep'), may hold values from -0.1875 to 0.1875
Outputs:
- mixed: bfloat16 [2048, 3584], P(('parts', 'ep'), 'tp'), parts along dimension 0
The draws below stay inside these ranges and needn't reach their ends.
There are 2 independent parts, one for each index of `parts`. The reference program is written for one: setup_inputs(seed, part) draws one part's arguments, and reference() takes and returns one part's arrays. A program takes and returns all parts, laid end to end along the dimension named above; an argument that names none is the same for every part. Nothing has to cross between parts.
Inputs may be any that keep to these rules, and one draw needn't show every extreme that they name: `expert_ids`: each row names 8 different experts; within the rows of one block of 64 rows no expert is named by more than 48 rows, a bound that some block reaches.
All inputs are finite; a program needn't handle non-finite values.
Results may differ from the reference program's by a relative error of at most 0.015.
Values may be sent and summed in bfloat16 or wider, within the bound.
No kernel may reach another device: no remote copies, remote signals or barrier semaphores. Data moves between devices by JAX's collectives and lax.ppermute only.
A program may use at most 128 MiB of HBM per device.

```python
import math
import jax
import jax.numpy as jnp
import numpy as np
from jax import lax

D = 3584
F = 1024
TOP = 8
TOK_DEV = 64
EXPERTS = 16
TOKENS = 1024
CS = 48
N_EP = 16


def steps_of(stream_key, extent, pieces, least, high):
    factor_of, own = 1.0, jax.random.fold_in(stream_key, 6)
    for dim, parts in pieces:
        draws = jnp.exp(jax.random.uniform(jax.random.fold_in(own, dim), (parts,), jnp.float32, least / len(pieces), high / len(pieces)))
        factor_of = factor_of * jnp.repeat(draws, extent[dim] // parts).reshape([-1 if axis == dim else 1 for axis in range(len(extent))])
    return factor_of


def routed_block(stream_key, own, number, rows, count, top, limit, lean):
    order = jax.random.permutation(stream_key, count)
    packed, common = load_shares(count, rows * top, limit, lean, True), load_shares(count, rows * top, limit, lean, False)
    places = jnp.arange(count)

    def named(lengths, rotation):
        used = int((lengths > 0).sum())
        fixed = max(1, used // 4)
        moved = fixed + (places - fixed + rotation * (used - fixed)) % max(1, count - fixed)
        return jnp.zeros((count,), jnp.int32).at[order[jnp.where(places < fixed, places, moved)]].set(jnp.asarray(lengths, jnp.int32))

    lengths = jnp.where(number % 4 == 0, named(packed, number // 4), named(common, number - number // 4 - 1))
    mixed = jax.random.permutation(jax.random.fold_in(own, 3), count)
    donor, sink = mixed[0:count // 2 * 2:2], mixed[1:count // 2 * 2:2]
    room = jnp.minimum(lengths[donor] - 1, limit - lengths[sink]) // 2
    room = jnp.where((donor == order[0]) | (sink == order[0]) | (lengths[sink] == 0), 0, jnp.maximum(room, 0))
    moved = jax.random.randint(jax.random.fold_in(own, 4), (count // 2,), 0, 1 << 20) % (room + 1)
    lengths = lengths.at[donor].add(-moved).at[sink].add(moved)
    labels = jnp.searchsorted(jnp.cumsum(lengths), jnp.arange(rows * top), side="right").astype(jnp.int32)
    listing = labels.reshape(top, rows).T
    listing = listing[jax.random.permutation(jax.random.fold_in(own, 1), rows)]
    rotation = jax.random.randint(jax.random.fold_in(own, 2), (rows, 1), 0, top)
    return jnp.take_along_axis(listing, (jnp.arange(top)[None, :] + rotation) % top, axis=1)


def load_shares(amount, total, limit, skew, full):
    portions = [(1 << 20) // math.isqrt(rank ** skew) + 1 for rank in range(1, amount + 1)]
    largest = limit if full else min(limit, max(-(-total // amount), total * portions[0] // sum(portions)))
    least = 1 if total - largest >= amount - 1 else 0
    counts, rest = [largest] + [least] * (amount - 1), total - largest - least * (amount - 1)
    while rest > 0:
        free = [i for i in range(1, amount) if counts[i] < largest] or [i for i in range(1, amount) if counts[i] < limit]
        pool, remaining = sum([portions[i] for i in free]), rest
        for i in free:
            extra = min(limit - counts[i], max(1, remaining * portions[i] // pool), rest)
            counts[i] = counts[i] + extra
            rest = rest - extra
    return np.array(counts)


def bell_draw(key, extent, scale, bound, split=(), kind=jnp.bfloat16):
    values = jax.random.normal(key, extent, jnp.float32) * scale
    if len(split) > 0:
        values = steps_of(key, extent, split, -0.22, 0.18) * values
    return jnp.clip(values, min=-bound, max=bound).astype(kind)


def setup_inputs(seed: int = 0, part: int = 0) -> dict:
    key_list = jax.random.split(jax.random.key(seed), 7)
    part_splits = jax.random.split(jax.random.fold_in(key_list[6], part), 7)
    tokens = bell_draw(part_splits[0], (TOKENS, D), 1.0, 6.0, ((0, 16),))
    expert_ids_keys = jax.random.split(jax.random.fold_in(part_splits[1], 1), TOKENS // TOK_DEV)
    expert_ids_turns = jax.random.permutation(jax.random.fold_in(part_splits[1], 3), TOKENS // TOK_DEV)
    expert_ids = jax.vmap(lambda own, number: routed_block(jax.random.fold_in(part_splits[1], 2), own, number, TOK_DEV, EXPERTS, TOP, CS, 1))(expert_ids_keys, expert_ids_turns).reshape((TOKENS, TOP))
    gate_weights = jnp.clip(jnp.exp(math.log(1.0) - 2.9957323 * jax.random.uniform(part_splits[2], (TOKENS, TOP), jnp.float32) ** steps_of(part_splits[2], (TOKENS, TOP), ((0, 16),), -0.2, 0.2)), 0.05, 1.0)
    w_gate = bell_draw(key_list[3], (EXPERTS, D, F), D ** -0.5, 0.09375, ((1, 16),))
    w_up = bell_draw(key_list[4], (EXPERTS, D, F), D ** -0.5, 0.09375, ((1, 16),))
    w_down = bell_draw(key_list[5], (EXPERTS, F, D), F ** -0.5, 0.1875, ((2, 16),))
    return {"tokens": tokens, "expert_ids": expert_ids, "gate_weights": gate_weights, "w_gate": w_gate, "w_up": w_up, "w_down": w_down}


def slots_of(block_ids):
    flat = block_ids.reshape(-1)
    onehot = (flat[:, None] == jnp.arange(EXPERTS, dtype=jnp.int32)[None, :]).astype(jnp.int32)
    before = jnp.cumsum(onehot, axis=0) - onehot
    return jnp.sum(before * onehot, axis=1).astype(jnp.int32).reshape(block_ids.shape)


def run_expert(operands):
    rows, gate_w, up_w, down_w = operands
    gate = jnp.dot(rows, gate_w, preferred_element_type=jnp.float32)
    up = jnp.dot(rows, up_w, preferred_element_type=jnp.float32)
    hidden = (jax.nn.silu(gate) * up).astype(jnp.bfloat16)
    return jnp.dot(hidden, down_w, preferred_element_type=jnp.float32).astype(jnp.bfloat16)


def reference(tokens, expert_ids, gate_weights, w_gate, w_up, w_down):
    blocks = expert_ids.reshape(N_EP, TOK_DEV, TOP)
    slot = jax.vmap(slots_of)(blocks).reshape(TOKENS, TOP)
    source = (jnp.arange(TOKENS, dtype=jnp.int32) // TOK_DEV)[:, None]
    position = (source * CS + slot).astype(jnp.int32)
    capacity = N_EP * CS
    spread = jnp.broadcast_to(tokens[:, None, :], (TOKENS, TOP, D))
    buffer = jnp.zeros((EXPERTS, capacity, D), jnp.bfloat16).at[expert_ids, position].set(spread)
    expert_out = lax.map(run_expert, (buffer, w_gate, w_up, w_down))
    picked = expert_out[expert_ids, position]
    mixed = jnp.sum(gate_weights[:, :, None] * picked.astype(jnp.float32), axis=1)
    return mixed.astype(jnp.bfloat16)
```

```python
import functools
import math

import jax
import jax.numpy as jnp
from jax import lax
from jax.experimental import pallas as pl
from jax.experimental.pallas import tpu as pltpu
from jax.sharding import PartitionSpec as P

BF16 = jnp.bfloat16
F32 = jnp.float32
TILE = 256
META = 32


def slots_of(block_ids, experts):
    flat = block_ids.reshape(-1)
    onehot = (flat[:, None] == jnp.arange(experts, dtype=jnp.int32)[None, :]).astype(jnp.int32)
    before = jnp.cumsum(onehot, axis=0) - onehot
    return jnp.sum(before * onehot, axis=1).reshape(block_ids.shape)


def fill_slots(rows, expert_ids, slot, experts, per_expert):
    count, picks = expert_ids.shape
    spread = jnp.broadcast_to(rows[:, None, :], (count, picks, rows.shape[1]))
    empty = jnp.zeros((experts, per_expert, rows.shape[1]), BF16)
    return empty.at[expert_ids, slot].set(spread)


def moved_weights(tokens, expert_ids, gate_weights, w_gate, w_up, w_down):
    tok_rows, picks = expert_ids.shape
    experts = w_gate.shape[0]
    per_expert = min(tok_rows, 3 * tok_rows * picks // (2 * experts))
    slot = slots_of(expert_ids, experts)
    features = lax.all_gather(tokens, "tp", axis=1, tiled=True)
    outgoing = fill_slots(features, expert_ids, slot, experts, per_expert)
    arrived = lax.all_to_all(outgoing, "ep", split_axis=0, concat_axis=1, tiled=True)
    gate_owned, up_owned = (
        lax.all_to_all(w_gate, "ep", split_axis=0, concat_axis=1, tiled=True),
        lax.all_to_all(w_up, "ep", split_axis=0, concat_axis=1, tiled=True),
    )
    gate = jnp.einsum("ecd,edf->ecf", arrived, gate_owned, preferred_element_type=F32)
    up = jnp.einsum("ecd,edf->ecf", arrived, up_owned, preferred_element_type=F32)
    hidden = (jax.nn.silu(gate) * up).astype(BF16)
    down_owned = lax.all_to_all(w_down, "ep", split_axis=0, concat_axis=2, tiled=True)
    partial_value = jnp.einsum("ecf,efd->ecd", hidden, down_owned, preferred_element_type=F32)
    expert_out = lax.psum_scatter(
        partial_value.astype(BF16), "tp", scatter_dimension=2, tiled=True
    )
    returned = lax.all_to_all(expert_out, "ep", split_axis=1, concat_axis=0, tiled=True)
    picked = returned[expert_ids, slot]
    mixed = jnp.sum(gate_weights[:, :, None] * picked.astype(F32), axis=1)
    return mixed.astype(BF16)


def dot(a, b, contract):
    return lax.dot_general(a, b, ((contract[0], contract[1]), ((), ())), preferred_element_type=F32)


def order_of(ids, weights, experts):
    names = jnp.arange(experts, dtype=jnp.int32)[:, None, None]
    hit = ids.T[None] == names
    mask = jnp.any(hit, axis=1)
    gates = jnp.sum(jnp.where(hit, weights.T[None], 0.0), axis=1)
    count = jnp.cumsum(mask.astype(jnp.int32), axis=1)
    total = count[:, -1]
    ends = jnp.cumsum(total)
    place = jnp.where(mask, count - 1 + (ends - total)[:, None], -1)
    base = jnp.concatenate([jnp.zeros((1,), jnp.int32), ends])
    return place, gates, base


def visits_of(base, rows, tile):
    experts = base.shape[0] - 1
    start, end = base[:-1], base[1:]
    first = start // tile
    count = jnp.where(end > start, (end - 1) // tile - first + 1, 0)
    upto = jnp.cumsum(count)
    number = jnp.minimum(jnp.arange(rows // tile + experts - 1, dtype=jnp.int32), upto[-1] - 1)
    expert = jnp.sum((upto[None, :] <= number[:, None]).astype(jnp.int32), axis=1)
    pick = expert[:, None] == jnp.arange(experts, dtype=jnp.int32)[None, :]
    tiles = number + jnp.sum(jnp.where(pick, (first - upto + count)[None, :], 0), axis=1)
    return tiles, expert, upto[-1:]


def spans_of(base, rows, tile):
    low = jnp.arange(rows // tile, dtype=jnp.int32)[:, None] * tile
    return (
        jnp.sum((base[None, 1:] <= low).astype(jnp.int32), axis=1),
        jnp.sum((base[None, :-1] < low + tile).astype(jnp.int32), axis=1),
    )


def match_of(row0, low, high, place_ref, tile):
    tokens = place_ref.shape[1]
    row = row0 + lax.broadcasted_iota(jnp.int32, (tile, 1), 0)

    def add(e, found):
        return jnp.where(place_ref[pl.ds(e, 1), :] == row, e, found)

    return lax.fori_loop(low, high, add, jnp.full((tile, tokens), -1, jnp.int32))


def sort_kernel(tile, low, high, place_ref, own_ref, other_ref, own_out, other_out):
    i = pl.program_id(0)
    match = match_of(i * tile, low[i], high[i], place_ref, tile)
    onehot = jnp.where(match >= 0, 1.0, 0.0).astype(BF16)
    own_out[...] = dot(onehot, own_ref[...], ((1,), (0,))).astype(BF16)
    other_out[...] = dot(onehot, other_ref[...], ((1,), (0,))).astype(BF16)


def sort_rows(spans, place, own, other, rows):
    experts, tokens = place.shape
    width = own.shape[1]
    whole = lambda i, *_: (0, 0)
    block = pl.BlockSpec((TILE, width), lambda i, *_: (i, 0))
    return pl.pallas_call(
        functools.partial(sort_kernel, TILE),
        grid_spec=pltpu.PrefetchScalarGridSpec(
            num_scalar_prefetch=2,
            grid=(rows // TILE,),
            in_specs=[
                pl.BlockSpec((experts, tokens), whole),
                pl.BlockSpec((tokens, width), whole),
                pl.BlockSpec((tokens, width), whole),
            ],
            out_specs=[block, block],
        ),
        out_shape=[jax.ShapeDtypeStruct((rows, width), BF16)] * 2,
        compiler_params=pltpu.CompilerParams(vmem_limit_bytes=48 << 20),
        cost_estimate=pl.CostEstimate(
            flops=4 * rows * tokens * width, bytes_accessed=4 * rows * width, transcendentals=0
        ),
        name="sort_rows",
    )(*spans, place, own, other)


def partial_kernel(
    tile, tiles, experts, total, base, core, own_ref, other_ref,
    gate_own, gate_other, up_own, up_other, gate_out, up_out,
):
    v = pl.program_id(0)

    @pl.when(v < total[0])
    def _():
        e = experts[v]
        row = tiles[v] * tile + lax.broadcasted_iota(jnp.int32, (tile, 1), 0)
        mine = (row >= base[e]) & (row < base[e + 1])
        for near, far, out in ((gate_own, gate_other, gate_out), (up_own, up_other, up_out)):
            value = dot(own_ref[...], near[...], ((1,), (0,)))
            value += dot(other_ref[...], far[...], ((1,), (0,)))
            out[...] = jnp.where(mine, value, out[...].astype(F32)).astype(BF16)


def partial_sums(visits, base, core, own, other, gate_own, gate_other, up_own, up_other):
    rows, width = own.shape
    half = gate_other.shape[2]
    tile_block = pl.BlockSpec((TILE, width), lambda v, t, e, *_: (t[v], 0))
    near = pl.BlockSpec((None, width, half), lambda v, t, e, n, b, c: (e[v], 0, c[0]))
    far = pl.BlockSpec((None, width, half), lambda v, t, e, *_: (e[v], 0, 0))
    out = pl.BlockSpec((TILE, half), lambda v, t, e, *_: (t[v], 0))
    return pl.pallas_call(
        functools.partial(partial_kernel, TILE),
        grid_spec=pltpu.PrefetchScalarGridSpec(
            num_scalar_prefetch=5,
            grid=(visits[0].shape[0],),
            in_specs=[tile_block, tile_block, near, far, near, far],
            out_specs=[out, out],
        ),
        out_shape=[jax.ShapeDtypeStruct((rows, half), BF16)] * 2,
        compiler_params=pltpu.CompilerParams(vmem_limit_bytes=48 << 20),
        cost_estimate=pl.CostEstimate(
            flops=8 * rows * width * half, bytes_accessed=8 * rows * half, transcendentals=0
        ),
        name="partial_sums",
    )(*visits, base, core, own, other, gate_own, gate_other, up_own, up_other)


def down_kernel(
    tile, tiles, experts, total, base, core, low, high, hidden_ref, near, far, place_ref, gates_ref,
    own_out, other_out, own_acc, other_acc,
):
    v = pl.program_id(0)
    m = tiles[v]

    @pl.when(v == 0)
    def _():
        own_out[...] = jnp.zeros_like(own_out)
        other_out[...] = jnp.zeros_like(other_out)

    @pl.when(v < total[0])
    def _():
        e = experts[v]
        row = m * tile + lax.broadcasted_iota(jnp.int32, (tile, 1), 0)
        mine = (row >= base[e]) & (row < base[e + 1])
        for weight, acc in ((near, own_acc), (far, other_acc)):
            value = dot(hidden_ref[...], weight[...], ((1,), (1,)))
            acc[...] = jnp.where(mine, value, acc[...])

    final = jnp.where(v + 1 < total[0], tiles[jnp.minimum(v + 1, total[0] - 1)] != m, v + 1 == total[0])

    @pl.when(final)
    def _():
        row = m * tile + lax.broadcasted_iota(jnp.int32, (tile, 1), 0)

        def add(e, found):
            return jnp.where(place_ref[pl.ds(e, 1), :] == row, gates_ref[pl.ds(e, 1), :], found)

        tokens = place_ref.shape[1]
        found = lax.fori_loop(low[m], high[m], add, jnp.zeros((tile, tokens), F32))
        scale = jnp.sum(found, axis=1, keepdims=True)
        onehot = jnp.where(found != 0.0, 1.0, 0.0).astype(BF16)
        for acc, out in ((own_acc, own_out), (other_acc, other_out)):
            scaled = (acc[...] * scale).astype(BF16)
            out[...] += dot(onehot, scaled, ((0,), (0,)))


def down_and_mix(visits, base, core, spans, hidden, down_own, down_other, place, gates):
    rows, half = hidden.shape
    width = down_own.shape[1]
    experts, tokens = place.shape
    whole = lambda v, *_: (0, 0)
    out = pl.BlockSpec((tokens, width), whole)
    return pl.pallas_call(
        functools.partial(down_kernel, TILE),
        grid_spec=pltpu.PrefetchScalarGridSpec(
            num_scalar_prefetch=7,
            grid=(visits[0].shape[0],),
            in_specs=[
                pl.BlockSpec((TILE, half), lambda v, t, e, *_: (t[v], 0)),
                pl.BlockSpec((None, width, half), lambda v, t, e, n, b, c, *_: (e[v], 0, c[0])),
                pl.BlockSpec((None, width, half), lambda v, t, e, *_: (e[v], 0, 0)),
                pl.BlockSpec((experts, tokens), whole),
                pl.BlockSpec((experts, tokens), whole),
            ],
            out_specs=[out, out],
            scratch_shapes=[pltpu.VMEM((TILE, width), F32)] * 2,
        ),
        out_shape=[jax.ShapeDtypeStruct((tokens, width), F32)] * 2,
        compiler_params=pltpu.CompilerParams(vmem_limit_bytes=48 << 20),
        cost_estimate=pl.CostEstimate(
            flops=4 * rows * width * half, bytes_accessed=2 * rows * half, transcendentals=0
        ),
        name="down_and_mix",
    )(*visits, base, core, *spans, hidden, down_own, down_other, place, gates)


def fixed_weights(size, tokens, expert_ids, gate_weights, w_gate, w_up, w_down):
    count, picks = expert_ids.shape
    experts, width, hidden_units = w_gate.shape
    half = hidden_units // 2
    rows = size * count * picks
    chips = size // 2
    core = lax.axis_index("ep") % 2
    pairs = [(i, i ^ 1) for i in range(size)]
    same_core = [[2 * c + k for c in range(chips)] for k in range(2)]
    w_down = jnp.swapaxes(w_down, 1, 2)

    def swap_halves(w):
        return lax.ppermute(lax.dynamic_slice_in_dim(w, (1 - core) * half, half, 2), "ep", pairs)

    high = lax.reduce_precision(gate_weights, 8, 7)
    rest = gate_weights - high
    middle = lax.reduce_precision(rest, 8, 7)
    note = jnp.concatenate(
        [expert_ids.astype(F32), high, middle, lax.reduce_precision(rest - middle, 8, 7)], axis=1
    ).astype(BF16)
    parcels = jnp.concatenate(
        [
            tokens.reshape(count, size, width).swapaxes(0, 1),
            jnp.broadcast_to(note[None], (size,) + note.shape),
        ],
        axis=2,
    )
    arrived = lax.all_to_all(parcels, "ep", split_axis=0, concat_axis=0, tiled=True)
    arrived = arrived.reshape(size * count, width + 4 * picks)
    own = arrived[:, :width]
    other = lax.ppermute(own, "ep", pairs)
    note = arrived[:, width:].astype(F32)
    ids = note[:, :picks].astype(jnp.int32)
    weights = note[:, picks : 2 * picks] + (note[:, 2 * picks : 3 * picks] + note[:, 3 * picks :])

    gate_other, up_other, down_other = swap_halves(w_gate), swap_halves(w_up), swap_halves(w_down)

    place, gates, base = order_of(ids, weights, experts)
    visits = visits_of(base, rows, TILE)
    spans = spans_of(base, rows, TILE)
    which = core.astype(jnp.int32).reshape(1)
    own, other = sort_rows(spans, place, own, other, rows)
    gate, up = partial_sums(visits, base, which, own, other, w_gate, gate_other, w_up, up_other)
    gate = lax.psum_scatter(gate, "ep", scatter_dimension=0, axis_index_groups=same_core, tiled=True)
    up = lax.psum_scatter(up, "ep", scatter_dimension=0, axis_index_groups=same_core, tiled=True)
    hidden = (jax.nn.silu(gate.astype(F32)) * up.astype(F32)).astype(BF16)
    hidden = lax.all_gather(hidden, "ep", axis=0, axis_index_groups=same_core, tiled=True)
    mine, theirs = down_and_mix(
        visits, base, which, spans, hidden, w_down, down_other, place, gates
    )
    mixed = (mine + lax.ppermute(theirs, "ep", pairs)).astype(BF16)
    mixed = lax.all_to_all(
        mixed.reshape(size, count, width), "ep", split_axis=0, concat_axis=0, tiled=True
    )
    return mixed.swapaxes(0, 1).reshape(count, size * width)


def solution(mesh):
    size, inner = mesh.shape["ep"], mesh.shape["tp"]

    def body(tokens, expert_ids, gate_weights, w_gate, w_up, w_down):
        rows = size * math.prod(expert_ids.shape)
        sums = rows * w_gate.shape[2]
        even = size % 4 == 0 and rows % (size * TILE) == 0 and w_gate.shape[2] % 256 == 0
        args = (tokens, expert_ids, gate_weights, w_gate, w_up, w_down)
        if inner == 1 and even and sums <= 3 * math.prod(w_gate.shape):
            return fixed_weights(size, *args)
        return moved_weights(*args)

    placed = (
        P(("parts", "ep"), "tp"),
        P(("parts", "ep"), None),
        P(("parts", "ep"), None),
        P(None, "ep", "tp"),
        P(None, "ep", "tp"),
        P(None, "tp", "ep"),
    )
    return jax.shard_map(
        body, mesh=mesh, in_specs=placed, out_specs=P(("parts", "ep"), "tp"), check_vma=False
    )
```

```python
import functools
import math

import jax
import jax.numpy as jnp
from jax import lax
from jax.experimental import pallas as pl
from jax.experimental.pallas import tpu as pltpu
from jax.sharding import PartitionSpec as P

BF16 = jnp.bfloat16
F32 = jnp.float32
TILE = 256
BLOCK = 1024
LANES = 256


def slots_of(block_ids, experts):
    flat = block_ids.reshape(-1)
    onehot = (flat[:, None] == jnp.arange(experts, dtype=jnp.int32)[None, :]).astype(jnp.int32)
    before = jnp.cumsum(onehot, axis=0) - onehot
    return jnp.sum(before * onehot, axis=1).reshape(block_ids.shape)


def fill_slots(rows, expert_ids, slot, experts, per_expert):
    count, picks = expert_ids.shape
    spread = jnp.broadcast_to(rows[:, None, :], (count, picks, rows.shape[1]))
    empty = jnp.zeros((experts, per_expert, rows.shape[1]), BF16)
    return empty.at[expert_ids, slot].set(spread)


def moved_weights(tokens, expert_ids, gate_weights, w_gate, w_up, w_down):
    tok_rows, picks = expert_ids.shape
    experts = w_gate.shape[0]
    per_expert = min(tok_rows, 3 * tok_rows * picks // (2 * experts))
    slot = slots_of(expert_ids, experts)
    features = lax.all_gather(tokens, "tp", axis=1, tiled=True)
    outgoing = fill_slots(features, expert_ids, slot, experts, per_expert)
    arrived = lax.all_to_all(outgoing, "ep", split_axis=0, concat_axis=1, tiled=True)
    gate_owned, up_owned = (
        lax.all_to_all(w_gate, "ep", split_axis=0, concat_axis=1, tiled=True),
        lax.all_to_all(w_up, "ep", split_axis=0, concat_axis=1, tiled=True),
    )
    gate = jnp.einsum("ecd,edf->ecf", arrived, gate_owned, preferred_element_type=F32)
    up = jnp.einsum("ecd,edf->ecf", arrived, up_owned, preferred_element_type=F32)
    hidden = (jax.nn.silu(gate) * up).astype(BF16)
    down_owned = lax.all_to_all(w_down, "ep", split_axis=0, concat_axis=2, tiled=True)
    partial_value = jnp.einsum("ecf,efd->ecd", hidden, down_owned, preferred_element_type=F32)
    expert_out = lax.psum_scatter(
        partial_value.astype(BF16), "tp", scatter_dimension=2, tiled=True
    )
    returned = lax.all_to_all(expert_out, "ep", split_axis=1, concat_axis=0, tiled=True)
    picked = returned[expert_ids, slot]
    mixed = jnp.sum(gate_weights[:, :, None] * picked.astype(F32), axis=1)
    return mixed.astype(BF16)


def dot(a, b, contract):
    return lax.dot_general(a, b, ((contract[0], contract[1]), ((), ())), preferred_element_type=F32)


def order_of(ids, weights, experts):
    names = jnp.arange(experts, dtype=jnp.int32)
    mask = jnp.any(ids.T[None] == names[:, None, None], axis=1)
    gates = jnp.sum(jnp.where(ids[:, :, None] == names, weights[:, :, None], 0.0), axis=1)
    count = jnp.cumsum(mask.astype(jnp.int32), axis=1)
    total = count[:, -1]
    ends = jnp.cumsum(total)
    place = jnp.where(mask, count - 1 + (ends - total)[:, None], -1)
    base = jnp.concatenate([jnp.zeros((1,), jnp.int32), ends])
    return place, gates, base


def spans_of(base, rows):
    low = jnp.arange(rows // TILE, dtype=jnp.int32)[:, None] * TILE
    return (
        jnp.sum((base[None, 1:] <= low).astype(jnp.int32), axis=1),
        jnp.sum((base[None, :-1] < low + TILE).astype(jnp.int32), axis=1),
    )


def split3(value):
    high = lax.reduce_precision(value, 8, 7)
    middle = lax.reduce_precision(value - high, 8, 7)
    return high, middle, lax.reduce_precision(value - high - middle, 8, 7)


def onehot_of(place_ref, row0, low, high):
    tokens = place_ref.shape[1]
    number = lax.broadcasted_iota(jnp.int32, (TILE, tokens), 0).astype(F32).astype(BF16)

    def add(e, found):
        away = place_ref[pl.ds(e, 1), :] - row0
        away = jnp.where((away >= 0) & (away < TILE), away, -1).astype(F32).astype(BF16)
        return jnp.where(number == away, jnp.ones((), BF16), found)

    return lax.fori_loop(low, high, add, jnp.zeros((TILE, tokens), BF16))


def mine_of(base, e, row0):
    row = row0 + lax.broadcasted_iota(jnp.int32, (TILE, 1), 0)
    return (row >= base[e]) & (row < base[e + 1])


def sort_kernel(low, high, base, place_ref, gates_ref, *refs):
    slices, (out, scale_out) = refs[:-2], refs[-2:]
    experts = place_ref.shape[0]
    lane = lax.broadcasted_iota(jnp.int32, (TILE, scale_out.shape[1]), 1)

    @pl.loop(0, BLOCK // TILE)
    def _(part):
        i = pl.program_id(0) * (BLOCK // TILE) + part
        row0 = i * TILE
        here = pl.ds(pl.multiple_of(part * TILE, TILE), TILE)
        onehot = onehot_of(place_ref, row0, low[i], high[i])
        for k, ref in enumerate(slices):
            out[here, k * LANES : (k + 1) * LANES] = dot(onehot, ref[...], ((1,), (0,))).astype(BF16)
        gates = dot(onehot, gates_ref[...], ((1,), (0,)))
        name = lax.fori_loop(
            low[i],
            high[i],
            lambda e, name: jnp.where(mine_of(base, e, row0), e, name),
            jnp.zeros((TILE, 1), jnp.int32),
        )
        kept = (lane == name) | (lane == name + experts) | (lane == name + 2 * experts)
        scale = jnp.sum(jnp.where(kept, gates, 0.0), axis=1, keepdims=True)
        scale_out[here, :] = jnp.broadcast_to(scale, lane.shape)


def sort_rows(spans, base, place, gates, slices, rows, units):
    experts, tokens = place.shape
    whole = lambda i, *_: (0, 0)
    width = len(slices) * LANES
    return pl.pallas_call(
        sort_kernel,
        grid_spec=pltpu.PrefetchScalarGridSpec(
            num_scalar_prefetch=3,
            grid=(rows // BLOCK,),
            in_specs=[
                pl.BlockSpec((experts, tokens), whole),
                pl.BlockSpec((tokens, units), whole),
            ]
            + [pl.BlockSpec((tokens, LANES), whole)] * len(slices),
            out_specs=[
                pl.BlockSpec((BLOCK, width), lambda i, *_: (i, 0)),
                pl.BlockSpec((BLOCK, units), lambda i, *_: (i, 0)),
            ],
        ),
        out_shape=[
            jax.ShapeDtypeStruct((rows, width), BF16),
            jax.ShapeDtypeStruct((rows, units), F32),
        ],
        compiler_params=pltpu.CompilerParams(vmem_limit_bytes=48 << 20),
        cost_estimate=pl.CostEstimate(
            flops=2 * rows * tokens * width, bytes_accessed=4 * rows * width, transcendentals=0
        ),
        name="sort_rows",
    )(*spans, base, place, gates, *slices)


def partial_kernel(low, high, base, rows_ref, *refs):
    weights, out = refs[:-1], refs[-1]
    width = weights[0].shape[1]

    @pl.loop(0, BLOCK // TILE)
    def _(part):
        i = pl.program_id(0) * (BLOCK // TILE) + part
        here = pl.ds(pl.multiple_of(part * TILE, TILE), TILE)

        def add(e, kept):
            value = kept
            total = 0.0
            for k, weight in enumerate(weights):
                total += dot(rows_ref[here, k * LANES : k * LANES + width], weight[e], ((1,), (0,)))
            return jnp.where(mine_of(base, e, i * TILE), total, value)

        out[here, :] = lax.fori_loop(
            low[i], high[i], add, jnp.zeros((TILE, out.shape[1]), F32)
        ).astype(BF16)


def partial_sums(spans, base, rows_in, weights):
    rows = rows_in.shape[0]
    experts, width, units = weights[0].shape
    return pl.pallas_call(
        partial_kernel,
        grid_spec=pltpu.PrefetchScalarGridSpec(
            num_scalar_prefetch=3,
            grid=(rows // BLOCK,),
            in_specs=[pl.BlockSpec((BLOCK, rows_in.shape[1]), lambda i, *_: (i, 0))]
            + [pl.BlockSpec((experts, width, units), lambda i, *_: (0, 0, 0))] * len(weights),
            out_specs=pl.BlockSpec((BLOCK, units), lambda i, *_: (i, 0)),
        ),
        out_shape=jax.ShapeDtypeStruct((rows, units), BF16),
        compiler_params=pltpu.CompilerParams(vmem_limit_bytes=48 << 20),
        cost_estimate=pl.CostEstimate(
            flops=2 * rows * rows_in.shape[1] * units,
            bytes_accessed=2 * rows * rows_in.shape[1],
            transcendentals=0,
        ),
        name="partial_sums",
    )(*spans, base, rows_in, *weights)


def down_kernel(low, high, base, place_ref, *refs):
    count = len(refs) // 2 - 1
    hidden, weights = refs[:2], refs[2 : 2 + 4]
    out, onehot_ref, value_ref = refs[6:]
    width = weights[0].shape[1]

    @pl.when(pl.program_id(0) == 0)
    def _():
        out[...] = jnp.zeros_like(out)
        value_ref[...] = jnp.zeros_like(value_ref)

    @pl.loop(0, BLOCK // TILE)
    def _(part):
        i = pl.program_id(0) * (BLOCK // TILE) + part
        here = pl.ds(pl.multiple_of(part * TILE, TILE), TILE)
        units = jnp.concatenate([hidden[0][here, :], hidden[1][here, :]], axis=1)
        onehot_ref[here, :] = onehot_of(place_ref, i * TILE, low[i], high[i])
        for k, weight in enumerate(weights):
            value_ref[here, k * LANES : k * LANES + width] = lax.fori_loop(
                low[i],
                high[i],
                lambda e, kept: jnp.where(
                    mine_of(base, e, i * TILE), dot(units, weight[e], ((1,), (1,))), kept
                ),
                jnp.zeros((TILE, width), F32),
            ).astype(BF16)

    out[...] += dot(onehot_ref[...], value_ref[...], ((0,), (0,)))


def down_and_mix(spans, base, place, hidden, weights):
    rows, units = hidden[0].shape
    experts, tokens = place.shape
    width = len(weights) * LANES
    block = pl.BlockSpec((BLOCK, units), lambda i, *_: (i, 0))
    return pl.pallas_call(
        down_kernel,
        grid_spec=pltpu.PrefetchScalarGridSpec(
            num_scalar_prefetch=3,
            grid=(rows // BLOCK,),
            in_specs=[pl.BlockSpec((experts, tokens), lambda i, *_: (0, 0)), block, block]
            + [pl.BlockSpec(weights[0].shape, lambda i, *_: (0, 0, 0))] * len(weights),
            out_specs=pl.BlockSpec((tokens, width), lambda i, *_: (0, 0)),
            scratch_shapes=[pltpu.VMEM((BLOCK, tokens), BF16), pltpu.VMEM((BLOCK, width), BF16)],
        ),
        out_shape=jax.ShapeDtypeStruct((tokens, width), F32),
        compiler_params=pltpu.CompilerParams(vmem_limit_bytes=52 << 20),
        cost_estimate=pl.CostEstimate(
            flops=4 * rows * width * units, bytes_accessed=4 * rows * units, transcendentals=0
        ),
        name="down_and_mix",
    )(*spans, base, place, *hidden, *weights)


def links_of(step, pieces, places, down):
    pairs = []
    for place in range(places):
        to = place - 1 if down else place + 1
        hop = places - 1 - place if down else place
        if 0 <= to < places and 0 <= step - hop < pieces:
            pairs += [(4 * place + k, 4 * to + k) for k in range(4)]
    return pairs


def sum_flow(take, pieces, places, place, down):
    hop = places - 1 - place if down else place
    sums, got = [], None
    for step in range(pieces + places - 1):
        piece = take(jnp.clip(step - hop, 0, pieces - 1))
        if got is not None:
            piece = (piece.astype(F32) + got.astype(F32)).astype(BF16)
        if step >= places - 1:
            sums.append(piece)
        if step < pieces + places - 2:
            got = lax.ppermute(piece, "ep", links_of(step, pieces, places, down))
    return sums


def copy_flow(chunks, places, place, down):
    hop = places - 1 - place if down else place
    pieces, held, got = len(chunks), [], None
    for step in range(pieces + places - 1):
        piece = chunks[min(step, pieces - 1)]
        if got is not None:
            piece = jnp.where(hop == 0, piece, got)
        held.append(piece)
        if step < pieces + places - 2:
            got = lax.ppermute(piece, "ep", links_of(step, pieces, places, down))
    size = chunks[0].shape[0]
    return lax.dynamic_slice_in_dim(jnp.concatenate(held, axis=0), hop * size, pieces * size, 0)


def fixed_weights(size, tokens, expert_ids, gate_weights, w_gate, w_up, w_down):
    count, picks = expert_ids.shape
    experts, width, hidden_units = w_gate.shape
    quarter = hidden_units // 4
    units = quarter // 2
    rows = size * count * picks
    places = size // 4
    me, plane = lax.axis_index("ep"), lax.axis_index("parts")
    core, place_on_line = me % 2, me // 4
    w_down = jnp.swapaxes(w_down, 1, 2)

    twins = [(i, i ^ 1) for i in range(size)]
    cross = [
        (p * size + i, p * size + (i ^ 2 ^ p)) for p in range(2) for i in range(size)
    ]
    to_twin = lambda value: lax.ppermute(value, "ep", twins)
    to_cross = lambda value: lax.ppermute(value, ("parts", "ep"), cross)
    to_plane = lambda value: lax.ppermute(value, "parts", [(0, 1), (1, 0)])
    my_quarter = me % 4
    twin_quarter = my_quarter ^ 1
    cross_quarter = my_quarter ^ 2 ^ plane

    def gate_up(f):
        def cut(q, e0, e1):
            at = q * quarter + f * units
            return jnp.concatenate(
                [lax.dynamic_slice_in_dim(w[e0:e1], at, units, 2) for w in (w_gate, w_up)], axis=2
            )
        return cut

    def down(q, e0, e1):
        return lax.dynamic_slice_in_dim(w_down[e0:e1], q * quarter, quarter, 2)

    note = jnp.concatenate([expert_ids.astype(F32), *split3(gate_weights)], axis=1).astype(BF16)
    fill = LANES - width - note.shape[1]
    parcels = jnp.concatenate(
        [
            tokens.reshape(count, size, width).swapaxes(0, 1),
            jnp.broadcast_to(jnp.pad(note, ((0, 0), (0, fill)))[None], (size, count, LANES - width)),
        ],
        axis=2,
    )
    own = lax.all_to_all(parcels, "ep", split_axis=0, concat_axis=0, tiled=True)
    own = own.reshape(size * count, LANES)
    far = to_cross(own)
    slices = [own, to_twin(own), far, to_twin(far)]
    note = own[:, width : width + 4 * picks].astype(F32)
    ids = note[:, :picks].astype(jnp.int32)
    weights = note[:, picks : 2 * picks] + (note[:, 2 * picks : 3 * picks] + note[:, 3 * picks :])
    place, gates, base = order_of(ids, weights, experts)
    spans = spans_of(base, rows)
    gates = jnp.concatenate(split3(gates), axis=1).astype(BF16)
    gates = jnp.pad(gates, ((0, 0), (0, units - gates.shape[1])))

    half = experts // 2
    last = None
    held = []
    for cut in (gate_up(0), gate_up(1), down):
        across, beside = [], []
        for e0 in (0, half):
            piece = cut(cross_quarter, e0, e0 + half)
            if last is not None:
                piece, _ = lax.optimization_barrier((piece, last))
            last = to_cross(piece)
            across.append(last)
            beside.append(to_plane(last))
        held.append(
            [
                cut(my_quarter, 0, experts),
                to_twin(cut(twin_quarter, 0, experts)),
                jnp.concatenate(across, axis=0),
                jnp.concatenate(beside, axis=0),
            ]
        )

    sorted_rows, scale = sort_rows(spans, base, place, gates, slices, rows, units)
    hidden = []
    chunks, streams = 4, 2
    side = rows // 2
    size_of = side // (chunks * streams)
    for f in range(2):
        sums = partial_sums(spans, base, sorted_rows, held[f])
        sides = []
        for is_down in (True, False):
            first_row = 0 if is_down else side
            flows = [
                sum_flow(
                    lambda k, m=m: lax.dynamic_slice_in_dim(
                        sums, first_row + (k * streams + m) * size_of, size_of, 0
                    ),
                    chunks, places, place_on_line, is_down,
                )
                for m in range(streams)
            ]
            ready = []
            for k in range(chunks):
                total = jnp.concatenate([flow[k] for flow in flows], axis=0).astype(F32)
                at = first_row + k * streams * size_of
                gate, up = total[:, :units], total[:, units:]
                ready.append(
                    (jax.nn.silu(gate) * up * scale[at : at + streams * size_of]).astype(BF16)
                )
            sides.append(copy_flow(ready, places, place_on_line, not is_down))
        hidden.append(jnp.concatenate(sides, axis=0))

    mixed = down_and_mix(spans, base, place, hidden, held[2])
    mine, twin, far, far_twin = (mixed[:, k * LANES : k * LANES + width] for k in range(4))
    moved = to_twin(jnp.concatenate([far_twin, twin], axis=0).astype(BF16)).astype(F32)
    tokens_all = size * count
    far = to_cross((far + moved[:tokens_all]).astype(BF16)).astype(F32)
    mixed = (mine + moved[tokens_all:] + far).astype(BF16)
    mixed = lax.all_to_all(
        mixed.reshape(size, count, width), "ep", split_axis=0, concat_axis=0, tiled=True
    )
    return mixed.swapaxes(0, 1).reshape(count, size * width)


def solution(mesh):
    size, inner = mesh.shape["ep"], mesh.shape["tp"]

    def body(tokens, expert_ids, gate_weights, w_gate, w_up, w_down):
        rows = size * math.prod(expert_ids.shape)
        sums = rows * w_gate.shape[2]
        experts, width, units = w_gate.shape
        even = (
            size % 4 == 0
            and size > 4
            and mesh.shape["parts"] == 2
            and rows % (2 * BLOCK) == 0
            and units % 1024 == 0
            and experts % 2 == 0
            and 3 * experts <= units // 8
            and width + 4 * expert_ids.shape[1] <= LANES
        )
        args = (tokens, expert_ids, gate_weights, w_gate, w_up, w_down)
        if inner == 1 and even and sums <= 3 * math.prod(w_gate.shape):
            return fixed_weights(size, *args)
        return moved_weights(*args)

    placed = (
        P(("parts", "ep"), "tp"),
        P(("parts", "ep"), None),
        P(("parts", "ep"), None),
        P(None, "ep", "tp"),
        P(None, "ep", "tp"),
        P(None, "tp", "ep"),
    )
    return jax.shard_map(
        body, mesh=mesh, in_specs=placed, out_specs=P(("parts", "ep"), "tp"), check_vma=False
    )
```

```python
import functools
import math

import jax
import jax.numpy as jnp
from jax import lax
from jax.experimental import pallas as pl
from jax.experimental.pallas import tpu as pltpu
from jax.sharding import PartitionSpec as P

BF16 = jnp.bfloat16
F32 = jnp.float32
TILE = 256
BLOCK = 1024
LANES = 256
UNITS = 128


def slots_of(block_ids, experts):
    flat = block_ids.reshape(-1)
    onehot = (flat[:, None] == jnp.arange(experts, dtype=jnp.int32)[None, :]).astype(jnp.int32)
    before = jnp.cumsum(onehot, axis=0) - onehot
    return jnp.sum(before * onehot, axis=1).reshape(block_ids.shape)


def fill_slots(rows, expert_ids, slot, experts, per_expert):
    count, picks = expert_ids.shape
    spread = jnp.broadcast_to(rows[:, None, :], (count, picks, rows.shape[1]))
    empty = jnp.zeros((experts, per_expert, rows.shape[1]), BF16)
    return empty.at[expert_ids, slot].set(spread)


def moved_weights(tokens, expert_ids, gate_weights, w_gate, w_up, w_down):
    tok_rows, picks = expert_ids.shape
    experts = w_gate.shape[0]
    per_expert = min(tok_rows, 3 * tok_rows * picks // (2 * experts))
    slot = slots_of(expert_ids, experts)
    features = lax.all_gather(tokens, "tp", axis=1, tiled=True)
    outgoing = fill_slots(features, expert_ids, slot, experts, per_expert)
    arrived = lax.all_to_all(outgoing, "ep", split_axis=0, concat_axis=1, tiled=True)
    gate_owned, up_owned = (
        lax.all_to_all(w_gate, "ep", split_axis=0, concat_axis=1, tiled=True),
        lax.all_to_all(w_up, "ep", split_axis=0, concat_axis=1, tiled=True),
    )
    gate = jnp.einsum("ecd,edf->ecf", arrived, gate_owned, preferred_element_type=F32)
    up = jnp.einsum("ecd,edf->ecf", arrived, up_owned, preferred_element_type=F32)
    hidden = (jax.nn.silu(gate) * up).astype(BF16)
    down_owned = lax.all_to_all(w_down, "ep", split_axis=0, concat_axis=2, tiled=True)
    partial_value = jnp.einsum("ecf,efd->ecd", hidden, down_owned, preferred_element_type=F32)
    expert_out = lax.psum_scatter(
        partial_value.astype(BF16), "tp", scatter_dimension=2, tiled=True
    )
    returned = lax.all_to_all(expert_out, "ep", split_axis=1, concat_axis=0, tiled=True)
    picked = returned[expert_ids, slot]
    mixed = jnp.sum(gate_weights[:, :, None] * picked.astype(F32), axis=1)
    return mixed.astype(BF16)


def dot(a, b, contract):
    return lax.dot_general(a, b, ((contract[0], contract[1]), ((), ())), preferred_element_type=F32)


def params(mib=48):
    return pltpu.CompilerParams(vmem_limit_bytes=mib << 20)


def cost(flops, moved):
    return pl.CostEstimate(flops=flops, bytes_accessed=moved, transcendentals=0)


def split3(value):
    high = lax.reduce_precision(value, 8, 7)
    middle = lax.reduce_precision(value - high, 8, 7)
    return high, middle, lax.reduce_precision(value - high - middle, 8, 7)


def order_kernel(width, picks, experts, note_ref, place_out, across_out, gates_out, base_out):
    tokens = note_ref.shape[0]
    note = note_ref[...].astype(F32)
    lane = lax.broadcasted_iota(jnp.int32, (tokens, UNITS), 1)
    name = jnp.where(lane < 3 * experts, lane % experts, -1).astype(F32)
    gates = jnp.zeros((tokens, UNITS), F32)
    for k in range(picks):
        one = note[:, width + k : width + k + 1]
        weight = (
            note[:, width + picks + k : width + picks + k + 1]
            + note[:, width + 2 * picks + k : width + 2 * picks + k + 1]
            + note[:, width + 3 * picks + k : width + 3 * picks + k + 1]
        )
        gates = jnp.where(name == one, weight, gates)
    mask = jnp.where((gates != 0.0) & (lane < experts), 1.0, 0.0)
    high = gates.astype(BF16)
    middle = (gates - high.astype(F32)).astype(BF16)
    rest = (gates - high.astype(F32) - middle.astype(F32)).astype(BF16)
    gates_out[...] = jnp.where(
        lane < experts,
        high.astype(F32),
        jnp.where(lane < 2 * experts, middle.astype(F32), rest.astype(F32)),
    ).astype(BF16)
    row = lax.broadcasted_iota(jnp.int32, (tokens, tokens), 0)
    column = lax.broadcasted_iota(jnp.int32, (tokens, tokens), 1)
    upto = jnp.where(column <= row, 1.0, 0.0).astype(BF16)
    count = dot(upto, mask.astype(BF16), ((1,), (0,)))
    total = jnp.broadcast_to(count[tokens - 1 : tokens, :], (8, UNITS))
    large = jnp.floor(total * (1.0 / 128.0))
    row = lax.broadcasted_iota(jnp.int32, (UNITS, UNITS), 0)
    column = lax.broadcasted_iota(jnp.int32, (UNITS, UNITS), 1)
    before = jnp.where(row < column, 1.0, 0.0).astype(BF16)
    base = 128.0 * dot(large.astype(BF16), before, ((1,), (0,)))
    base += dot((total - 128.0 * large).astype(BF16), before, ((1,), (0,)))
    base_out[...] = base.astype(jnp.int32)
    place = jnp.where(mask > 0.0, count - 1.0 + base[0:1, :], -1.0)
    place_out[...] = place.astype(jnp.int32)
    across_out[...] = place.T.astype(jnp.int32)


def order_of(note, width, picks, experts):
    tokens = note.shape[0]
    return pl.pallas_call(
        functools.partial(order_kernel, width, picks, experts),
        out_shape=[
            jax.ShapeDtypeStruct((tokens, UNITS), jnp.int32),
            jax.ShapeDtypeStruct((UNITS, tokens), jnp.int32),
            jax.ShapeDtypeStruct((tokens, UNITS), BF16),
            jax.ShapeDtypeStruct((8, UNITS), jnp.int32),
        ],
        compiler_params=params(),
        cost_estimate=cost(2 * tokens * tokens * UNITS, 4 * tokens * tokens),
        name="order",
    )(note)


def spans_of(base, rows):
    low = jnp.arange(rows // TILE, dtype=jnp.int32)[:, None] * TILE
    return (
        jnp.sum((base[None, 1:] <= low).astype(jnp.int32), axis=1),
        jnp.sum((base[None, :-1] < low + TILE).astype(jnp.int32), axis=1),
    )


def mine_of(base, e, row0):
    row = row0 + lax.broadcasted_iota(jnp.int32, (TILE, 1), 0)
    return (row >= base[e]) & (row < base[e + 1])


def sort_kernel(experts, low, high, base, across_ref, gates_ref, *refs):
    slices, (out, scale_out, onehot_ref, name_ref) = refs[:-4], refs[-4:]
    tokens = onehot_ref.shape[1]
    number = lax.broadcasted_iota(jnp.int32, (TILE, 128), 0).astype(F32).astype(BF16)

    @pl.loop(0, BLOCK // TILE)
    def _(part):
        i = pl.program_id(0) * (BLOCK // TILE) + part
        row0 = i * TILE
        here = pl.ds(pl.multiple_of(part * TILE, TILE), TILE)
        for c in range(tokens // 128):

            def add(e, found):
                away = across_ref[e][c : c + 1, :] - row0
                away = jnp.where((away >= 0) & (away < TILE), away, -1).astype(F32).astype(BF16)
                return jnp.where(number == away, jnp.ones((), BF16), found)

            onehot_ref[here, c * 128 : (c + 1) * 128] = lax.fori_loop(
                low[i], high[i], add, jnp.zeros((TILE, 128), BF16)
            )
        name_ref[here, :] = lax.fori_loop(
            low[i],
            high[i],
            lambda e, name: jnp.where(mine_of(base, e, row0), e, name),
            jnp.zeros((TILE, UNITS), jnp.int32),
        )

    onehot = onehot_ref[...]
    for k, ref in enumerate(slices):
        out[:, k * LANES : (k + 1) * LANES] = dot(onehot, ref[...], ((1,), (0,))).astype(BF16)
    gates = dot(onehot, gates_ref[...], ((1,), (0,)))
    lane = lax.broadcasted_iota(jnp.int32, (BLOCK, UNITS), 1)
    name = name_ref[...]
    kept = (lane == name) | (lane == name + experts) | (lane == name + 2 * experts)
    scale = jnp.sum(jnp.where(kept, gates, 0.0), axis=1, keepdims=True)
    scale_out[...] = jnp.broadcast_to(scale, lane.shape)


def sort_rows(spans, base, across, gates, slices, rows, experts):
    tokens = gates.shape[0]
    across = across[:experts].reshape(experts, tokens // 128, 128)
    whole = lambda i, *_: (0, 0)
    width = len(slices) * LANES
    return pl.pallas_call(
        functools.partial(sort_kernel, experts),
        grid_spec=pltpu.PrefetchScalarGridSpec(
            num_scalar_prefetch=3,
            grid=(rows // BLOCK,),
            in_specs=[
                pl.BlockSpec(across.shape, lambda i, *_: (0, 0, 0)),
                pl.BlockSpec((tokens, UNITS), whole),
            ]
            + [pl.BlockSpec((tokens, LANES), whole)] * len(slices),
            out_specs=[
                pl.BlockSpec((BLOCK, width), lambda i, *_: (i, 0)),
                pl.BlockSpec((BLOCK, UNITS), lambda i, *_: (i, 0)),
            ],
            scratch_shapes=[
                pltpu.VMEM((BLOCK, tokens), BF16),
                pltpu.VMEM((BLOCK, UNITS), jnp.int32),
            ],
        ),
        out_shape=[
            jax.ShapeDtypeStruct((rows, width), BF16),
            jax.ShapeDtypeStruct((rows, UNITS), F32),
        ],
        compiler_params=params(),
        cost_estimate=cost(2 * rows * tokens * width, 4 * rows * width),
        name="sort_rows",
    )(*spans, base, across, gates, *slices)


def partial_kernel(low, high, base, quarter, rows_ref, *refs):
    pairs, out = [refs[j : j + 2] for j in range(0, 8, 2)], refs[-1]
    width = pairs[0][0].shape[1]

    @pl.loop(0, BLOCK // TILE)
    def _(part):
        i = pl.program_id(0) * (BLOCK // TILE) + part
        here = pl.ds(pl.multiple_of(part * TILE, TILE), TILE)

        def add(e, kept):
            total = 0.0
            for k, pair in enumerate(pairs):
                weight = jnp.concatenate([pair[0][e], pair[1][e]], axis=1)
                rows = rows_ref[here, k * LANES : k * LANES + width]
                total += dot(rows, weight, ((1,), (0,)))
            return jnp.where(mine_of(base, e, i * TILE), total, kept)

        out[here, :] = lax.fori_loop(
            low[i], high[i], add, jnp.zeros((TILE, out.shape[1]), F32)
        ).astype(BF16)


def partial_sums(f, spans, base, quarter, rows_in, w_gate, w_up, pieces):
    rows = rows_in.shape[0]
    experts, width, _ = w_gate.shape
    own = pl.BlockSpec((experts, width, UNITS), lambda i, lo, hi, b, q: (0, 0, 2 * q[0] + f))
    block = pl.BlockSpec((experts, width, UNITS), lambda i, *_: (0, 0, 0))
    return pl.pallas_call(
        partial_kernel,
        grid_spec=pltpu.PrefetchScalarGridSpec(
            num_scalar_prefetch=4,
            grid=(rows // BLOCK,),
            in_specs=[pl.BlockSpec((BLOCK, rows_in.shape[1]), lambda i, *_: (i, 0)), own, own]
            + [block] * len(pieces),
            out_specs=pl.BlockSpec((BLOCK, 2 * UNITS), lambda i, *_: (i, 0)),
        ),
        out_shape=jax.ShapeDtypeStruct((rows, 2 * UNITS), BF16),
        compiler_params=params(),
        cost_estimate=cost(4 * rows * rows_in.shape[1] * UNITS, 2 * rows * rows_in.shape[1]),
        name="partial_sums",
    )(*spans, base, quarter, rows_in, w_gate, w_up, *pieces)


def down_kernel(low, high, base, quarter, place_ref, hidden0, hidden1, own_ref, *refs):
    pairs, (out, onehot_ref, value_ref) = [refs[j : j + 2] for j in range(0, 6, 2)], refs[6:]
    width = own_ref.shape[1]
    tokens = place_ref.shape[1]
    lane = lax.broadcasted_iota(jnp.int32, (tokens, 128), 1)

    @pl.when(pl.program_id(0) == 0)
    def _():
        out[...] = jnp.zeros_like(out)
        value_ref[...] = jnp.zeros_like(value_ref)

    for part in range(BLOCK // TILE):
        i = pl.program_id(0) * (BLOCK // TILE) + part
        here = slice(part * TILE, (part + 1) * TILE)
        units = jnp.concatenate([hidden0[here, :], hidden1[here, :]], axis=1)
        onehot_ref[:, here] = jnp.zeros((tokens, TILE), BF16)

        @pl.loop(low[i], high[i])
        def _(e):
            mine = mine_of(base, e, i * TILE)
            for k in range(4):
                weight = own_ref[e]
                if k:
                    weight = jnp.concatenate([pairs[k - 1][0][e], pairs[k - 1][1][e]], axis=1)
                value = dot(units, weight, ((1,), (1,)))
                at = slice(k * LANES, k * LANES + width)
                value_ref[here, at] = jnp.where(
                    mine, value, value_ref[here, at].astype(F32)
                ).astype(BF16)
            place = place_ref[e] - i * TILE
            for c in range(TILE // 128):
                at = slice(part * TILE + c * 128, part * TILE + (c + 1) * 128)
                hit = jnp.where(place == lane + c * 128, 1.0, 0.0).astype(BF16)
                onehot_ref[:, at] += hit

    out[...] += dot(onehot_ref[...], value_ref[...], ((1,), (0,)))


def down_and_mix(spans, base, quarter, place, hidden, w_down, pieces):
    rows = hidden[0].shape[0]
    experts, width, _ = w_down.shape
    tokens = place.shape[1]
    block = pl.BlockSpec((BLOCK, UNITS), lambda i, *_: (i, 0))
    own = pl.BlockSpec((experts, width, 2 * UNITS), lambda i, lo, hi, b, q: (0, 0, q[0]))
    return pl.pallas_call(
        down_kernel,
        grid_spec=pltpu.PrefetchScalarGridSpec(
            num_scalar_prefetch=4,
            grid=(rows // BLOCK,),
            in_specs=[
                pl.BlockSpec((experts, tokens, 128), lambda i, *_: (0, 0, 0)),
                block,
                block,
                own,
            ]
            + [pl.BlockSpec((experts, width, UNITS), lambda i, *_: (0, 0, 0))] * len(pieces),
            out_specs=pl.BlockSpec((tokens, 4 * LANES), lambda i, *_: (0, 0)),
            scratch_shapes=[
                pltpu.VMEM((tokens, BLOCK), BF16),
                pltpu.VMEM((BLOCK, 4 * LANES), BF16),
            ],
        ),
        out_shape=jax.ShapeDtypeStruct((tokens, 4 * LANES), F32),
        compiler_params=params(56),
        cost_estimate=cost(8 * rows * tokens * LANES, 16 * rows * UNITS),
        name="down_and_mix",
    )(*spans, base, quarter, place, *hidden, w_down, *pieces)


def fixed_weights(size, tokens, expert_ids, gate_weights, w_gate, w_up, w_down):
    count, picks = expert_ids.shape
    experts, width, hidden_units = w_gate.shape
    quarter = hidden_units // 4
    rows = size * count * picks
    places = size // 4
    me, plane = lax.axis_index("ep"), lax.axis_index("parts")
    w_down = jnp.swapaxes(w_down, 1, 2)

    twins = [(i, i ^ 1) for i in range(size)]
    cross = [(p * size + i, p * size + (i ^ 2 ^ p)) for p in range(2) for i in range(size)]
    to_twin = lambda value: lax.ppermute(value, "ep", twins)
    to_cross = lambda value: lax.ppermute(value, ("parts", "ep"), cross)
    to_plane = lambda value: lax.ppermute(value, "parts", [(0, 1), (1, 0)])
    line = [[4 * p + k for p in range(places)] for k in range(4)]
    my_quarter = me % 4
    twin_quarter = my_quarter ^ 1
    cross_quarter = my_quarter ^ 2 ^ plane

    note = jnp.concatenate([expert_ids.astype(F32), *split3(gate_weights)], axis=1).astype(BF16)
    fill = LANES - width - note.shape[1]
    parcels = jnp.concatenate(
        [
            tokens.reshape(count, size, width).swapaxes(0, 1),
            jnp.broadcast_to(jnp.pad(note, ((0, 0), (0, fill)))[None], (size, count, LANES - width)),
        ],
        axis=2,
    )
    own = lax.all_to_all(parcels, "ep", split_axis=0, concat_axis=0, tiled=True)
    own = own.reshape(size * count, LANES)
    far = to_cross(own)
    slices = [own, to_twin(own), far, to_twin(far)]
    place, across, gates, base = order_of(own, width, picks, experts)
    base = base[0, : experts + 1]
    spans = spans_of(base, rows)
    which = my_quarter.astype(jnp.int32).reshape(1)

    def cut(w, q, f):
        return lax.dynamic_slice_in_dim(w, q * quarter + f * UNITS, UNITS, 2)

    last = []
    held = []
    for f, w in ((0, w_gate), (0, w_up), (1, w_gate), (1, w_up), (0, w_down), (1, w_down)):
        piece = cut(w, cross_quarter, f)
        if last:
            piece = lax.optimization_barrier((piece, *last))[0]
        across_x = to_cross(piece)
        last = [across_x, far]
        held.append((to_twin(cut(w, twin_quarter, f)), across_x, to_plane(across_x)))
    weave = lambda pair: [piece for both in zip(*pair) for piece in both]

    sorted_rows, scale = sort_rows(spans, base, across, gates, slices, rows, experts)
    scale = lax.dynamic_slice_in_dim(scale, (me // 4) * (rows // places), rows // places, 0)
    hidden = []
    for f in range(2):
        pieces = weave(held[2 * f : 2 * f + 2])
        sums = partial_sums(f, spans, base, which, sorted_rows, w_gate, w_up, pieces)
        sums = lax.psum_scatter(
            sums, "ep", scatter_dimension=0, axis_index_groups=line, tiled=True
        ).astype(F32)
        units = (jax.nn.silu(sums[:, :UNITS]) * sums[:, UNITS:] * scale).astype(BF16)
        hidden.append(lax.all_gather(units, "ep", axis=0, axis_index_groups=line, tiled=True))

    place = jnp.broadcast_to(across[:experts, :, None], (experts, size * count, 128))
    mixed = down_and_mix(spans, base, which, place, hidden, w_down, weave(held[4:]))
    mine, twin, far, far_twin = (mixed[:, k * LANES : k * LANES + width] for k in range(4))
    moved = to_twin(jnp.concatenate([far_twin, twin], axis=0).astype(BF16)).astype(F32)
    tokens_all = size * count
    far = to_cross((far + moved[:tokens_all]).astype(BF16)).astype(F32)
    mixed = (mine + moved[tokens_all:] + far).astype(BF16)
    mixed = lax.all_to_all(
        mixed.reshape(size, count, width), "ep", split_axis=0, concat_axis=0, tiled=True
    )
    return mixed.swapaxes(0, 1).reshape(count, size * width)


def solution(mesh):
    size, inner = mesh.shape["ep"], mesh.shape["tp"]

    def body(tokens, expert_ids, gate_weights, w_gate, w_up, w_down):
        rows = size * math.prod(expert_ids.shape)
        sums = rows * w_gate.shape[2]
        experts, width, units = w_gate.shape
        even = (
            size % 4 == 0
            and size > 4
            and mesh.shape["parts"] == 2
            and rows % (2 * BLOCK) == 0
            and units == 8 * UNITS
            and 3 * experts <= UNITS
            and size * math.prod(expert_ids.shape[:1]) % 128 == 0
            and width + 4 * expert_ids.shape[1] <= LANES
        )
        args = (tokens, expert_ids, gate_weights, w_gate, w_up, w_down)
        if inner == 1 and even and sums <= 3 * math.prod(w_gate.shape):
            return fixed_weights(size, *args)
        return moved_weights(*args)

    placed = (
        P(("parts", "ep"), "tp"),
        P(("parts", "ep"), None),
        P(("parts", "ep"), None),
        P(None, "ep", "tp"),
        P(None, "ep", "tp"),
        P(None, "tp", "ep"),
    )
    return jax.shard_map(
        body, mesh=mesh, in_specs=placed, out_specs=P(("parts", "ep"), "tp"), check_vma=False
    )
```

```python
import functools
import math

import jax
import jax.numpy as jnp
from jax import lax
from jax.experimental import pallas as pl
from jax.experimental.pallas import tpu as pltpu
from jax.sharding import PartitionSpec as P

BF16 = jnp.bfloat16
F32 = jnp.float32
TILE = 256
BLOCK = 1024
LANES = 256
UNITS = 128


def slots_of(block_ids, experts):
    flat = block_ids.reshape(-1)
    onehot = (flat[:, None] == jnp.arange(experts, dtype=jnp.int32)[None, :]).astype(jnp.int32)
    before = jnp.cumsum(onehot, axis=0) - onehot
    return jnp.sum(before * onehot, axis=1).reshape(block_ids.shape)


def fill_slots(rows, expert_ids, slot, experts, per_expert):
    count, picks = expert_ids.shape
    spread = jnp.broadcast_to(rows[:, None, :], (count, picks, rows.shape[1]))
    empty = jnp.zeros((experts, per_expert, rows.shape[1]), BF16)
    return empty.at[expert_ids, slot].set(spread)


def moved_weights(tokens, expert_ids, gate_weights, w_gate, w_up, w_down):
    tok_rows, picks = expert_ids.shape
    experts = w_gate.shape[0]
    per_expert = min(tok_rows, 3 * tok_rows * picks // (2 * experts))
    slot = slots_of(expert_ids, experts)
    features = lax.all_gather(tokens, "tp", axis=1, tiled=True)
    outgoing = fill_slots(features, expert_ids, slot, experts, per_expert)
    arrived = lax.all_to_all(outgoing, "ep", split_axis=0, concat_axis=1, tiled=True)
    gate_owned, up_owned = (
        lax.all_to_all(w_gate, "ep", split_axis=0, concat_axis=1, tiled=True),
        lax.all_to_all(w_up, "ep", split_axis=0, concat_axis=1, tiled=True),
    )
    gate = jnp.einsum("ecd,edf->ecf", arrived, gate_owned, preferred_element_type=F32)
    up = jnp.einsum("ecd,edf->ecf", arrived, up_owned, preferred_element_type=F32)
    hidden = (jax.nn.silu(gate) * up).astype(BF16)
    down_owned = lax.all_to_all(w_down, "ep", split_axis=0, concat_axis=2, tiled=True)
    partial_value = jnp.einsum("ecf,efd->ecd", hidden, down_owned, preferred_element_type=F32)
    expert_out = lax.psum_scatter(
        partial_value.astype(BF16), "tp", scatter_dimension=2, tiled=True
    )
    returned = lax.all_to_all(expert_out, "ep", split_axis=1, concat_axis=0, tiled=True)
    picked = returned[expert_ids, slot]
    mixed = jnp.sum(gate_weights[:, :, None] * picked.astype(F32), axis=1)
    return mixed.astype(BF16)


def dot(a, b, contract):
    return lax.dot_general(a, b, ((contract[0], contract[1]), ((), ())), preferred_element_type=F32)


def params(mib=48):
    return pltpu.CompilerParams(vmem_limit_bytes=mib << 20)


def cost(flops, moved):
    return pl.CostEstimate(flops=flops, bytes_accessed=moved, transcendentals=0)


def split3(value):
    high = lax.reduce_precision(value, 8, 7)
    middle = lax.reduce_precision(value - high, 8, 7)
    return high, middle, lax.reduce_precision(value - high - middle, 8, 7)


def order_kernel(width, picks, experts, note_ref, place_out, across_out, gates_out, base_out):
    tokens = note_ref.shape[0]
    note = note_ref[...].astype(F32)
    lane = lax.broadcasted_iota(jnp.int32, (tokens, UNITS), 1)
    name = jnp.where(lane < 3 * experts, lane % experts, -1).astype(F32)
    gates = jnp.zeros((tokens, UNITS), F32)
    for k in range(picks):
        one = note[:, width + k : width + k + 1]
        weight = (
            note[:, width + picks + k : width + picks + k + 1]
            + note[:, width + 2 * picks + k : width + 2 * picks + k + 1]
            + note[:, width + 3 * picks + k : width + 3 * picks + k + 1]
        )
        gates = jnp.where(name == one, weight, gates)
    mask = jnp.where((gates != 0.0) & (lane < experts), 1.0, 0.0)
    high = gates.astype(BF16)
    middle = (gates - high.astype(F32)).astype(BF16)
    rest = (gates - high.astype(F32) - middle.astype(F32)).astype(BF16)
    gates_out[...] = jnp.where(
        lane < experts,
        high.astype(F32),
        jnp.where(lane < 2 * experts, middle.astype(F32), rest.astype(F32)),
    ).astype(BF16)
    row = lax.broadcasted_iota(jnp.int32, (tokens, tokens), 0)
    column = lax.broadcasted_iota(jnp.int32, (tokens, tokens), 1)
    upto = jnp.where(column <= row, 1.0, 0.0).astype(BF16)
    count = dot(upto, mask.astype(BF16), ((1,), (0,)))
    total = jnp.broadcast_to(count[tokens - 1 : tokens, :], (8, UNITS))
    large = jnp.floor(total * (1.0 / 128.0))
    row = lax.broadcasted_iota(jnp.int32, (UNITS, UNITS), 0)
    column = lax.broadcasted_iota(jnp.int32, (UNITS, UNITS), 1)
    before = jnp.where(row < column, 1.0, 0.0).astype(BF16)
    base = 128.0 * dot(large.astype(BF16), before, ((1,), (0,)))
    base += dot((total - 128.0 * large).astype(BF16), before, ((1,), (0,)))
    base_out[...] = base.astype(jnp.int32)
    place = jnp.where(mask > 0.0, count - 1.0 + base[0:1, :], -1.0)
    place_out[...] = place.astype(jnp.int32)
    across_out[...] = place.T.astype(jnp.int32)


def order_of(note, width, picks, experts):
    tokens = note.shape[0]
    return pl.pallas_call(
        functools.partial(order_kernel, width, picks, experts),
        out_shape=[
            jax.ShapeDtypeStruct((tokens, UNITS), jnp.int32),
            jax.ShapeDtypeStruct((UNITS, tokens), jnp.int32),
            jax.ShapeDtypeStruct((tokens, UNITS), BF16),
            jax.ShapeDtypeStruct((8, UNITS), jnp.int32),
        ],
        compiler_params=params(),
        cost_estimate=cost(2 * tokens * tokens * UNITS, 4 * tokens * tokens),
        name="order",
    )(note)


def spans_of(base, rows):
    low = jnp.arange(rows // TILE, dtype=jnp.int32)[:, None] * TILE
    return (
        jnp.sum((base[None, 1:] <= low).astype(jnp.int32), axis=1),
        jnp.sum((base[None, :-1] < low + TILE).astype(jnp.int32), axis=1),
    )


def mine_of(base, e, row0):
    row = row0 + lax.broadcasted_iota(jnp.int32, (TILE, 1), 0)
    return (row >= base[e]) & (row < base[e + 1])


def sort_kernel(experts, low, high, base, across_ref, gates_ref, *refs):
    slices, (out, scale_out, onehot_ref, name_ref) = refs[:-4], refs[-4:]
    tokens = onehot_ref.shape[1]
    number = lax.broadcasted_iota(jnp.int32, (TILE, 128), 0).astype(F32).astype(BF16)
    onehot_ref[...] = jnp.zeros_like(onehot_ref)

    @pl.loop(0, BLOCK // TILE)
    def _(part):
        i = pl.program_id(0) * (BLOCK // TILE) + part
        row0 = i * TILE
        here = pl.ds(pl.multiple_of(part * TILE, TILE), TILE)

        @pl.loop(low[i], high[i])
        def _(e):
            away = across_ref[e] - row0
            away = jnp.where((away >= 0) & (away < TILE), away, -1).astype(F32)
            for c in range(tokens // 128):
                at = slice(c * 128, (c + 1) * 128)
                hit = number == away[c : c + 1, :].astype(BF16)
                onehot_ref[here, at] = jnp.where(hit, jnp.ones((), BF16), onehot_ref[here, at])
            name_ref[here, :] = jnp.where(mine_of(base, e, row0), e, name_ref[here, :])

    onehot = onehot_ref[...]
    for k, ref in enumerate(slices):
        out[:, k * LANES : (k + 1) * LANES] = dot(onehot, ref[...], ((1,), (0,))).astype(BF16)
    gates = dot(onehot, gates_ref[...], ((1,), (0,)))
    lane = lax.broadcasted_iota(jnp.int32, (BLOCK, UNITS), 1)
    name = name_ref[...]
    kept = (lane == name) | (lane == name + experts) | (lane == name + 2 * experts)
    scale = jnp.sum(jnp.where(kept, gates, 0.0), axis=1, keepdims=True)
    scale_out[...] = jnp.broadcast_to(scale, lane.shape)


def sort_rows(spans, base, across, gates, slices, rows, experts):
    tokens = gates.shape[0]
    across = across[:experts].reshape(experts, tokens // 128, 128)
    whole = lambda i, *_: (0, 0)
    width = len(slices) * LANES
    return pl.pallas_call(
        functools.partial(sort_kernel, experts),
        grid_spec=pltpu.PrefetchScalarGridSpec(
            num_scalar_prefetch=3,
            grid=(rows // BLOCK,),
            in_specs=[
                pl.BlockSpec(across.shape, lambda i, *_: (0, 0, 0)),
                pl.BlockSpec((tokens, UNITS), whole),
            ]
            + [pl.BlockSpec((tokens, LANES), whole)] * len(slices),
            out_specs=[
                pl.BlockSpec((BLOCK, width), lambda i, *_: (i, 0)),
                pl.BlockSpec((BLOCK, UNITS), lambda i, *_: (i, 0)),
                pl.BlockSpec((BLOCK, tokens), lambda i, *_: (i, 0)),
            ],
            scratch_shapes=[pltpu.VMEM((BLOCK, UNITS), jnp.int32)],
        ),
        out_shape=[
            jax.ShapeDtypeStruct((rows, width), BF16),
            jax.ShapeDtypeStruct((rows, UNITS), F32),
            jax.ShapeDtypeStruct((rows, tokens), BF16),
        ],
        compiler_params=params(),
        cost_estimate=cost(2 * rows * tokens * width, 8 * rows * width),
        name="sort_rows",
    )(*spans, base, across, gates, *slices)


def sort_more_kernel(onehot_ref, *refs):
    for k, ref in enumerate(refs[:-1]):
        at = slice(k * LANES, (k + 1) * LANES)
        refs[-1][:, at] = dot(onehot_ref[...], ref[...], ((1,), (0,))).astype(BF16)


def sort_more(onehot, slices):
    rows, tokens = onehot.shape
    width = len(slices) * LANES
    return pl.pallas_call(
        sort_more_kernel,
        grid=(rows // BLOCK,),
        in_specs=[pl.BlockSpec((BLOCK, tokens), lambda i: (i, 0))]
        + [pl.BlockSpec((tokens, LANES), lambda i: (0, 0))] * len(slices),
        out_specs=pl.BlockSpec((BLOCK, width), lambda i: (i, 0)),
        out_shape=jax.ShapeDtypeStruct((rows, width), BF16),
        compiler_params=params(),
        cost_estimate=cost(2 * rows * tokens * width, 8 * rows * width),
        name="sort_more",
    )(onehot, *slices)


def scatter_kernel(low, high, place_ref, onehot_ref):
    tokens = place_ref.shape[1]
    lane = lax.broadcasted_iota(jnp.int32, (tokens, 128), 1)
    onehot_ref[...] = jnp.zeros_like(onehot_ref)
    for part in range(BLOCK // TILE):
        i = pl.program_id(0) * (BLOCK // TILE) + part

        @pl.loop(low[i], high[i])
        def _(e):
            place = place_ref[e] - i * TILE
            for c in range(TILE // 128):
                at = slice(part * TILE + c * 128, part * TILE + (c + 1) * 128)
                onehot_ref[:, at] += jnp.where(place == lane + c * 128, 1.0, 0.0).astype(BF16)


def scatter_rows(spans, place, rows):
    tokens = place.shape[1]
    return pl.pallas_call(
        scatter_kernel,
        grid_spec=pltpu.PrefetchScalarGridSpec(
            num_scalar_prefetch=2,
            grid=(rows // BLOCK,),
            in_specs=[pl.BlockSpec(place.shape, lambda i, *_: (0, 0, 0))],
            out_specs=pl.BlockSpec((tokens, BLOCK), lambda i, *_: (0, i)),
        ),
        out_shape=jax.ShapeDtypeStruct((tokens, rows), BF16),
        compiler_params=params(),
        cost_estimate=cost(rows * tokens, 2 * rows * tokens),
        name="scatter_rows",
    )(*spans, place)


def partial_kernel(low, high, base, quarter, near_ref, far_ref, *refs):
    pairs, out = [refs[j : j + 2] for j in range(0, 8, 2)], refs[-1]
    width = pairs[0][0].shape[1]

    @pl.loop(0, BLOCK // TILE)
    def _(part):
        i = pl.program_id(0) * (BLOCK // TILE) + part
        here = pl.ds(pl.multiple_of(part * TILE, TILE), TILE)

        def add(e, kept):
            total = 0.0
            for k, pair in enumerate(pairs):
                weight = jnp.concatenate([pair[0][e], pair[1][e]], axis=1)
                rows_ref, at = (near_ref, far_ref)[k // 2], k % 2 * LANES
                rows = rows_ref[here, at : at + width]
                total += dot(rows, weight, ((1,), (0,)))
            return jnp.where(mine_of(base, e, i * TILE), total, kept)

        out[here, :] = lax.fori_loop(
            low[i], high[i], add, jnp.zeros((TILE, out.shape[1]), F32)
        ).astype(BF16)


def partial_sums(f, spans, base, quarter, near, far, w_gate, w_up, pieces):
    rows = near.shape[0]
    experts, width, _ = w_gate.shape
    own = pl.BlockSpec((experts, width, UNITS), lambda i, lo, hi, b, q: (0, 0, 2 * q[0] + f))
    block = pl.BlockSpec((experts, width, UNITS), lambda i, *_: (0, 0, 0))
    return pl.pallas_call(
        partial_kernel,
        grid_spec=pltpu.PrefetchScalarGridSpec(
            num_scalar_prefetch=4,
            grid=(rows // BLOCK,),
            in_specs=[pl.BlockSpec((BLOCK, 2 * LANES), lambda i, *_: (i, 0))] * 2 + [own] * 2
            + [block] * len(pieces),
            out_specs=pl.BlockSpec((BLOCK, 2 * UNITS), lambda i, *_: (i, 0)),
        ),
        out_shape=jax.ShapeDtypeStruct((rows, 2 * UNITS), BF16),
        compiler_params=params(),
        cost_estimate=cost(16 * rows * LANES * UNITS, 8 * rows * LANES),
        name="partial_sums",
    )(*spans, base, quarter, near, far, w_gate, w_up, *pieces)


def down_kernel(near, half, low, high, base, quarter, onehot_ref, hidden, start, *refs):
    weights, (out, total_ref, value_ref) = refs[:-3], refs[-3:]
    count = out.shape[1] // LANES
    width = weights[0].shape[1]
    j = pl.program_id(0)

    @pl.when(j == 0)
    def _():
        total_ref[...] = jnp.zeros_like(total_ref) if start is None else start[...]
        value_ref[...] = jnp.zeros_like(value_ref)

    for part in range(BLOCK // TILE):
        i = (2 * j + half) * (BLOCK // TILE) + part
        here = slice(part * TILE, (part + 1) * TILE)
        units = hidden[here, :]

        @pl.loop(low[i], high[i])
        def _(e):
            mine = mine_of(base, e, i * TILE)
            rest = list(weights)
            for k in range(count):
                first = rest.pop(0)
                weight = first[e]
                if not (near and k == 0):
                    weight = jnp.concatenate([weight, rest.pop(0)[e]], axis=1)
                value = dot(units, weight, ((1,), (1,)))
                at = slice(k * LANES, k * LANES + width)
                value_ref[here, at] = jnp.where(
                    mine, value, value_ref[here, at].astype(F32)
                ).astype(BF16)

    total_ref[...] += dot(onehot_ref[...], value_ref[...], ((1,), (0,)))

    @pl.when(j == pl.num_programs(0) - 1)
    def _():
        out[...] = total_ref[...].astype(out.dtype)


def down_and_mix(near, half, spans, base, quarter, onehot, hidden, start, weights, count, dtype):
    rows, units = hidden.shape
    experts, width, _ = weights[0].shape
    tokens = onehot.shape[0]
    block = pl.BlockSpec((BLOCK, units), lambda j, *_: (j, 0))
    own = pl.BlockSpec((experts, width, units), lambda j, lo, hi, b, q: (0, 0, q[0]))
    piece = pl.BlockSpec((experts, width, UNITS), lambda j, *_: (0, 0, 0))
    whole = pl.BlockSpec((tokens, count * LANES), lambda j, *_: (0, 0))
    kernel = functools.partial(down_kernel, near, half)
    if start is None:
        kernel = lambda *refs: down_kernel(near, half, *refs[:6], None, *refs[6:])
    return pl.pallas_call(
        kernel,
        grid_spec=pltpu.PrefetchScalarGridSpec(
            num_scalar_prefetch=4,
            grid=(rows // BLOCK,),
            in_specs=[pl.BlockSpec((tokens, BLOCK), lambda j, *_: (0, 2 * j + half)), block]
            + ([] if start is None else [whole])
            + ([own] + [piece] * (len(weights) - 1) if near else [piece] * len(weights)),
            out_specs=whole,
            scratch_shapes=[
                pltpu.VMEM((tokens, count * LANES), F32),
                pltpu.VMEM((BLOCK, count * LANES), BF16),
            ],
        ),
        out_shape=jax.ShapeDtypeStruct((tokens, count * LANES), dtype),
        compiler_params=params(56),
        cost_estimate=cost(2 * rows * tokens * LANES * count, 2 * rows * tokens),
        name="down_and_mix",
    )(*spans, base, quarter, onehot, hidden, *([] if start is None else [start]), *weights)


def fixed_weights(size, tokens, expert_ids, gate_weights, w_gate, w_up, w_down):
    count, picks = expert_ids.shape
    experts, width, hidden_units = w_gate.shape
    quarter = hidden_units // 4
    rows = size * count * picks
    places = size // 4
    me, plane = lax.axis_index("ep"), lax.axis_index("parts")
    w_down = jnp.swapaxes(w_down, 1, 2)

    twins = [(i, i ^ 1) for i in range(size)]
    cross = [(p * size + i, p * size + (i ^ 2 ^ p)) for p in range(2) for i in range(size)]
    to_twin = lambda value: lax.ppermute(value, "ep", twins)
    to_cross = lambda value: lax.ppermute(value, ("parts", "ep"), cross)
    to_plane = lambda value: lax.ppermute(value, "parts", [(0, 1), (1, 0)])
    line = [[4 * p + k for p in range(places)] for k in range(4)]
    my_quarter = me % 4
    twin_quarter = my_quarter ^ 1
    cross_quarter = my_quarter ^ 2 ^ plane

    note = jnp.concatenate([expert_ids.astype(F32), *split3(gate_weights)], axis=1).astype(BF16)
    fill = LANES - width - note.shape[1]
    parcels = jnp.concatenate(
        [
            tokens.reshape(count, size, width).swapaxes(0, 1),
            jnp.broadcast_to(jnp.pad(note, ((0, 0), (0, fill)))[None], (size, count, LANES - width)),
        ],
        axis=2,
    )
    own = lax.all_to_all(parcels, "ep", split_axis=0, concat_axis=0, tiled=True)
    own = own.reshape(size * count, LANES)
    far = to_cross(own)
    slices = [own, to_twin(own), far, to_twin(far)]
    place, across, gates, base = order_of(own, width, picks, experts)
    base = base[0, : experts + 1]
    spans = spans_of(base, rows)
    which = my_quarter.astype(jnp.int32).reshape(1)

    def cut(w, q, f):
        return lax.dynamic_slice_in_dim(w, q * quarter + f * UNITS, UNITS, 2)

    last = ()
    held, crossed = [], []
    for n, (f, w) in enumerate(
        ((0, w_gate), (0, w_up), (1, w_gate), (1, w_up), (0, w_down), (1, w_down))
    ):
        piece = cut(w, cross_quarter, f)
        if n:
            last = (crossed[0],) if n == 1 else (far, crossed[1], crossed[n // 2 * 2 - 1])
            piece = lax.optimization_barrier((piece, *last))[0]
        crossed.append(to_cross(piece))
        held.append((to_twin(cut(w, twin_quarter, f)), crossed[n], to_plane(crossed[n])))
    weave = lambda pair: [piece for both in zip(*pair) for piece in both]

    near_rows, scale, onehot = sort_rows(spans, base, across, gates, slices[:2], rows, experts)
    far_rows = sort_more(onehot, slices[2:])
    scale = lax.dynamic_slice_in_dim(scale, (me // 4) * (rows // places), rows // places, 0)
    units = []
    for f in range(2):
        pieces = weave(held[2 * f : 2 * f + 2])
        sums = partial_sums(f, spans, base, which, near_rows, far_rows, w_gate, w_up, pieces)
        later = sums
        sums = lax.psum_scatter(
            sums, "ep", scatter_dimension=0, axis_index_groups=line, tiled=True
        ).astype(F32)
        units.append((jax.nn.silu(sums[:, :UNITS]) * sums[:, UNITS:] * scale).astype(BF16))
    units = jnp.concatenate(units, axis=1).reshape(-1, BLOCK, 2 * UNITS)
    hidden = [
        lax.all_gather(units[half], "ep", axis=0, axis_index_groups=line, tiled=True)
        for half in range(2)
    ]

    across = lax.optimization_barrier((across[:experts], later))[0]
    place = jnp.broadcast_to(across[:, :, None], (experts, size * count, 128))
    columns = scatter_rows(spans, place, rows)
    near_weights, far_weights = weave(held[4:])[:2], weave(held[4:])[2:]
    near_weights = [w_down] + near_weights
    mix = lambda near, half, start, dtype: down_and_mix(
        near, half, spans, base, which, columns, hidden[half], start,
        near_weights if near else far_weights, 2, dtype,
    )
    far = mix(False, 1, mix(False, 0, None, F32), BF16)
    near = mix(True, 0, None, F32)
    near = mix(True, 1, lax.optimization_barrier((near, far))[0], F32)
    far, far_twin = far[:, :width], far[:, LANES : LANES + width]
    far = (far.astype(F32) + to_twin(far_twin).astype(F32)).astype(BF16)
    far = to_cross(far).astype(F32)
    twin = to_twin(near[:, LANES : LANES + width].astype(BF16)).astype(F32)
    mixed = (near[:, :width] + twin + far).astype(BF16)
    mixed = lax.all_to_all(
        mixed.reshape(size, count, width), "ep", split_axis=0, concat_axis=0, tiled=True
    )
    return mixed.swapaxes(0, 1).reshape(count, size * width)


def solution(mesh):
    size, inner = mesh.shape["ep"], mesh.shape["tp"]

    def body(tokens, expert_ids, gate_weights, w_gate, w_up, w_down):
        rows = size * math.prod(expert_ids.shape)
        sums = rows * w_gate.shape[2]
        experts, width, units = w_gate.shape
        even = (
            size % 4 == 0
            and size > 4
            and mesh.shape["parts"] == 2
            and rows == size // 4 * 2 * BLOCK
            and units == 8 * UNITS
            and 3 * experts <= UNITS
            and size * math.prod(expert_ids.shape[:1]) % 128 == 0
            and width + 4 * expert_ids.shape[1] <= LANES
        )
        args = (tokens, expert_ids, gate_weights, w_gate, w_up, w_down)
        if inner == 1 and even and sums <= 3 * math.prod(w_gate.shape):
            return fixed_weights(size, *args)
        return moved_weights(*args)

    placed = (
        P(("parts", "ep"), "tp"),
        P(("parts", "ep"), None),
        P(("parts", "ep"), None),
        P(None, "ep", "tp"),
        P(None, "ep", "tp"),
        P(None, "tp", "ep"),
    )
    return jax.shard_map(
        body, mesh=mesh, in_specs=placed, out_specs=P(("parts", "ep"), "tp"), check_vma=False
    )
```

```python
import functools
import math

import jax
import jax.numpy as jnp
from jax import lax
from jax.experimental import pallas as pl
from jax.experimental.pallas import tpu as pltpu
from jax.sharding import PartitionSpec as P

BF16 = jnp.bfloat16
F32 = jnp.float32
TILE = 256
BLOCK = 1024
LANES = 256
UNITS = 128


def slots_of(block_ids, experts):
    flat = block_ids.reshape(-1)
    onehot = (flat[:, None] == jnp.arange(experts, dtype=jnp.int32)[None, :]).astype(jnp.int32)
    before = jnp.cumsum(onehot, axis=0) - onehot
    return jnp.sum(before * onehot, axis=1).reshape(block_ids.shape)


def fill_slots(rows, expert_ids, slot, experts, per_expert):
    count, picks = expert_ids.shape
    spread = jnp.broadcast_to(rows[:, None, :], (count, picks, rows.shape[1]))
    empty = jnp.zeros((experts, per_expert, rows.shape[1]), BF16)
    return empty.at[expert_ids, slot].set(spread)


def moved_weights(tokens, expert_ids, gate_weights, w_gate, w_up, w_down):
    tok_rows, picks = expert_ids.shape
    experts = w_gate.shape[0]
    per_expert = min(tok_rows, 3 * tok_rows * picks // (2 * experts))
    slot = slots_of(expert_ids, experts)
    features = lax.all_gather(tokens, "tp", axis=1, tiled=True)
    outgoing = fill_slots(features, expert_ids, slot, experts, per_expert)
    arrived = lax.all_to_all(outgoing, "ep", split_axis=0, concat_axis=1, tiled=True)
    gate_owned, up_owned = (
        lax.all_to_all(w_gate, "ep", split_axis=0, concat_axis=1, tiled=True),
        lax.all_to_all(w_up, "ep", split_axis=0, concat_axis=1, tiled=True),
    )
    gate = jnp.einsum("ecd,edf->ecf", arrived, gate_owned, preferred_element_type=F32)
    up = jnp.einsum("ecd,edf->ecf", arrived, up_owned, preferred_element_type=F32)
    hidden = (jax.nn.silu(gate) * up).astype(BF16)
    down_owned = lax.all_to_all(w_down, "ep", split_axis=0, concat_axis=2, tiled=True)
    partial_value = jnp.einsum("ecf,efd->ecd", hidden, down_owned, preferred_element_type=F32)
    expert_out = lax.psum_scatter(
        partial_value.astype(BF16), "tp", scatter_dimension=2, tiled=True
    )
    returned = lax.all_to_all(expert_out, "ep", split_axis=1, concat_axis=0, tiled=True)
    picked = returned[expert_ids, slot]
    mixed = jnp.sum(gate_weights[:, :, None] * picked.astype(F32), axis=1)
    return mixed.astype(BF16)


def dot(a, b, contract):
    return lax.dot_general(a, b, ((contract[0], contract[1]), ((), ())), preferred_element_type=F32)


def params(mib=48):
    return pltpu.CompilerParams(vmem_limit_bytes=mib << 20)


def cost(flops, moved):
    return pl.CostEstimate(flops=flops, bytes_accessed=moved, transcendentals=0)


def split3(value):
    high = lax.reduce_precision(value, 8, 7)
    middle = lax.reduce_precision(value - high, 8, 7)
    return high, middle, lax.reduce_precision(value - high - middle, 8, 7)


def order_kernel(width, picks, experts, note_ref, place_out, across_out, gates_out, base_out):
    tokens = note_ref.shape[0]
    note = note_ref[...].astype(F32)
    lane = lax.broadcasted_iota(jnp.int32, (tokens, UNITS), 1)
    name = jnp.where(lane < 3 * experts, lane % experts, -1).astype(F32)
    gates = jnp.zeros((tokens, UNITS), F32)
    for k in range(picks):
        one = note[:, width + k : width + k + 1]
        weight = (
            note[:, width + picks + k : width + picks + k + 1]
            + note[:, width + 2 * picks + k : width + 2 * picks + k + 1]
            + note[:, width + 3 * picks + k : width + 3 * picks + k + 1]
        )
        gates = jnp.where(name == one, weight, gates)
    mask = jnp.where((gates != 0.0) & (lane < experts), 1.0, 0.0)
    high = gates.astype(BF16)
    middle = (gates - high.astype(F32)).astype(BF16)
    rest = (gates - high.astype(F32) - middle.astype(F32)).astype(BF16)
    gates_out[...] = jnp.where(
        lane < experts,
        high.astype(F32),
        jnp.where(lane < 2 * experts, middle.astype(F32), rest.astype(F32)),
    ).astype(BF16)
    row = lax.broadcasted_iota(jnp.int32, (tokens, tokens), 0)
    column = lax.broadcasted_iota(jnp.int32, (tokens, tokens), 1)
    upto = jnp.where(column <= row, 1.0, 0.0).astype(BF16)
    count = dot(upto, mask.astype(BF16), ((1,), (0,)))
    total = jnp.broadcast_to(count[tokens - 1 : tokens, :], (8, UNITS))
    large = jnp.floor(total * (1.0 / 128.0))
    row = lax.broadcasted_iota(jnp.int32, (UNITS, UNITS), 0)
    column = lax.broadcasted_iota(jnp.int32, (UNITS, UNITS), 1)
    before = jnp.where(row < column, 1.0, 0.0).astype(BF16)
    base = 128.0 * dot(large.astype(BF16), before, ((1,), (0,)))
    base += dot((total - 128.0 * large).astype(BF16), before, ((1,), (0,)))
    base_out[...] = base.astype(jnp.int32)
    place = jnp.where(mask > 0.0, count - 1.0 + base[0:1, :], -1.0)
    place_out[...] = place.astype(jnp.int32)
    across_out[...] = place.T.astype(jnp.int32)


def order_of(note, width, picks, experts):
    tokens = note.shape[0]
    return pl.pallas_call(
        functools.partial(order_kernel, width, picks, experts),
        out_shape=[
            jax.ShapeDtypeStruct((tokens, UNITS), jnp.int32),
            jax.ShapeDtypeStruct((UNITS, tokens), jnp.int32),
            jax.ShapeDtypeStruct((tokens, UNITS), BF16),
            jax.ShapeDtypeStruct((8, UNITS), jnp.int32),
        ],
        compiler_params=params(),
        cost_estimate=cost(2 * tokens * tokens * UNITS, 4 * tokens * tokens),
        name="order",
    )(note)


def spans_of(base, rows):
    low = jnp.arange(rows // TILE, dtype=jnp.int32)[:, None] * TILE
    return (
        jnp.sum((base[None, 1:] <= low).astype(jnp.int32), axis=1),
        jnp.sum((base[None, :-1] < low + TILE).astype(jnp.int32), axis=1),
    )


def mine_of(base, e, row0):
    row = row0 + lax.broadcasted_iota(jnp.int32, (TILE, 1), 0)
    return (row >= base[e]) & (row < base[e + 1])


def sort_kernel(experts, low, high, base, across_ref, gates_ref, *refs):
    slices, (out, scale_out, onehot_ref, name_ref) = refs[:-4], refs[-4:]
    tokens = onehot_ref.shape[1]
    number = lax.broadcasted_iota(jnp.int32, (TILE, 128), 0).astype(F32).astype(BF16)
    onehot_ref[...] = jnp.zeros_like(onehot_ref)

    @pl.loop(0, BLOCK // TILE)
    def _(part):
        i = pl.program_id(0) * (BLOCK // TILE) + part
        row0 = i * TILE
        here = pl.ds(pl.multiple_of(part * TILE, TILE), TILE)

        @pl.loop(low[i], high[i])
        def _(e):
            away = across_ref[e] - row0
            away = jnp.where((away >= 0) & (away < TILE), away, -1).astype(F32)
            for c in range(tokens // 128):
                at = slice(c * 128, (c + 1) * 128)
                hit = number == away[c : c + 1, :].astype(BF16)
                onehot_ref[here, at] = jnp.where(hit, jnp.ones((), BF16), onehot_ref[here, at])
            name_ref[here, :] = jnp.where(mine_of(base, e, row0), e, name_ref[here, :])

    onehot = onehot_ref[...]
    for k, ref in enumerate(slices):
        out[:, k * LANES : (k + 1) * LANES] = dot(onehot, ref[...], ((1,), (0,))).astype(BF16)
    gates = dot(onehot, gates_ref[...], ((1,), (0,)))
    lane = lax.broadcasted_iota(jnp.int32, (BLOCK, UNITS), 1)
    name = name_ref[...]
    kept = (lane == name) | (lane == name + experts) | (lane == name + 2 * experts)
    scale = jnp.sum(jnp.where(kept, gates, 0.0), axis=1, keepdims=True)
    scale_out[...] = jnp.broadcast_to(scale, lane.shape)


def sort_rows(spans, base, across, gates, slices, rows, experts):
    tokens = gates.shape[0]
    across = across[:experts].reshape(experts, tokens // 128, 128)
    whole = lambda i, *_: (0, 0)
    width = len(slices) * LANES
    return pl.pallas_call(
        functools.partial(sort_kernel, experts),
        grid_spec=pltpu.PrefetchScalarGridSpec(
            num_scalar_prefetch=3,
            grid=(rows // BLOCK,),
            in_specs=[
                pl.BlockSpec(across.shape, lambda i, *_: (0, 0, 0)),
                pl.BlockSpec((tokens, UNITS), whole),
            ]
            + [pl.BlockSpec((tokens, LANES), whole)] * len(slices),
            out_specs=[
                pl.BlockSpec((BLOCK, width), lambda i, *_: (i, 0)),
                pl.BlockSpec((BLOCK, UNITS), lambda i, *_: (i, 0)),
                pl.BlockSpec((BLOCK, tokens), lambda i, *_: (i, 0)),
            ],
            scratch_shapes=[pltpu.VMEM((BLOCK, UNITS), jnp.int32)],
        ),
        out_shape=[
            jax.ShapeDtypeStruct((rows, width), BF16),
            jax.ShapeDtypeStruct((rows, UNITS), F32),
            jax.ShapeDtypeStruct((rows, tokens), BF16),
        ],
        compiler_params=params(),
        cost_estimate=cost(2 * rows * tokens * width, 8 * rows * width),
        name="sort_rows",
    )(*spans, base, across, gates, *slices)


def sort_more_kernel(onehot_ref, *refs):
    for k, ref in enumerate(refs[:-1]):
        at = slice(k * LANES, (k + 1) * LANES)
        refs[-1][:, at] = dot(onehot_ref[...], ref[...], ((1,), (0,))).astype(BF16)


def sort_more(onehot, slices):
    rows, tokens = onehot.shape
    width = len(slices) * LANES
    return pl.pallas_call(
        sort_more_kernel,
        grid=(rows // BLOCK,),
        in_specs=[pl.BlockSpec((BLOCK, tokens), lambda i: (i, 0))]
        + [pl.BlockSpec((tokens, LANES), lambda i: (0, 0))] * len(slices),
        out_specs=pl.BlockSpec((BLOCK, width), lambda i: (i, 0)),
        out_shape=jax.ShapeDtypeStruct((rows, width), BF16),
        compiler_params=params(),
        cost_estimate=cost(2 * rows * tokens * width, 8 * rows * width),
        name="sort_more",
    )(onehot, *slices)


def scatter_kernel(low, high, place_ref, onehot_ref):
    tokens = place_ref.shape[1]
    lane = lax.broadcasted_iota(jnp.int32, (tokens, 128), 1)
    onehot_ref[...] = jnp.zeros_like(onehot_ref)
    for part in range(BLOCK // TILE):
        i = pl.program_id(0) * (BLOCK // TILE) + part

        @pl.loop(low[i], high[i])
        def _(e):
            place = place_ref[e] - i * TILE
            for c in range(TILE // 128):
                at = slice(part * TILE + c * 128, part * TILE + (c + 1) * 128)
                onehot_ref[:, at] += jnp.where(place == lane + c * 128, 1.0, 0.0).astype(BF16)


def scatter_rows(spans, place, rows):
    tokens = place.shape[1]
    return pl.pallas_call(
        scatter_kernel,
        grid_spec=pltpu.PrefetchScalarGridSpec(
            num_scalar_prefetch=2,
            grid=(rows // BLOCK,),
            in_specs=[pl.BlockSpec(place.shape, lambda i, *_: (0, 0, 0))],
            out_specs=pl.BlockSpec((tokens, BLOCK), lambda i, *_: (0, i)),
        ),
        out_shape=jax.ShapeDtypeStruct((tokens, rows), BF16),
        compiler_params=params(),
        cost_estimate=cost(rows * tokens, 2 * rows * tokens),
        name="scatter_rows",
    )(*spans, place)


def partial_kernel(low, high, base, quarter, near_ref, far_ref, *refs):
    pairs, out = [refs[j : j + 2] for j in range(0, 8, 2)], refs[-1]
    width = pairs[0][0].shape[1]

    @pl.loop(0, BLOCK // TILE)
    def _(part):
        i = pl.program_id(0) * (BLOCK // TILE) + part
        here = pl.ds(pl.multiple_of(part * TILE, TILE), TILE)

        def add(e, kept):
            total = 0.0
            for k, pair in enumerate(pairs):
                weight = jnp.concatenate([pair[0][e], pair[1][e]], axis=1)
                rows_ref, at = (near_ref, far_ref)[k // 2], k % 2 * LANES
                rows = rows_ref[here, at : at + width]
                total += dot(rows, weight, ((1,), (0,)))
            return jnp.where(mine_of(base, e, i * TILE), total, kept)

        out[here, :] = lax.fori_loop(
            low[i], high[i], add, jnp.zeros((TILE, out.shape[1]), F32)
        ).astype(BF16)


def partial_sums(f, spans, base, quarter, near, far, w_gate, w_up, pieces):
    rows = near.shape[0]
    experts, width, _ = w_gate.shape
    own = pl.BlockSpec((experts, width, UNITS), lambda i, lo, hi, b, q: (0, 0, 2 * q[0] + f))
    block = pl.BlockSpec((experts, width, UNITS), lambda i, *_: (0, 0, 0))
    return pl.pallas_call(
        partial_kernel,
        grid_spec=pltpu.PrefetchScalarGridSpec(
            num_scalar_prefetch=4,
            grid=(rows // BLOCK,),
            in_specs=[pl.BlockSpec((BLOCK, 2 * LANES), lambda i, *_: (i, 0))] * 2 + [own] * 2
            + [block] * len(pieces),
            out_specs=pl.BlockSpec((BLOCK, 2 * UNITS), lambda i, *_: (i, 0)),
        ),
        out_shape=jax.ShapeDtypeStruct((rows, 2 * UNITS), BF16),
        compiler_params=params(),
        cost_estimate=cost(16 * rows * LANES * UNITS, 8 * rows * LANES),
        name="partial_sums",
    )(*spans, base, quarter, near, far, w_gate, w_up, *pieces)


def down_kernel(near, half, low, high, base, quarter, onehot_ref, hidden, start, *refs):
    weights, (out, total_ref, value_ref) = refs[:-3], refs[-3:]
    count = out.shape[1] // LANES
    width = weights[0].shape[1]
    j = pl.program_id(0)

    @pl.when(j == 0)
    def _():
        total_ref[...] = jnp.zeros_like(total_ref) if start is None else start[...]
        value_ref[...] = jnp.zeros_like(value_ref)

    for part in range(BLOCK // TILE):
        i = (2 * j + half) * (BLOCK // TILE) + part
        here = slice(part * TILE, (part + 1) * TILE)
        units = hidden[here, :]

        @pl.loop(low[i], high[i])
        def _(e):
            mine = mine_of(base, e, i * TILE)
            rest = list(weights)
            for k in range(count):
                first = rest.pop(0)
                weight = first[e]
                if not (near and k == 0):
                    weight = jnp.concatenate([weight, rest.pop(0)[e]], axis=1)
                value = dot(units, weight, ((1,), (1,)))
                at = slice(k * LANES, k * LANES + width)
                value_ref[here, at] = jnp.where(
                    mine, value, value_ref[here, at].astype(F32)
                ).astype(BF16)

    total_ref[...] += dot(onehot_ref[...], value_ref[...], ((1,), (0,)))

    @pl.when(j == pl.num_programs(0) - 1)
    def _():
        out[...] = total_ref[...].astype(out.dtype)


def down_and_mix(near, half, spans, base, quarter, onehot, hidden, start, weights, count, dtype):
    rows, units = hidden.shape
    experts, width, _ = weights[0].shape
    tokens = onehot.shape[0]
    block = pl.BlockSpec((BLOCK, units), lambda j, *_: (j, 0))
    own = pl.BlockSpec((experts, width, units), lambda j, lo, hi, b, q: (0, 0, q[0]))
    piece = pl.BlockSpec((experts, width, UNITS), lambda j, *_: (0, 0, 0))
    whole = pl.BlockSpec((tokens, count * LANES), lambda j, *_: (0, 0))
    kernel = functools.partial(down_kernel, near, half)
    if start is None:
        kernel = lambda *refs: down_kernel(near, half, *refs[:6], None, *refs[6:])
    return pl.pallas_call(
        kernel,
        grid_spec=pltpu.PrefetchScalarGridSpec(
            num_scalar_prefetch=4,
            grid=(rows // BLOCK,),
            in_specs=[pl.BlockSpec((tokens, BLOCK), lambda j, *_: (0, 2 * j + half)), block]
            + ([] if start is None else [whole])
            + ([own] + [piece] * (len(weights) - 1) if near else [piece] * len(weights)),
            out_specs=whole,
            scratch_shapes=[
                pltpu.VMEM((tokens, count * LANES), F32),
                pltpu.VMEM((BLOCK, count * LANES), BF16),
            ],
        ),
        out_shape=jax.ShapeDtypeStruct((tokens, count * LANES), dtype),
        compiler_params=params(56),
        cost_estimate=cost(2 * rows * tokens * LANES * count, 2 * rows * tokens),
        name="down_and_mix",
    )(*spans, base, quarter, onehot, hidden, *([] if start is None else [start]), *weights)


def fixed_weights(size, tokens, expert_ids, gate_weights, w_gate, w_up, w_down):
    count, picks = expert_ids.shape
    experts, width, hidden_units = w_gate.shape
    quarter = hidden_units // 4
    rows = size * count * picks
    places = size // 4
    me, plane = lax.axis_index("ep"), lax.axis_index("parts")
    w_down = jnp.swapaxes(w_down, 1, 2)

    twins = [(i, i ^ 1) for i in range(size)]
    cross = [(p * size + i, p * size + (i ^ 2 ^ p)) for p in range(2) for i in range(size)]
    to_twin = lambda value: lax.ppermute(value, "ep", twins)
    to_cross = lambda value: lax.ppermute(value, ("parts", "ep"), cross)
    to_plane = lambda value: lax.ppermute(value, "parts", [(0, 1), (1, 0)])
    line = [[4 * p + k for p in range(places)] for k in range(4)]
    my_quarter = me % 4
    twin_quarter = my_quarter ^ 1
    cross_quarter = my_quarter ^ 2 ^ plane

    note = jnp.concatenate([expert_ids.astype(F32), *split3(gate_weights)], axis=1).astype(BF16)
    fill = LANES - width - note.shape[1]
    parcels = jnp.concatenate(
        [
            tokens.reshape(count, size, width).swapaxes(0, 1),
            jnp.broadcast_to(jnp.pad(note, ((0, 0), (0, fill)))[None], (size, count, LANES - width)),
        ],
        axis=2,
    )
    own = lax.all_to_all(parcels, "ep", split_axis=0, concat_axis=0, tiled=True)
    own = own.reshape(size * count, LANES)
    far, near = to_cross(own), [own, to_twin(own)]
    place, across, gates, base = order_of(own, width, picks, experts)
    base = base[0, : experts + 1]
    spans = spans_of(base, rows)
    which = my_quarter.astype(jnp.int32).reshape(1)

    def cut(w, q, f):
        return lax.dynamic_slice_in_dim(w, q * quarter + f * UNITS, UNITS, 2)

    def after(value, *others):
        return lax.optimization_barrier((value, *others))[0]

    near_rows, scale, onehot = sort_rows(spans, base, across, gates, near, rows, experts)
    far = after(far, near_rows)
    far_rows = sort_more(onehot, [far, to_twin(far)])
    scale = lax.dynamic_slice_in_dim(scale, (me // 4) * (rows // places), rows // places, 0)

    held, crossed = [], []
    for n, (f, w) in enumerate(
        ((0, w_gate), (0, w_up), (1, w_gate), (1, w_up), (0, w_down), (1, w_down))
    ):
        piece = cut(w, cross_quarter, f)
        if n:
            piece = after(piece, crossed[n - 1] if n < 4 else crossed[3])
        if n == 2:
            piece = after(piece, far)
        crossed.append(to_cross(piece))
        held.append((to_twin(cut(w, twin_quarter, f)), crossed[n], to_plane(crossed[n])))
    weave = lambda pair: [piece for both in zip(*pair) for piece in both]

    units, later = [], crossed[2]
    for f in range(2):
        pieces = weave(held[2 * f : 2 * f + 2])
        far_rows = after(far_rows, later)
        later = partial_sums(f, spans, base, which, near_rows, far_rows, w_gate, w_up, pieces)
        sums = lax.psum_scatter(
            later, "ep", scatter_dimension=0, axis_index_groups=line, tiled=True
        ).astype(F32)
        units.append((jax.nn.silu(sums[:, :UNITS]) * sums[:, UNITS:] * scale).astype(BF16))

    place = jnp.broadcast_to(
        after(across[:experts], later)[:, :, None], (experts, size * count, 128)
    )
    columns = scatter_rows(spans, place, rows)
    units, columns, pieces = lax.optimization_barrier((units, columns, weave(held[4:])))
    units = jnp.concatenate(units, axis=1).reshape(-1, BLOCK, 2 * UNITS)
    first, second = (
        lax.all_gather(units[half], "ep", axis=0, axis_index_groups=line, tiled=True)
        for half in range(2)
    )
    far_mix = lambda half, hidden, start, dtype: down_and_mix(
        False, half, spans, base, which, columns, hidden, start, pieces[2:], 2, dtype
    )
    near_mix = lambda half, hidden, start, dtype: down_and_mix(
        True, half, spans, base, which, columns, hidden, start, [w_down] + pieces[:2], 2, dtype
    )
    far, near = far_mix(0, first, None, F32), near_mix(0, first, None, F32)
    second, far, near = lax.optimization_barrier((second, far, near))
    far = far_mix(1, second, far, BF16)
    far, far_twin = far[:, :width], far[:, LANES : LANES + width]
    far = (far.astype(F32) + to_twin(far_twin).astype(F32)).astype(BF16)
    near, far = lax.optimization_barrier((near, far))
    far = to_cross(far)
    near = near_mix(1, second, near, F32)
    twin = to_twin(near[:, LANES : LANES + width].astype(BF16)).astype(F32)
    mixed = (near[:, :width] + twin + far.astype(F32)).astype(BF16)
    mixed = lax.all_to_all(
        mixed.reshape(size, count, width), "ep", split_axis=0, concat_axis=0, tiled=True
    )
    return mixed.swapaxes(0, 1).reshape(count, size * width)


def solution(mesh):
    size, inner = mesh.shape["ep"], mesh.shape["tp"]

    def body(tokens, expert_ids, gate_weights, w_gate, w_up, w_down):
        rows = size * math.prod(expert_ids.shape)
        sums = rows * w_gate.shape[2]
        experts, width, units = w_gate.shape
        even = (
            size % 4 == 0
            and size > 4
            and mesh.shape["parts"] == 2
            and rows == size // 4 * 2 * BLOCK
            and units == 8 * UNITS
            and 3 * experts <= UNITS
            and size * math.prod(expert_ids.shape[:1]) % 128 == 0
            and width + 4 * expert_ids.shape[1] <= LANES
        )
        args = (tokens, expert_ids, gate_weights, w_gate, w_up, w_down)
        if inner == 1 and even and sums <= 3 * math.prod(w_gate.shape):
            return fixed_weights(size, *args)
        return moved_weights(*args)

    placed = (
        P(("parts", "ep"), "tp"),
        P(("parts", "ep"), None),
        P(("parts", "ep"), None),
        P(None, "ep", "tp"),
        P(None, "ep", "tp"),
        P(None, "tp", "ep"),
    )
    return jax.shard_map(
        body, mesh=mesh, in_specs=placed, out_specs=P(("parts", "ep"), "tp"), check_vma=False
    )
```

```python
import functools
import math

import jax
import jax.numpy as jnp
from jax import lax
from jax.experimental import pallas as pl
from jax.experimental.pallas import tpu as pltpu
from jax.sharding import PartitionSpec as P

BF16 = jnp.bfloat16
F32 = jnp.float32
TILE = 256
BLOCK = 1024
LANES = 256
UNITS = 128


def slots_of(block_ids, experts):
    flat = block_ids.reshape(-1)
    onehot = (flat[:, None] == jnp.arange(experts, dtype=jnp.int32)[None, :]).astype(jnp.int32)
    before = jnp.cumsum(onehot, axis=0) - onehot
    return jnp.sum(before * onehot, axis=1).reshape(block_ids.shape)


def fill_slots(rows, expert_ids, slot, experts, per_expert):
    count, picks = expert_ids.shape
    spread = jnp.broadcast_to(rows[:, None, :], (count, picks, rows.shape[1]))
    empty = jnp.zeros((experts, per_expert, rows.shape[1]), BF16)
    return empty.at[expert_ids, slot].set(spread)


def moved_weights(tokens, expert_ids, gate_weights, w_gate, w_up, w_down):
    tok_rows, picks = expert_ids.shape
    experts = w_gate.shape[0]
    per_expert = min(tok_rows, 3 * tok_rows * picks // (2 * experts))
    slot = slots_of(expert_ids, experts)
    features = lax.all_gather(tokens, "tp", axis=1, tiled=True)
    outgoing = fill_slots(features, expert_ids, slot, experts, per_expert)
    arrived = lax.all_to_all(outgoing, "ep", split_axis=0, concat_axis=1, tiled=True)
    gate_owned, up_owned = (
        lax.all_to_all(w_gate, "ep", split_axis=0, concat_axis=1, tiled=True),
        lax.all_to_all(w_up, "ep", split_axis=0, concat_axis=1, tiled=True),
    )
    gate = jnp.einsum("ecd,edf->ecf", arrived, gate_owned, preferred_element_type=F32)
    up = jnp.einsum("ecd,edf->ecf", arrived, up_owned, preferred_element_type=F32)
    hidden = (jax.nn.silu(gate) * up).astype(BF16)
    down_owned = lax.all_to_all(w_down, "ep", split_axis=0, concat_axis=2, tiled=True)
    partial_value = jnp.einsum("ecf,efd->ecd", hidden, down_owned, preferred_element_type=F32)
    expert_out = lax.psum_scatter(
        partial_value.astype(BF16), "tp", scatter_dimension=2, tiled=True
    )
    returned = lax.all_to_all(expert_out, "ep", split_axis=1, concat_axis=0, tiled=True)
    picked = returned[expert_ids, slot]
    mixed = jnp.sum(gate_weights[:, :, None] * picked.astype(F32), axis=1)
    return mixed.astype(BF16)


def dot(a, b, contract):
    return lax.dot_general(a, b, ((contract[0], contract[1]), ((), ())), preferred_element_type=F32)


def params(mib=48):
    return pltpu.CompilerParams(vmem_limit_bytes=mib << 20)


def cost(flops, moved):
    return pl.CostEstimate(flops=4 * flops, bytes_accessed=4 * moved, transcendentals=0)


def split3(value):
    high = lax.reduce_precision(value, 8, 7)
    middle = lax.reduce_precision(value - high, 8, 7)
    return high, middle, lax.reduce_precision(value - high - middle, 8, 7)


def order_kernel(width, picks, experts, note_ref, place_out, across_out, gates_out, base_out):
    tokens = note_ref.shape[0]
    note = note_ref[...].astype(F32)
    lane = lax.broadcasted_iota(jnp.int32, (tokens, UNITS), 1)
    name = jnp.where(lane < 3 * experts, lane % experts, -1).astype(F32)
    gates = jnp.zeros((tokens, UNITS), F32)
    for k in range(picks):
        one = note[:, width + k : width + k + 1]
        weight = (
            note[:, width + picks + k : width + picks + k + 1]
            + note[:, width + 2 * picks + k : width + 2 * picks + k + 1]
            + note[:, width + 3 * picks + k : width + 3 * picks + k + 1]
        )
        gates = jnp.where(name == one, weight, gates)
    mask = jnp.where((gates != 0.0) & (lane < experts), 1.0, 0.0)
    high = gates.astype(BF16)
    middle = (gates - high.astype(F32)).astype(BF16)
    rest = (gates - high.astype(F32) - middle.astype(F32)).astype(BF16)
    gates_out[...] = jnp.where(
        lane < experts,
        high.astype(F32),
        jnp.where(lane < 2 * experts, middle.astype(F32), rest.astype(F32)),
    ).astype(BF16)
    row = lax.broadcasted_iota(jnp.int32, (tokens, tokens), 0)
    column = lax.broadcasted_iota(jnp.int32, (tokens, tokens), 1)
    upto = jnp.where(column <= row, 1.0, 0.0).astype(BF16)
    count = dot(upto, mask.astype(BF16), ((1,), (0,)))
    total = jnp.broadcast_to(count[tokens - 1 : tokens, :], (8, UNITS))
    large = jnp.floor(total * (1.0 / 128.0))
    row = lax.broadcasted_iota(jnp.int32, (UNITS, UNITS), 0)
    column = lax.broadcasted_iota(jnp.int32, (UNITS, UNITS), 1)
    before = jnp.where(row < column, 1.0, 0.0).astype(BF16)
    base = 128.0 * dot(large.astype(BF16), before, ((1,), (0,)))
    base += dot((total - 128.0 * large).astype(BF16), before, ((1,), (0,)))
    base_out[...] = base.astype(jnp.int32)
    place = jnp.where(mask > 0.0, count - 1.0 + base[0:1, :], -1.0)
    place_out[...] = place.astype(jnp.int32)
    across_out[...] = place.T.astype(jnp.int32)


def order_of(note, width, picks, experts):
    tokens = note.shape[0]
    return pl.pallas_call(
        functools.partial(order_kernel, width, picks, experts),
        out_shape=[
            jax.ShapeDtypeStruct((tokens, UNITS), jnp.int32),
            jax.ShapeDtypeStruct((UNITS, tokens), jnp.int32),
            jax.ShapeDtypeStruct((tokens, UNITS), BF16),
            jax.ShapeDtypeStruct((8, UNITS), jnp.int32),
        ],
        compiler_params=params(),
        cost_estimate=cost(2 * tokens * tokens * UNITS, 4 * tokens * tokens),
        name="order",
    )(note)


def spans_of(base, rows):
    low = jnp.arange(rows // TILE, dtype=jnp.int32)[:, None] * TILE
    return (
        jnp.sum((base[None, 1:] <= low).astype(jnp.int32), axis=1),
        jnp.sum((base[None, :-1] < low + TILE).astype(jnp.int32), axis=1),
    )


def mine_of(base, e, row0):
    row = row0 + lax.broadcasted_iota(jnp.int32, (TILE, 1), 0)
    return (row >= base[e]) & (row < base[e + 1])


def sort_kernel(experts, low, high, base, across_ref, gates_ref, *refs):
    slices, (out, scale_out, onehot_ref, name_ref) = refs[:-4], refs[-4:]
    tokens = onehot_ref.shape[1]
    number = lax.broadcasted_iota(jnp.int32, (TILE, 128), 0).astype(F32).astype(BF16)
    onehot_ref[...] = jnp.zeros_like(onehot_ref)

    @pl.loop(0, BLOCK // TILE)
    def _(part):
        i = pl.program_id(0) * (BLOCK // TILE) + part
        row0 = i * TILE
        here = pl.ds(pl.multiple_of(part * TILE, TILE), TILE)

        @pl.loop(low[i], high[i])
        def _(e):
            away = across_ref[e] - row0
            away = jnp.where((away >= 0) & (away < TILE), away, -1).astype(F32)
            for c in range(tokens // 128):
                at = slice(c * 128, (c + 1) * 128)
                hit = number == away[c : c + 1, :].astype(BF16)
                onehot_ref[here, at] = jnp.where(hit, jnp.ones((), BF16), onehot_ref[here, at])
            name_ref[here, :] = jnp.where(mine_of(base, e, row0), e, name_ref[here, :])

    onehot = onehot_ref[...]
    for k, ref in enumerate(slices):
        out[:, k * LANES : (k + 1) * LANES] = dot(onehot, ref[...], ((1,), (0,))).astype(BF16)
    gates = dot(onehot, gates_ref[...], ((1,), (0,)))
    lane = lax.broadcasted_iota(jnp.int32, (BLOCK, UNITS), 1)
    name = name_ref[...]
    kept = (lane == name) | (lane == name + experts) | (lane == name + 2 * experts)
    scale = jnp.sum(jnp.where(kept, gates, 0.0), axis=1, keepdims=True)
    scale_out[...] = jnp.broadcast_to(scale, lane.shape)


def sort_rows(spans, base, across, gates, slices, rows, experts):
    tokens = gates.shape[0]
    across = across[:experts].reshape(experts, tokens // 128, 128)
    whole = lambda i, *_: (0, 0)
    width = len(slices) * LANES
    return pl.pallas_call(
        functools.partial(sort_kernel, experts),
        grid_spec=pltpu.PrefetchScalarGridSpec(
            num_scalar_prefetch=3,
            grid=(rows // BLOCK,),
            in_specs=[
                pl.BlockSpec(across.shape, lambda i, *_: (0, 0, 0)),
                pl.BlockSpec((tokens, UNITS), whole),
            ]
            + [pl.BlockSpec((tokens, LANES), whole)] * len(slices),
            out_specs=[
                pl.BlockSpec((BLOCK, width), lambda i, *_: (i, 0)),
                pl.BlockSpec((BLOCK, UNITS), lambda i, *_: (i, 0)),
                pl.BlockSpec((BLOCK, tokens), lambda i, *_: (i, 0)),
            ],
            scratch_shapes=[pltpu.VMEM((BLOCK, UNITS), jnp.int32)],
        ),
        out_shape=[
            jax.ShapeDtypeStruct((rows, width), BF16),
            jax.ShapeDtypeStruct((rows, UNITS), F32),
            jax.ShapeDtypeStruct((rows, tokens), BF16),
        ],
        compiler_params=params(),
        cost_estimate=cost(2 * rows * tokens * width, 8 * rows * width),
        name="sort_rows",
    )(*spans, base, across, gates, *slices)


def sort_more_kernel(onehot_ref, *refs):
    for k, ref in enumerate(refs[:-1]):
        at = slice(k * LANES, (k + 1) * LANES)
        refs[-1][:, at] = dot(onehot_ref[...], ref[...], ((1,), (0,))).astype(BF16)


def sort_more(onehot, slices):
    rows, tokens = onehot.shape
    width = len(slices) * LANES
    return pl.pallas_call(
        sort_more_kernel,
        grid=(rows // BLOCK,),
        in_specs=[pl.BlockSpec((BLOCK, tokens), lambda i: (i, 0))]
        + [pl.BlockSpec((tokens, LANES), lambda i: (0, 0))] * len(slices),
        out_specs=pl.BlockSpec((BLOCK, width), lambda i: (i, 0)),
        out_shape=jax.ShapeDtypeStruct((rows, width), BF16),
        compiler_params=params(),
        cost_estimate=cost(2 * rows * tokens * width, 8 * rows * width),
        name="sort_more",
    )(onehot, *slices)


def scatter_kernel(low, high, place_ref, onehot_ref):
    tokens = place_ref.shape[1]
    lane = lax.broadcasted_iota(jnp.int32, (tokens, 128), 1)
    onehot_ref[...] = jnp.zeros_like(onehot_ref)
    for part in range(BLOCK // TILE):
        i = pl.program_id(0) * (BLOCK // TILE) + part

        @pl.loop(low[i], high[i])
        def _(e):
            place = place_ref[e] - i * TILE
            for c in range(TILE // 128):
                at = slice(part * TILE + c * 128, part * TILE + (c + 1) * 128)
                onehot_ref[:, at] += jnp.where(place == lane + c * 128, 1.0, 0.0).astype(BF16)


def scatter_rows(spans, place, rows):
    tokens = place.shape[1]
    return pl.pallas_call(
        scatter_kernel,
        grid_spec=pltpu.PrefetchScalarGridSpec(
            num_scalar_prefetch=2,
            grid=(rows // BLOCK,),
            in_specs=[pl.BlockSpec(place.shape, lambda i, *_: (0, 0, 0))],
            out_specs=pl.BlockSpec((tokens, BLOCK), lambda i, *_: (0, i)),
        ),
        out_shape=jax.ShapeDtypeStruct((tokens, rows), BF16),
        compiler_params=params(),
        cost_estimate=cost(rows * tokens, 2 * rows * tokens),
        name="scatter_rows",
    )(*spans, place)


def partial_kernel(low, high, base, quarter, near_ref, far_ref, *refs):
    pairs, out = [refs[j : j + 2] for j in range(0, 8, 2)], refs[-1]
    width = pairs[0][0].shape[1]

    @pl.loop(0, BLOCK // TILE)
    def _(part):
        i = pl.program_id(0) * (BLOCK // TILE) + part
        here = pl.ds(pl.multiple_of(part * TILE, TILE), TILE)

        def add(e, kept):
            total = 0.0
            for k, pair in enumerate(pairs):
                weight = jnp.concatenate([pair[0][e], pair[1][e]], axis=1)
                rows_ref, at = (near_ref, far_ref)[k // 2], k % 2 * LANES
                rows = rows_ref[here, at : at + width]
                total += dot(rows, weight, ((1,), (0,)))
            return jnp.where(mine_of(base, e, i * TILE), total, kept)

        out[here, :] = lax.fori_loop(
            low[i], high[i], add, jnp.zeros((TILE, out.shape[1]), F32)
        ).astype(BF16)


def partial_sums(f, spans, base, quarter, near, far, w_gate, w_up, pieces):
    rows = near.shape[0]
    experts, width, _ = w_gate.shape
    own = pl.BlockSpec((experts, width, UNITS), lambda i, lo, hi, b, q: (0, 0, 2 * q[0] + f))
    block = pl.BlockSpec((experts, width, UNITS), lambda i, *_: (0, 0, 0))
    return pl.pallas_call(
        partial_kernel,
        grid_spec=pltpu.PrefetchScalarGridSpec(
            num_scalar_prefetch=4,
            grid=(rows // BLOCK,),
            in_specs=[pl.BlockSpec((BLOCK, 2 * LANES), lambda i, *_: (i, 0))] * 2 + [own] * 2
            + [block] * len(pieces),
            out_specs=pl.BlockSpec((BLOCK, 2 * UNITS), lambda i, *_: (i, 0)),
        ),
        out_shape=jax.ShapeDtypeStruct((rows, 2 * UNITS), BF16),
        compiler_params=params(),
        cost_estimate=cost(16 * rows * LANES * UNITS, 8 * rows * LANES),
        name="partial_sums",
    )(*spans, base, quarter, near, far, w_gate, w_up, *pieces)


def down_kernel(half, low, high, base, onehot_ref, hidden, start, *refs):
    weights, (out, total_ref, value_ref) = refs[:-3], refs[-3:]
    width = weights[0].shape[2]
    j = pl.program_id(0)

    @pl.when(j == 0)
    def _():
        total_ref[...] = jnp.zeros_like(total_ref) if start is None else start[...]
        value_ref[...] = jnp.zeros_like(value_ref)

    for part in range(BLOCK // TILE):
        i = (2 * j + half) * (BLOCK // TILE) + part
        here = slice(part * TILE, (part + 1) * TILE)
        units = hidden[here, :]

        @pl.loop(low[i], high[i])
        def _(e):
            mine = mine_of(base, e, i * TILE)
            for k, weight in enumerate(weights):
                value = dot(units, weight[e], ((1,), (0,)))
                at = slice(k * LANES, k * LANES + width)
                value_ref[here, at] = jnp.where(
                    mine, value, value_ref[here, at].astype(F32)
                ).astype(BF16)

    total_ref[...] += dot(onehot_ref[...], value_ref[...], ((1,), (0,)))

    @pl.when(j == pl.num_programs(0) - 1)
    def _():
        out[...] = total_ref[...].astype(out.dtype)


def down_and_mix(half, spans, base, onehot, hidden, start, weights, dtype):
    rows, units = hidden.shape
    count, tokens = len(weights), onehot.shape[0]
    block = pl.BlockSpec((BLOCK, units), lambda j, *_: (j, 0))
    whole = pl.BlockSpec((tokens, count * LANES), lambda j, *_: (0, 0))
    kernel = functools.partial(down_kernel, half)
    if start is None:
        kernel = lambda *refs: down_kernel(half, *refs[:5], None, *refs[5:])
    return pl.pallas_call(
        kernel,
        grid_spec=pltpu.PrefetchScalarGridSpec(
            num_scalar_prefetch=3,
            grid=(rows // BLOCK,),
            in_specs=[pl.BlockSpec((tokens, BLOCK), lambda j, *_: (0, 2 * j + half)), block]
            + ([] if start is None else [whole])
            + [pl.BlockSpec(w.shape, lambda j, *_: (0, 0, 0)) for w in weights],
            out_specs=whole,
            scratch_shapes=[
                pltpu.VMEM((tokens, count * LANES), F32),
                pltpu.VMEM((BLOCK, count * LANES), BF16),
            ],
        ),
        out_shape=jax.ShapeDtypeStruct((tokens, count * LANES), dtype),
        compiler_params=params(56),
        cost_estimate=cost(2 * rows * tokens * LANES * count, 2 * rows * tokens),
        name="down_and_mix",
    )(*spans, base, onehot, hidden, *([] if start is None else [start]), *weights)


def fixed_weights(size, tokens, expert_ids, gate_weights, w_gate, w_up, w_down):
    count, picks = expert_ids.shape
    experts, width, hidden_units = w_gate.shape
    quarter = hidden_units // 4
    rows = size * count * picks
    places = size // 4
    me, plane = lax.axis_index("ep"), lax.axis_index("parts")
    w_down = jnp.swapaxes(w_down, 1, 2)

    twins = [(i, i ^ 1) for i in range(size)]
    cross = [(p * size + i, p * size + (i ^ 2 ^ p)) for p in range(2) for i in range(size)]
    to_twin = lambda value: lax.ppermute(value, "ep", twins)
    other = [(p * size + i, p * size + (i ^ 3 ^ p)) for p in range(2) for i in range(size)]
    to_cross = lambda value: lax.ppermute(value, ("parts", "ep"), cross)
    to_other = lambda value: lax.ppermute(value, ("parts", "ep"), other)
    to_plane = lambda value: lax.ppermute(value, "parts", [(0, 1), (1, 0)])
    line = [[4 * p + k for p in range(places)] for k in range(4)]
    my_quarter = me % 4
    twin_quarter = my_quarter ^ 1
    cross_quarter = my_quarter ^ 2 ^ plane
    other_quarter = cross_quarter ^ 1

    note = jnp.concatenate([expert_ids.astype(F32), *split3(gate_weights)], axis=1).astype(BF16)
    fill = LANES - width - note.shape[1]
    parcels = jnp.concatenate(
        [
            tokens.reshape(count, size, width).swapaxes(0, 1),
            jnp.broadcast_to(jnp.pad(note, ((0, 0), (0, fill)))[None], (size, count, LANES - width)),
        ],
        axis=2,
    )
    own = lax.all_to_all(parcels, "ep", split_axis=0, concat_axis=0, tiled=True)
    own = own.reshape(size * count, LANES)
    far, near = to_cross(own), [own, to_twin(own)]
    place, across, gates, base = order_of(own, width, picks, experts)
    base = base[0, : experts + 1]
    spans = spans_of(base, rows)
    which = my_quarter.astype(jnp.int32).reshape(1)

    def cut(w, q, f):
        return lax.dynamic_slice_in_dim(w, q * quarter + f * UNITS, UNITS, 2)

    def after(value, *others):
        return lax.optimization_barrier((value, *others))[0]

    near_rows, scale, onehot = sort_rows(spans, base, across, gates, near, rows, experts)
    far = after(far, near_rows)
    far_rows = sort_more(onehot, [far, to_twin(far)])
    scale = lax.dynamic_slice_in_dim(scale, (me // 4) * (rows // places), rows // places, 0)

    held, crossed = [], []
    for n, (f, w) in enumerate(
        ((0, w_gate), (0, w_up), (1, w_gate), (1, w_up), (0, w_down), (1, w_down))
    ):
        piece = cut(w, cross_quarter, f)
        if n > 1:
            piece = after(piece, far_rows, crossed[n - 1], *[pieces[2] for pieces in held[:2]])
        crossed.append(to_cross(piece))
        beside = to_plane(crossed[n]) if n > 1 else to_other(cut(w, other_quarter, f))
        held.append((to_twin(cut(w, twin_quarter, f)), crossed[n], beside))
    weave = lambda pair: [piece for both in zip(*pair) for piece in both]

    units = []
    for f in range(2):
        pieces = weave(held[2 * f : 2 * f + 2])
        later = partial_sums(f, spans, base, which, near_rows, far_rows, w_gate, w_up, pieces)
        sums = lax.psum_scatter(
            later, "ep", scatter_dimension=0, axis_index_groups=line, tiled=True
        ).astype(F32)
        units.append((jax.nn.silu(sums[:, :UNITS]) * sums[:, UNITS:] * scale).astype(BF16))

    place = jnp.broadcast_to(
        after(across[:experts], later)[:, :, None], (experts, size * count, 128)
    )
    columns = scatter_rows(spans, place, rows)
    turned = weave(held[4:])
    turned = [
        jnp.concatenate([jnp.swapaxes(piece, 1, 2) for piece in turned[k : k + 2]], axis=1)
        for k in (0, 2, 4)
    ]
    turned = [
        jnp.swapaxes(lax.dynamic_slice_in_dim(w_down, my_quarter * quarter, quarter, 2), 1, 2)
    ] + turned
    turned = after(turned, later)
    units, columns, turned = lax.optimization_barrier((units, columns, turned))
    units = jnp.concatenate(units, axis=1).reshape(-1, BLOCK, 2 * UNITS)
    first, second = (
        lax.all_gather(units[half], "ep", axis=0, axis_index_groups=line, tiled=True)
        for half in range(2)
    )
    far_mix = lambda half, hidden, start, dtype: down_and_mix(
        half, spans, base, columns, hidden, start, turned[2:], dtype
    )
    near_mix = lambda half, hidden, start, dtype: down_and_mix(
        half, spans, base, columns, hidden, start, turned[:2], dtype
    )
    far, near = far_mix(0, first, None, F32), near_mix(0, first, None, F32)
    second, far, near = lax.optimization_barrier((second, far, near))
    far = far_mix(1, second, far, BF16)
    far, far_twin = far[:, :width], far[:, LANES : LANES + width]
    far = (far.astype(F32) + to_twin(far_twin).astype(F32)).astype(BF16)
    near, far = lax.optimization_barrier((near, far))
    far = to_cross(far)
    near = near_mix(1, second, near, F32)
    twin = near[:, LANES : LANES + width].astype(BF16)
    twin = to_twin(after(twin, far)).astype(F32)
    mixed = (near[:, :width] + twin + far.astype(F32)).astype(BF16)
    mixed = lax.all_to_all(
        mixed.reshape(size, count, width), "ep", split_axis=0, concat_axis=0, tiled=True
    )
    return mixed.swapaxes(0, 1).reshape(count, size * width)


def solution(mesh):
    size, inner = mesh.shape["ep"], mesh.shape["tp"]

    def body(tokens, expert_ids, gate_weights, w_gate, w_up, w_down):
        rows = size * math.prod(expert_ids.shape)
        sums = rows * w_gate.shape[2]
        experts, width, units = w_gate.shape
        even = (
            size % 4 == 0
            and size > 4
            and mesh.shape["parts"] == 2
            and rows == size // 4 * 2 * BLOCK
            and units == 8 * UNITS
            and 3 * experts <= UNITS
            and size * math.prod(expert_ids.shape[:1]) % 128 == 0
            and width + 4 * expert_ids.shape[1] <= LANES
        )
        args = (tokens, expert_ids, gate_weights, w_gate, w_up, w_down)
        if inner == 1 and even and sums <= 3 * math.prod(w_gate.shape):
            return fixed_weights(size, *args)
        return moved_weights(*args)

    placed = (
        P(("parts", "ep"), "tp"),
        P(("parts", "ep"), None),
        P(("parts", "ep"), None),
        P(None, "ep", "tp"),
        P(None, "ep", "tp"),
        P(None, "tp", "ep"),
    )
    return jax.shard_map(
        body, mesh=mesh, in_specs=placed, out_specs=P(("parts", "ep"), "tp"), check_vma=False
    )
```

```python
import functools
import math

import jax
import jax.numpy as jnp
from jax import lax
from jax.experimental import pallas as pl
from jax.experimental.pallas import tpu as pltpu
from jax.sharding import PartitionSpec as P

BF16 = jnp.bfloat16
F32 = jnp.float32
TILE = 256
BLOCK = 1024
LANES = 256
UNITS = 128


def slots_of(block_ids, experts):
    flat = block_ids.reshape(-1)
    onehot = (flat[:, None] == jnp.arange(experts, dtype=jnp.int32)[None, :]).astype(jnp.int32)
    before = jnp.cumsum(onehot, axis=0) - onehot
    return jnp.sum(before * onehot, axis=1).reshape(block_ids.shape)


def fill_slots(rows, expert_ids, slot, experts, per_expert):
    count, picks = expert_ids.shape
    spread = jnp.broadcast_to(rows[:, None, :], (count, picks, rows.shape[1]))
    empty = jnp.zeros((experts, per_expert, rows.shape[1]), BF16)
    return empty.at[expert_ids, slot].set(spread)


def moved_weights(tokens, expert_ids, gate_weights, w_gate, w_up, w_down):
    tok_rows, picks = expert_ids.shape
    experts = w_gate.shape[0]
    per_expert = min(tok_rows, 3 * tok_rows * picks // (2 * experts))
    slot = slots_of(expert_ids, experts)
    features = lax.all_gather(tokens, "tp", axis=1, tiled=True)
    outgoing = fill_slots(features, expert_ids, slot, experts, per_expert)
    arrived = lax.all_to_all(outgoing, "ep", split_axis=0, concat_axis=1, tiled=True)
    gate_owned, up_owned = (
        lax.all_to_all(w_gate, "ep", split_axis=0, concat_axis=1, tiled=True),
        lax.all_to_all(w_up, "ep", split_axis=0, concat_axis=1, tiled=True),
    )
    gate = jnp.einsum("ecd,edf->ecf", arrived, gate_owned, preferred_element_type=F32)
    up = jnp.einsum("ecd,edf->ecf", arrived, up_owned, preferred_element_type=F32)
    hidden = (jax.nn.silu(gate) * up).astype(BF16)
    down_owned = lax.all_to_all(w_down, "ep", split_axis=0, concat_axis=2, tiled=True)
    partial_value = jnp.einsum("ecf,efd->ecd", hidden, down_owned, preferred_element_type=F32)
    expert_out = lax.psum_scatter(
        partial_value.astype(BF16), "tp", scatter_dimension=2, tiled=True
    )
    returned = lax.all_to_all(expert_out, "ep", split_axis=1, concat_axis=0, tiled=True)
    picked = returned[expert_ids, slot]
    mixed = jnp.sum(gate_weights[:, :, None] * picked.astype(F32), axis=1)
    return mixed.astype(BF16)


def dot(a, b, contract):
    return lax.dot_general(a, b, ((contract[0], contract[1]), ((), ())), preferred_element_type=F32)


def params(mib=48):
    return pltpu.CompilerParams(vmem_limit_bytes=mib << 20)


def cost(flops, moved):
    return pl.CostEstimate(flops=flops, bytes_accessed=moved, transcendentals=0)


def split3(value):
    high = lax.reduce_precision(value, 8, 7)
    middle = lax.reduce_precision(value - high, 8, 7)
    return high, middle, lax.reduce_precision(value - high - middle, 8, 7)


def order_kernel(width, picks, experts, note_ref, place_out, across_out, gates_out, base_out):
    tokens = note_ref.shape[0]
    note = note_ref[...].astype(F32)
    lane = lax.broadcasted_iota(jnp.int32, (tokens, UNITS), 1)
    name = jnp.where(lane < 3 * experts, lane % experts, -1).astype(F32)
    gates = jnp.zeros((tokens, UNITS), F32)
    for k in range(picks):
        one = note[:, width + k : width + k + 1]
        weight = (
            note[:, width + picks + k : width + picks + k + 1]
            + note[:, width + 2 * picks + k : width + 2 * picks + k + 1]
            + note[:, width + 3 * picks + k : width + 3 * picks + k + 1]
        )
        gates = jnp.where(name == one, weight, gates)
    mask = jnp.where((gates != 0.0) & (lane < experts), 1.0, 0.0)
    high = gates.astype(BF16)
    middle = (gates - high.astype(F32)).astype(BF16)
    rest = (gates - high.astype(F32) - middle.astype(F32)).astype(BF16)
    gates_out[...] = jnp.where(
        lane < experts,
        high.astype(F32),
        jnp.where(lane < 2 * experts, middle.astype(F32), rest.astype(F32)),
    ).astype(BF16)
    row = lax.broadcasted_iota(jnp.int32, (tokens, tokens), 0)
    column = lax.broadcasted_iota(jnp.int32, (tokens, tokens), 1)
    upto = jnp.where(column <= row, 1.0, 0.0).astype(BF16)
    count = dot(upto, mask.astype(BF16), ((1,), (0,)))
    total = jnp.broadcast_to(count[tokens - 1 : tokens, :], (8, UNITS))
    large = jnp.floor(total * (1.0 / 128.0))
    row = lax.broadcasted_iota(jnp.int32, (UNITS, UNITS), 0)
    column = lax.broadcasted_iota(jnp.int32, (UNITS, UNITS), 1)
    before = jnp.where(row < column, 1.0, 0.0).astype(BF16)
    base = 128.0 * dot(large.astype(BF16), before, ((1,), (0,)))
    base += dot((total - 128.0 * large).astype(BF16), before, ((1,), (0,)))
    base_out[...] = base.astype(jnp.int32)
    place = jnp.where(mask > 0.0, count - 1.0 + base[0:1, :], -1.0)
    place_out[...] = place.astype(jnp.int32)
    across_out[...] = place.T.astype(jnp.int32)


def order_of(note, width, picks, experts):
    tokens = note.shape[0]
    return pl.pallas_call(
        functools.partial(order_kernel, width, picks, experts),
        out_shape=[
            jax.ShapeDtypeStruct((tokens, UNITS), jnp.int32),
            jax.ShapeDtypeStruct((UNITS, tokens), jnp.int32),
            jax.ShapeDtypeStruct((tokens, UNITS), BF16),
            jax.ShapeDtypeStruct((8, UNITS), jnp.int32),
        ],
        compiler_params=params(),
        cost_estimate=cost(2 * tokens * tokens * UNITS, 4 * tokens * tokens),
        name="order",
    )(note)


def spans_of(base, rows):
    low = jnp.arange(rows // TILE, dtype=jnp.int32)[:, None] * TILE
    return (
        jnp.sum((base[None, 1:] <= low).astype(jnp.int32), axis=1),
        jnp.sum((base[None, :-1] < low + TILE).astype(jnp.int32), axis=1),
    )


def mine_of(base, e, row0):
    row = row0 + lax.broadcasted_iota(jnp.int32, (TILE, 1), 0)
    return (row >= base[e]) & (row < base[e + 1])


def sort_kernel(experts, low, high, base, across_ref, gates_ref, *refs):
    slices, (out, scale_out, onehot_ref, name_ref) = refs[:-4], refs[-4:]
    tokens = onehot_ref.shape[1]
    number = lax.broadcasted_iota(jnp.int32, (TILE, 128), 0).astype(F32).astype(BF16)
    onehot_ref[...] = jnp.zeros_like(onehot_ref)

    @pl.loop(0, BLOCK // TILE)
    def _(part):
        i = pl.program_id(0) * (BLOCK // TILE) + part
        row0 = i * TILE
        here = pl.ds(pl.multiple_of(part * TILE, TILE), TILE)

        @pl.loop(low[i], high[i])
        def _(e):
            away = across_ref[e] - row0
            away = jnp.where((away >= 0) & (away < TILE), away, -1).astype(F32)
            for c in range(tokens // 128):
                at = slice(c * 128, (c + 1) * 128)
                hit = number == away[c : c + 1, :].astype(BF16)
                onehot_ref[here, at] = jnp.where(hit, jnp.ones((), BF16), onehot_ref[here, at])
            name_ref[here, :] = jnp.where(mine_of(base, e, row0), e, name_ref[here, :])

    onehot = onehot_ref[...]
    for k, ref in enumerate(slices):
        out[:, k * LANES : (k + 1) * LANES] = dot(onehot, ref[...], ((1,), (0,))).astype(BF16)
    gates = dot(onehot, gates_ref[...], ((1,), (0,)))
    lane = lax.broadcasted_iota(jnp.int32, (BLOCK, UNITS), 1)
    name = name_ref[...]
    kept = (lane == name) | (lane == name + experts) | (lane == name + 2 * experts)
    scale = jnp.sum(jnp.where(kept, gates, 0.0), axis=1, keepdims=True)
    scale_out[...] = jnp.broadcast_to(scale, lane.shape)


def sort_rows(spans, base, across, gates, slices, rows, experts):
    tokens = gates.shape[0]
    across = across[:experts].reshape(experts, tokens // 128, 128)
    whole = lambda i, *_: (0, 0)
    width = len(slices) * LANES
    return pl.pallas_call(
        functools.partial(sort_kernel, experts),
        grid_spec=pltpu.PrefetchScalarGridSpec(
            num_scalar_prefetch=3,
            grid=(rows // BLOCK,),
            in_specs=[
                pl.BlockSpec(across.shape, lambda i, *_: (0, 0, 0)),
                pl.BlockSpec((tokens, UNITS), whole),
            ]
            + [pl.BlockSpec((tokens, LANES), whole)] * len(slices),
            out_specs=[
                pl.BlockSpec((BLOCK, width), lambda i, *_: (i, 0)),
                pl.BlockSpec((BLOCK, UNITS), lambda i, *_: (i, 0)),
                pl.BlockSpec((BLOCK, tokens), lambda i, *_: (i, 0)),
            ],
            scratch_shapes=[pltpu.VMEM((BLOCK, UNITS), jnp.int32)],
        ),
        out_shape=[
            jax.ShapeDtypeStruct((rows, width), BF16),
            jax.ShapeDtypeStruct((rows, UNITS), F32),
            jax.ShapeDtypeStruct((rows, tokens), BF16),
        ],
        compiler_params=params(),
        cost_estimate=cost(2 * rows * tokens * width, 8 * rows * width),
        name="sort_rows",
    )(*spans, base, across, gates, *slices)


def sort_more_kernel(onehot_ref, *refs):
    for k, ref in enumerate(refs[:-1]):
        at = slice(k * LANES, (k + 1) * LANES)
        refs[-1][:, at] = dot(onehot_ref[...], ref[...], ((1,), (0,))).astype(BF16)


def sort_more(onehot, slices):
    rows, tokens = onehot.shape
    width = len(slices) * LANES
    return pl.pallas_call(
        sort_more_kernel,
        grid=(rows // BLOCK,),
        in_specs=[pl.BlockSpec((BLOCK, tokens), lambda i: (i, 0))]
        + [pl.BlockSpec((tokens, LANES), lambda i: (0, 0))] * len(slices),
        out_specs=pl.BlockSpec((BLOCK, width), lambda i: (i, 0)),
        out_shape=jax.ShapeDtypeStruct((rows, width), BF16),
        compiler_params=params(),
        cost_estimate=cost(2 * rows * tokens * width, 8 * rows * width),
        name="sort_more",
    )(onehot, *slices)


def scatter_kernel(low, high, place_ref, onehot_ref):
    tokens = place_ref.shape[1]
    lane = lax.broadcasted_iota(jnp.int32, (tokens, 128), 1)
    onehot_ref[...] = jnp.zeros_like(onehot_ref)
    for part in range(BLOCK // TILE):
        i = pl.program_id(0) * (BLOCK // TILE) + part

        @pl.loop(low[i], high[i])
        def _(e):
            place = place_ref[e] - i * TILE
            for c in range(TILE // 128):
                at = slice(part * TILE + c * 128, part * TILE + (c + 1) * 128)
                onehot_ref[:, at] += jnp.where(place == lane + c * 128, 1.0, 0.0).astype(BF16)


def scatter_rows(spans, place, rows):
    tokens = place.shape[1]
    return pl.pallas_call(
        scatter_kernel,
        grid_spec=pltpu.PrefetchScalarGridSpec(
            num_scalar_prefetch=2,
            grid=(rows // BLOCK,),
            in_specs=[pl.BlockSpec(place.shape, lambda i, *_: (0, 0, 0))],
            out_specs=pl.BlockSpec((tokens, BLOCK), lambda i, *_: (0, i)),
        ),
        out_shape=jax.ShapeDtypeStruct((tokens, rows), BF16),
        compiler_params=params(),
        cost_estimate=cost(rows * tokens, 2 * rows * tokens),
        name="scatter_rows",
    )(*spans, place)


def partial_kernel(low, high, base, quarter, near_ref, far_ref, *refs):
    own, stacked, out = refs[:2], refs[2:-1], refs[-1]
    experts, width, _ = own[0].shape

    @pl.loop(0, BLOCK // TILE)
    def _(part):
        i = pl.program_id(0) * (BLOCK // TILE) + part
        here = pl.ds(pl.multiple_of(part * TILE, TILE), TILE)

        def add(e, kept):
            total = 0.0
            for k in range(4):
                pair = stacked[k - 1] if k else own
                pair = [pair[e], pair[experts + e]] if k else [pair[0][e], pair[1][e]]
                weight = jnp.concatenate(pair, axis=1)
                rows_ref, at = (near_ref, far_ref)[k // 2], k % 2 * LANES
                rows = rows_ref[here, at : at + width]
                total += dot(rows, weight, ((1,), (0,)))
            return jnp.where(mine_of(base, e, i * TILE), total, kept)

        out[here, :] = lax.fori_loop(
            low[i], high[i], add, jnp.zeros((TILE, out.shape[1]), F32)
        ).astype(BF16)


def partial_sums(f, spans, base, quarter, near, far, w_gate, w_up, pieces):
    rows = near.shape[0]
    experts, width, _ = w_gate.shape
    own = pl.BlockSpec((experts, width, UNITS), lambda i, lo, hi, b, q: (0, 0, 2 * q[0] + f))
    block = pl.BlockSpec((2 * experts, width, UNITS), lambda i, *_: (0, 0, 0))
    return pl.pallas_call(
        partial_kernel,
        grid_spec=pltpu.PrefetchScalarGridSpec(
            num_scalar_prefetch=4,
            grid=(rows // BLOCK,),
            in_specs=[pl.BlockSpec((BLOCK, 2 * LANES), lambda i, *_: (i, 0))] * 2 + [own] * 2
            + [block] * len(pieces),
            out_specs=pl.BlockSpec((BLOCK, 2 * UNITS), lambda i, *_: (i, 0)),
        ),
        out_shape=jax.ShapeDtypeStruct((rows, 2 * UNITS), BF16),
        compiler_params=params(),
        cost_estimate=cost(16 * rows * LANES * UNITS, 8 * rows * LANES),
        name="partial_sums",
    )(*spans, base, quarter, near, far, w_gate, w_up, *pieces)


def down_kernel(half, low, high, base, onehot_ref, hidden, start, *refs):
    weights, (out, total_ref, value_ref) = refs[:-3], refs[-3:]
    width = weights[0].shape[1]
    j = pl.program_id(0)

    @pl.when(j == 0)
    def _():
        total_ref[...] = jnp.zeros_like(total_ref) if start is None else start[...]
        value_ref[...] = jnp.zeros_like(value_ref)

    for part in range(BLOCK // TILE):
        i = (2 * j + half) * (BLOCK // TILE) + part
        here = slice(part * TILE, (part + 1) * TILE)
        units = hidden[here, :]

        @pl.loop(low[i], high[i])
        def _(e):
            mine = mine_of(base, e, i * TILE)
            for k, weight in enumerate(weights):
                value = dot(units, weight[e], ((1,), (1,)))
                at = slice(k * LANES, k * LANES + width)
                value_ref[here, at] = jnp.where(
                    mine, value, value_ref[here, at].astype(F32)
                ).astype(BF16)

    total_ref[...] += dot(onehot_ref[...], value_ref[...], ((1,), (0,)))

    @pl.when(j == pl.num_programs(0) - 1)
    def _():
        out[...] = total_ref[...].astype(out.dtype)


def down_and_mix(half, spans, base, onehot, hidden, start, weights, dtype):
    rows, units = hidden.shape
    count, tokens = len(weights), onehot.shape[0]
    block = pl.BlockSpec((BLOCK, units), lambda j, *_: (j, 0))
    whole = pl.BlockSpec((tokens, count * LANES), lambda j, *_: (0, 0))
    kernel = functools.partial(down_kernel, half)
    if start is None:
        kernel = lambda *refs: down_kernel(half, *refs[:5], None, *refs[5:])
    return pl.pallas_call(
        kernel,
        grid_spec=pltpu.PrefetchScalarGridSpec(
            num_scalar_prefetch=3,
            grid=(rows // BLOCK,),
            in_specs=[pl.BlockSpec((tokens, BLOCK), lambda j, *_: (0, 2 * j + half)), block]
            + ([] if start is None else [whole])
            + [pl.BlockSpec(w.shape, lambda j, *_: (0, 0, 0)) for w in weights],
            out_specs=whole,
            scratch_shapes=[
                pltpu.VMEM((tokens, count * LANES), F32),
                pltpu.VMEM((BLOCK, count * LANES), BF16),
            ],
        ),
        out_shape=jax.ShapeDtypeStruct((tokens, count * LANES), dtype),
        compiler_params=params(56),
        cost_estimate=cost(2 * rows * tokens * LANES * count, 2 * rows * tokens),
        name="down_and_mix",
    )(*spans, base, onehot, hidden, *([] if start is None else [start]), *weights)


def fixed_weights(size, tokens, expert_ids, gate_weights, w_gate, w_up, w_down):
    count, picks = expert_ids.shape
    experts, width, hidden_units = w_gate.shape
    quarter = hidden_units // 4
    rows = size * count * picks
    places = size // 4
    me, plane = lax.axis_index("ep"), lax.axis_index("parts")
    w_down = jnp.swapaxes(w_down, 1, 2)

    twins = [(i, i ^ 1) for i in range(size)]
    cross = [(p * size + i, p * size + (i ^ 2 ^ p)) for p in range(2) for i in range(size)]
    to_twin = lambda value: lax.ppermute(value, "ep", twins)
    other = [(p * size + i, p * size + (i ^ 3 ^ p)) for p in range(2) for i in range(size)]
    to_cross = lambda value: lax.ppermute(value, ("parts", "ep"), cross)
    to_other = lambda value: lax.ppermute(value, ("parts", "ep"), other)
    to_plane = lambda value: lax.ppermute(value, "parts", [(0, 1), (1, 0)])
    line = [[4 * p + k for p in range(places)] for k in range(4)]
    my_quarter = me % 4
    twin_quarter = my_quarter ^ 1
    cross_quarter = my_quarter ^ 2 ^ plane
    other_quarter = cross_quarter ^ 1

    note = jnp.concatenate([expert_ids.astype(F32), *split3(gate_weights)], axis=1).astype(BF16)
    fill = LANES - width - note.shape[1]
    parcels = jnp.concatenate(
        [
            tokens.reshape(count, size, width).swapaxes(0, 1),
            jnp.broadcast_to(jnp.pad(note, ((0, 0), (0, fill)))[None], (size, count, LANES - width)),
        ],
        axis=2,
    )
    own = lax.all_to_all(parcels, "ep", split_axis=0, concat_axis=0, tiled=True)
    own = own.reshape(size * count, LANES)
    far, near = to_cross(own), [own, to_twin(own)]
    place, across, gates, base = order_of(own, width, picks, experts)
    base = base[0, : experts + 1]
    spans = spans_of(base, rows)
    which = my_quarter.astype(jnp.int32).reshape(1)

    def cut(n, q):
        if n == 2:
            return lax.dynamic_slice_in_dim(w_down, q * quarter, quarter, 2)
        at = q * quarter + n * UNITS
        return jnp.concatenate(
            [lax.dynamic_slice_in_dim(w, at, UNITS, 2) for w in (w_gate, w_up)], axis=0
        )

    def after(value, *others):
        return lax.optimization_barrier((value, *others))[0]

    near_rows, scale, onehot = sort_rows(spans, base, across, gates, near, rows, experts)
    far = after(far, near_rows)
    far_rows = sort_more(onehot, [far, to_twin(far)])
    scale = lax.dynamic_slice_in_dim(scale, (me // 4) * (rows // places), rows // places, 0)

    held = []
    for n in range(3):
        piece = cut(n, cross_quarter)
        if n:
            piece = after(piece, far_rows, *held[-1][1:])
        across_x = to_cross(piece)
        beside = to_plane(across_x) if n else to_other(cut(n, other_quarter))
        held.append((to_twin(cut(n, twin_quarter)), across_x, beside))

    units = []
    for f in range(2):
        later = partial_sums(f, spans, base, which, near_rows, far_rows, w_gate, w_up, held[f])
        sums = lax.psum_scatter(
            later, "ep", scatter_dimension=0, axis_index_groups=line, tiled=True
        ).astype(F32)
        units.append((jax.nn.silu(sums[:, :UNITS]) * sums[:, UNITS:] * scale).astype(BF16))

    place = jnp.broadcast_to(
        after(across[:experts], later)[:, :, None], (experts, size * count, 128)
    )
    columns = scatter_rows(spans, place, rows)
    pieces = [after(cut(2, my_quarter), later), *held[2]]
    units, columns, pieces = lax.optimization_barrier((units, columns, pieces))
    units = jnp.concatenate(units, axis=1).reshape(-1, BLOCK, 2 * UNITS)
    first, second = (
        lax.all_gather(units[half], "ep", axis=0, axis_index_groups=line, tiled=True)
        for half in range(2)
    )
    far_mix = lambda half, hidden, start, dtype: down_and_mix(
        half, spans, base, columns, hidden, start, pieces[2:], dtype
    )
    near_mix = lambda half, hidden, start, dtype: down_and_mix(
        half, spans, base, columns, hidden, start, pieces[:2], dtype
    )
    far, near = far_mix(0, first, None, F32), near_mix(0, first, None, F32)
    second, far, near = lax.optimization_barrier((second, far, near))
    far = far_mix(1, second, far, BF16)
    far, far_twin = far[:, :width], far[:, LANES : LANES + width]
    far = (far.astype(F32) + to_twin(far_twin).astype(F32)).astype(BF16)
    near, far = lax.optimization_barrier((near, far))
    far = to_cross(far)
    near = near_mix(1, second, near, F32)
    twin = near[:, LANES : LANES + width].astype(BF16)
    twin = to_twin(after(twin, far)).astype(F32)
    mixed = (near[:, :width] + twin + far.astype(F32)).astype(BF16)
    mixed = lax.all_to_all(
        mixed.reshape(size, count, width), "ep", split_axis=0, concat_axis=0, tiled=True
    )
    return mixed.swapaxes(0, 1).reshape(count, size * width)


def solution(mesh):
    size, inner = mesh.shape["ep"], mesh.shape["tp"]

    def body(tokens, expert_ids, gate_weights, w_gate, w_up, w_down):
        rows = size * math.prod(expert_ids.shape)
        sums = rows * w_gate.shape[2]
        experts, width, units = w_gate.shape
        even = (
            size % 4 == 0
            and size > 4
            and mesh.shape["parts"] == 2
            and rows == size // 4 * 2 * BLOCK
            and units == 8 * UNITS
            and 3 * experts <= UNITS
            and size * math.prod(expert_ids.shape[:1]) % 128 == 0
            and width + 4 * expert_ids.shape[1] <= LANES
        )
        args = (tokens, expert_ids, gate_weights, w_gate, w_up, w_down)
        if inner == 1 and even and sums <= 3 * math.prod(w_gate.shape):
            return fixed_weights(size, *args)
        return moved_weights(*args)

    placed = (
        P(("parts", "ep"), "tp"),
        P(("parts", "ep"), None),
        P(("parts", "ep"), None),
        P(None, "ep", "tp"),
        P(None, "ep", "tp"),
        P(None, "tp", "ep"),
    )
    return jax.shard_map(
        body, mesh=mesh, in_specs=placed, out_specs=P(("parts", "ep"), "tp"), check_vma=False
    )
```

```python
import functools
import math

import jax
import jax.numpy as jnp
from jax import lax
from jax.experimental import pallas as pl
from jax.experimental.pallas import tpu as pltpu
from jax.sharding import PartitionSpec as P

BF16 = jnp.bfloat16
F32 = jnp.float32
TILE = 256
BLOCK = 1024
LANES = 256
UNITS = 128


def slots_of(block_ids, experts):
    flat = block_ids.reshape(-1)
    onehot = (flat[:, None] == jnp.arange(experts, dtype=jnp.int32)[None, :]).astype(jnp.int32)
    before = jnp.cumsum(onehot, axis=0) - onehot
    return jnp.sum(before * onehot, axis=1).reshape(block_ids.shape)


def fill_slots(rows, expert_ids, slot, experts, per_expert):
    count, picks = expert_ids.shape
    spread = jnp.broadcast_to(rows[:, None, :], (count, picks, rows.shape[1]))
    empty = jnp.zeros((experts, per_expert, rows.shape[1]), BF16)
    return empty.at[expert_ids, slot].set(spread)


def moved_weights(tokens, expert_ids, gate_weights, w_gate, w_up, w_down):
    tok_rows, picks = expert_ids.shape
    experts = w_gate.shape[0]
    per_expert = min(tok_rows, 3 * tok_rows * picks // (2 * experts))
    slot = slots_of(expert_ids, experts)
    features = lax.all_gather(tokens, "tp", axis=1, tiled=True)
    outgoing = fill_slots(features, expert_ids, slot, experts, per_expert)
    arrived = lax.all_to_all(outgoing, "ep", split_axis=0, concat_axis=1, tiled=True)
    gate_owned, up_owned = (
        lax.all_to_all(w_gate, "ep", split_axis=0, concat_axis=1, tiled=True),
        lax.all_to_all(w_up, "ep", split_axis=0, concat_axis=1, tiled=True),
    )
    gate = jnp.einsum("ecd,edf->ecf", arrived, gate_owned, preferred_element_type=F32)
    up = jnp.einsum("ecd,edf->ecf", arrived, up_owned, preferred_element_type=F32)
    hidden = (jax.nn.silu(gate) * up).astype(BF16)
    down_owned = lax.all_to_all(w_down, "ep", split_axis=0, concat_axis=2, tiled=True)
    partial_value = jnp.einsum("ecf,efd->ecd", hidden, down_owned, preferred_element_type=F32)
    expert_out = lax.psum_scatter(
        partial_value.astype(BF16), "tp", scatter_dimension=2, tiled=True
    )
    returned = lax.all_to_all(expert_out, "ep", split_axis=1, concat_axis=0, tiled=True)
    picked = returned[expert_ids, slot]
    mixed = jnp.sum(gate_weights[:, :, None] * picked.astype(F32), axis=1)
    return mixed.astype(BF16)


def dot(a, b, contract):
    return lax.dot_general(a, b, ((contract[0], contract[1]), ((), ())), preferred_element_type=F32)


def params(mib=48):
    return pltpu.CompilerParams(vmem_limit_bytes=mib << 20)


def cost(flops, moved):
    return pl.CostEstimate(flops=flops, bytes_accessed=moved, transcendentals=0)


def split3(value):
    high = lax.reduce_precision(value, 8, 7)
    middle = lax.reduce_precision(value - high, 8, 7)
    return high, middle, lax.reduce_precision(value - high - middle, 8, 7)


def order_kernel(width, picks, experts, note_ref, place_out, across_out, gates_out, base_out):
    tokens = note_ref.shape[0]
    note = note_ref[...].astype(F32)
    lane = lax.broadcasted_iota(jnp.int32, (tokens, UNITS), 1)
    name = jnp.where(lane < 3 * experts, lane % experts, -1).astype(F32)
    gates = jnp.zeros((tokens, UNITS), F32)
    for k in range(picks):
        one = note[:, width + k : width + k + 1]
        weight = (
            note[:, width + picks + k : width + picks + k + 1]
            + note[:, width + 2 * picks + k : width + 2 * picks + k + 1]
            + note[:, width + 3 * picks + k : width + 3 * picks + k + 1]
        )
        gates = jnp.where(name == one, weight, gates)
    mask = jnp.where((gates != 0.0) & (lane < experts), 1.0, 0.0)
    high = gates.astype(BF16)
    middle = (gates - high.astype(F32)).astype(BF16)
    rest = (gates - high.astype(F32) - middle.astype(F32)).astype(BF16)
    gates_out[...] = jnp.where(
        lane < experts,
        high.astype(F32),
        jnp.where(lane < 2 * experts, middle.astype(F32), rest.astype(F32)),
    ).astype(BF16)
    row = lax.broadcasted_iota(jnp.int32, (tokens, tokens), 0)
    column = lax.broadcasted_iota(jnp.int32, (tokens, tokens), 1)
    upto = jnp.where(column <= row, 1.0, 0.0).astype(BF16)
    count = dot(upto, mask.astype(BF16), ((1,), (0,)))
    total = jnp.broadcast_to(count[tokens - 1 : tokens, :], (8, UNITS))
    large = jnp.floor(total * (1.0 / 128.0))
    row = lax.broadcasted_iota(jnp.int32, (UNITS, UNITS), 0)
    column = lax.broadcasted_iota(jnp.int32, (UNITS, UNITS), 1)
    before = jnp.where(row < column, 1.0, 0.0).astype(BF16)
    base = 128.0 * dot(large.astype(BF16), before, ((1,), (0,)))
    base += dot((total - 128.0 * large).astype(BF16), before, ((1,), (0,)))
    base_out[...] = base.astype(jnp.int32)
    place = jnp.where(mask > 0.0, count - 1.0 + base[0:1, :], -1.0)
    place_out[...] = place.astype(jnp.int32)
    across_out[...] = place.T.astype(jnp.int32)


def order_of(note, width, picks, experts):
    tokens = note.shape[0]
    return pl.pallas_call(
        functools.partial(order_kernel, width, picks, experts),
        out_shape=[
            jax.ShapeDtypeStruct((tokens, UNITS), jnp.int32),
            jax.ShapeDtypeStruct((UNITS, tokens), jnp.int32),
            jax.ShapeDtypeStruct((tokens, UNITS), BF16),
            jax.ShapeDtypeStruct((8, UNITS), jnp.int32),
        ],
        compiler_params=params(),
        cost_estimate=cost(2 * tokens * tokens * UNITS, 4 * tokens * tokens),
        name="order",
    )(note)


def spans_of(base, rows):
    low = jnp.arange(rows // TILE, dtype=jnp.int32)[:, None] * TILE
    return (
        jnp.sum((base[None, 1:] <= low).astype(jnp.int32), axis=1),
        jnp.sum((base[None, :-1] < low + TILE).astype(jnp.int32), axis=1),
    )


def mine_of(base, e, row0):
    row = row0 + lax.broadcasted_iota(jnp.int32, (TILE, 1), 0)
    return (row >= base[e]) & (row < base[e + 1])


def sort_kernel(experts, low, high, base, across_ref, gates_ref, *refs):
    slices, (out, scale_out, onehot_ref, name_ref) = refs[:-4], refs[-4:]
    tokens = onehot_ref.shape[1]
    number = lax.broadcasted_iota(jnp.int32, (TILE, 128), 0).astype(F32).astype(BF16)
    onehot_ref[...] = jnp.zeros_like(onehot_ref)

    @pl.loop(0, BLOCK // TILE)
    def _(part):
        i = pl.program_id(0) * (BLOCK // TILE) + part
        row0 = i * TILE
        here = pl.ds(pl.multiple_of(part * TILE, TILE), TILE)

        @pl.loop(low[i], high[i])
        def _(e):
            away = across_ref[e] - row0
            away = jnp.where((away >= 0) & (away < TILE), away, -1).astype(F32)
            for c in range(tokens // 128):
                at = slice(c * 128, (c + 1) * 128)
                hit = number == away[c : c + 1, :].astype(BF16)
                onehot_ref[here, at] = jnp.where(hit, jnp.ones((), BF16), onehot_ref[here, at])
            name_ref[here, :] = jnp.where(mine_of(base, e, row0), e, name_ref[here, :])

    onehot = onehot_ref[...]
    for k, ref in enumerate(slices):
        out[:, k * LANES : (k + 1) * LANES] = dot(onehot, ref[...], ((1,), (0,))).astype(BF16)
    gates = dot(onehot, gates_ref[...], ((1,), (0,)))
    lane = lax.broadcasted_iota(jnp.int32, (BLOCK, UNITS), 1)
    name = name_ref[...]
    kept = (lane == name) | (lane == name + experts) | (lane == name + 2 * experts)
    scale = jnp.sum(jnp.where(kept, gates, 0.0), axis=1, keepdims=True)
    scale_out[...] = jnp.broadcast_to(scale, lane.shape)


def sort_rows(spans, base, across, gates, slices, rows, experts):
    tokens = gates.shape[0]
    across = across[:experts].reshape(experts, tokens // 128, 128)
    whole = lambda i, *_: (0, 0)
    width = len(slices) * LANES
    return pl.pallas_call(
        functools.partial(sort_kernel, experts),
        grid_spec=pltpu.PrefetchScalarGridSpec(
            num_scalar_prefetch=3,
            grid=(rows // BLOCK,),
            in_specs=[
                pl.BlockSpec(across.shape, lambda i, *_: (0, 0, 0)),
                pl.BlockSpec((tokens, UNITS), whole),
            ]
            + [pl.BlockSpec((tokens, LANES), whole)] * len(slices),
            out_specs=[
                pl.BlockSpec((BLOCK, width), lambda i, *_: (i, 0)),
                pl.BlockSpec((BLOCK, UNITS), lambda i, *_: (i, 0)),
                pl.BlockSpec((BLOCK, tokens), lambda i, *_: (i, 0)),
            ],
            scratch_shapes=[pltpu.VMEM((BLOCK, UNITS), jnp.int32)],
        ),
        out_shape=[
            jax.ShapeDtypeStruct((rows, width), BF16),
            jax.ShapeDtypeStruct((rows, UNITS), F32),
            jax.ShapeDtypeStruct((rows, tokens), BF16),
        ],
        compiler_params=params(),
        cost_estimate=cost(2 * rows * tokens * width, 8 * rows * width),
        name="sort_rows",
    )(*spans, base, across, gates, *slices)


def sort_more_kernel(onehot_ref, *refs):
    for k, ref in enumerate(refs[:-1]):
        at = slice(k * LANES, (k + 1) * LANES)
        refs[-1][:, at] = dot(onehot_ref[...], ref[...], ((1,), (0,))).astype(BF16)


def sort_more(onehot, slices):
    rows, tokens = onehot.shape
    width = len(slices) * LANES
    return pl.pallas_call(
        sort_more_kernel,
        grid=(rows // BLOCK,),
        in_specs=[pl.BlockSpec((BLOCK, tokens), lambda i: (i, 0))]
        + [pl.BlockSpec((tokens, LANES), lambda i: (0, 0))] * len(slices),
        out_specs=pl.BlockSpec((BLOCK, width), lambda i: (i, 0)),
        out_shape=jax.ShapeDtypeStruct((rows, width), BF16),
        compiler_params=params(),
        cost_estimate=cost(2 * rows * tokens * width, 8 * rows * width),
        name="sort_more",
    )(onehot, *slices)


def scatter_kernel(low, high, place_ref, onehot_ref):
    tokens = place_ref.shape[1]
    lane = lax.broadcasted_iota(jnp.int32, (tokens, 128), 1)
    onehot_ref[...] = jnp.zeros_like(onehot_ref)
    for part in range(BLOCK // TILE):
        i = pl.program_id(0) * (BLOCK // TILE) + part

        @pl.loop(low[i], high[i])
        def _(e):
            place = place_ref[e] - i * TILE
            for c in range(TILE // 128):
                at = slice(part * TILE + c * 128, part * TILE + (c + 1) * 128)
                onehot_ref[:, at] += jnp.where(place == lane + c * 128, 1.0, 0.0).astype(BF16)


def scatter_rows(spans, place, rows):
    tokens = place.shape[1]
    return pl.pallas_call(
        scatter_kernel,
        grid_spec=pltpu.PrefetchScalarGridSpec(
            num_scalar_prefetch=2,
            grid=(rows // BLOCK,),
            in_specs=[pl.BlockSpec(place.shape, lambda i, *_: (0, 0, 0))],
            out_specs=pl.BlockSpec((tokens, BLOCK), lambda i, *_: (0, i)),
        ),
        out_shape=jax.ShapeDtypeStruct((tokens, rows), BF16),
        compiler_params=params(),
        cost_estimate=cost(rows * tokens, 2 * rows * tokens),
        name="scatter_rows",
    )(*spans, place)


def partial_kernel(low, high, base, quarter, near_ref, far_ref, *refs):
    own, stacked, out = refs[:2], refs[2:-1], refs[-1]
    experts, width, _ = own[0].shape

    @pl.loop(0, BLOCK // TILE)
    def _(part):
        i = pl.program_id(0) * (BLOCK // TILE) + part
        here = pl.ds(pl.multiple_of(part * TILE, TILE), TILE)

        def add(e, kept):
            total = 0.0
            for k in range(4):
                pair = stacked[k - 1] if k else own
                pair = [pair[e], pair[experts + e]] if k else [pair[0][e], pair[1][e]]
                weight = jnp.concatenate(pair, axis=1)
                rows_ref, at = (near_ref, far_ref)[k // 2], k % 2 * LANES
                rows = rows_ref[here, at : at + width]
                total += dot(rows, weight, ((1,), (0,)))
            return jnp.where(mine_of(base, e, i * TILE), total, kept)

        out[here, :] = lax.fori_loop(
            low[i], high[i], add, jnp.zeros((TILE, out.shape[1]), F32)
        ).astype(BF16)


def partial_sums(f, spans, base, quarter, near, far, w_gate, w_up, pieces):
    rows = near.shape[0]
    experts, width, _ = w_gate.shape
    own = pl.BlockSpec((experts, width, UNITS), lambda i, lo, hi, b, q: (0, 0, 2 * q[0] + f))
    block = pl.BlockSpec((2 * experts, width, UNITS), lambda i, *_: (0, 0, 0))
    return pl.pallas_call(
        partial_kernel,
        grid_spec=pltpu.PrefetchScalarGridSpec(
            num_scalar_prefetch=4,
            grid=(rows // BLOCK,),
            in_specs=[pl.BlockSpec((BLOCK, 2 * LANES), lambda i, *_: (i, 0))] * 2 + [own] * 2
            + [block] * len(pieces),
            out_specs=pl.BlockSpec((BLOCK, 2 * UNITS), lambda i, *_: (i, 0)),
        ),
        out_shape=jax.ShapeDtypeStruct((rows, 2 * UNITS), BF16),
        compiler_params=params(),
        cost_estimate=cost(16 * rows * LANES * UNITS, 8 * rows * LANES),
        name="partial_sums",
    )(*spans, base, quarter, near, far, w_gate, w_up, *pieces)


def down_kernel(half, low, high, base, onehot_ref, hidden, start, *refs):
    weights, (out, total_ref, value_ref) = refs[:-3], refs[-3:]
    width = weights[0].shape[1]
    j = pl.program_id(0)

    @pl.when(j == 0)
    def _():
        total_ref[...] = jnp.zeros_like(total_ref) if start is None else start[...]
        value_ref[...] = jnp.zeros_like(value_ref)

    for part in range(BLOCK // TILE):
        i = (2 * j + half) * (BLOCK // TILE) + part
        here = slice(part * TILE, (part + 1) * TILE)
        units = hidden[here, :]

        @pl.loop(low[i], high[i])
        def _(e):
            mine = mine_of(base, e, i * TILE)
            for k, weight in enumerate(weights):
                value = dot(units, weight[e], ((1,), (1,)))
                at = slice(k * LANES, k * LANES + width)
                value_ref[here, at] = jnp.where(
                    mine, value, value_ref[here, at].astype(F32)
                ).astype(BF16)

    total_ref[...] += dot(onehot_ref[...], value_ref[...], ((1,), (0,)))

    @pl.when(j == pl.num_programs(0) - 1)
    def _():
        out[...] = total_ref[...].astype(out.dtype)


def down_and_mix(half, spans, base, onehot, hidden, start, weights, dtype):
    rows, units = hidden.shape
    count, tokens = len(weights), onehot.shape[0]
    block = pl.BlockSpec((BLOCK, units), lambda j, *_: (j, 0))
    whole = pl.BlockSpec((tokens, count * LANES), lambda j, *_: (0, 0))
    kernel = functools.partial(down_kernel, half)
    if start is None:
        kernel = lambda *refs: down_kernel(half, *refs[:5], None, *refs[5:])
    return pl.pallas_call(
        kernel,
        grid_spec=pltpu.PrefetchScalarGridSpec(
            num_scalar_prefetch=3,
            grid=(rows // BLOCK,),
            in_specs=[pl.BlockSpec((tokens, BLOCK), lambda j, *_: (0, 2 * j + half)), block]
            + ([] if start is None else [whole])
            + [pl.BlockSpec(w.shape, lambda j, *_: (0, 0, 0)) for w in weights],
            out_specs=whole,
            scratch_shapes=[
                pltpu.VMEM((tokens, count * LANES), F32),
                pltpu.VMEM((BLOCK, count * LANES), BF16),
            ],
        ),
        out_shape=jax.ShapeDtypeStruct((tokens, count * LANES), dtype),
        compiler_params=params(56),
        cost_estimate=cost(2 * rows * tokens * LANES * count, 2 * rows * tokens),
        name="down_and_mix",
    )(*spans, base, onehot, hidden, *([] if start is None else [start]), *weights)


def fixed_weights(size, tokens, expert_ids, gate_weights, w_gate, w_up, w_down):
    count, picks = expert_ids.shape
    experts, width, hidden_units = w_gate.shape
    quarter = hidden_units // 4
    rows = size * count * picks
    places = size // 4
    me, plane = lax.axis_index("ep"), lax.axis_index("parts")
    w_down = jnp.swapaxes(w_down, 1, 2)

    twins = [(i, i ^ 1) for i in range(size)]
    cross = [(p * size + i, p * size + (i ^ 2 ^ p)) for p in range(2) for i in range(size)]
    to_twin = lambda value: lax.ppermute(value, "ep", twins)
    to_cross = lambda value: lax.ppermute(value, ("parts", "ep"), cross)
    to_plane = lambda value: lax.ppermute(value, "parts", [(0, 1), (1, 0)])
    line = [[4 * p + k for p in range(places)] for k in range(4)]
    my_quarter = me % 4
    twin_quarter = my_quarter ^ 1
    cross_quarter = my_quarter ^ 2 ^ plane

    note = jnp.concatenate([expert_ids.astype(F32), *split3(gate_weights)], axis=1).astype(BF16)
    fill = LANES - width - note.shape[1]
    parcels = jnp.concatenate(
        [
            tokens.reshape(count, size, width).swapaxes(0, 1),
            jnp.broadcast_to(jnp.pad(note, ((0, 0), (0, fill)))[None], (size, count, LANES - width)),
        ],
        axis=2,
    )
    own = lax.all_to_all(parcels, "ep", split_axis=0, concat_axis=0, tiled=True)
    own = own.reshape(size * count, LANES)
    far, near = to_cross(own), [own, to_twin(own)]
    place, across, gates, base = order_of(own, width, picks, experts)
    base = base[0, : experts + 1]
    spans = spans_of(base, rows)
    which = my_quarter.astype(jnp.int32).reshape(1)

    def cut(n, q):
        if n == 2:
            return lax.dynamic_slice_in_dim(w_down, q * quarter, quarter, 2)
        at = q * quarter + n * UNITS
        return jnp.concatenate(
            [lax.dynamic_slice_in_dim(w, at, UNITS, 2) for w in (w_gate, w_up)], axis=0
        )

    def after(value, *others):
        return lax.optimization_barrier((value, *others))[0]

    near_rows, scale, onehot = sort_rows(spans, base, across, gates, near, rows, experts)
    far = after(far, near_rows)
    far_rows = sort_more(onehot, [far, to_twin(far)])
    scale = lax.dynamic_slice_in_dim(scale, (me // 4) * (rows // places), rows // places, 0)

    def fetch(n, *first):
        return to_cross(after(cut(n, cross_quarter), *first) if first else cut(n, cross_quarter))

    def group(n, across_x, *first):
        return (to_twin(cut(n, twin_quarter)), across_x, to_plane(after(across_x, *first)))

    def sums_of(f, held, *first):
        rows_in = after(far_rows, *first)
        return partial_sums(f, spans, base, which, near_rows, rows_in, w_gate, w_up, held)

    def units_of(sums):
        sums = lax.psum_scatter(
            sums, "ep", scatter_dimension=0, axis_index_groups=line, tiled=True
        ).astype(F32)
        return (jax.nn.silu(sums[:, :UNITS]) * sums[:, UNITS:] * scale).astype(BF16)

    second = fetch(1, far)
    third = fetch(2, second)
    sums = sums_of(0, group(0, fetch(0), near_rows), second)
    later = sums_of(1, group(1, second, far_rows), sums, third)
    units = [units_of(sums), units_of(later)]
    held = group(2, third, later)

    place = jnp.broadcast_to(
        after(across[:experts], later)[:, :, None], (experts, size * count, 128)
    )
    columns = scatter_rows(spans, place, rows)
    pieces = [after(cut(2, my_quarter), later), *held]
    units, columns, pieces = lax.optimization_barrier((units, columns, pieces))
    units = jnp.concatenate(units, axis=1).reshape(-1, BLOCK, 2 * UNITS)
    first, second = (
        lax.all_gather(units[half], "ep", axis=0, axis_index_groups=line, tiled=True)
        for half in range(2)
    )
    far_mix = lambda half, hidden, start, dtype: down_and_mix(
        half, spans, base, columns, hidden, start, pieces[2:], dtype
    )
    near_mix = lambda half, hidden, start, dtype: down_and_mix(
        half, spans, base, columns, hidden, start, pieces[:2], dtype
    )
    far, near = far_mix(0, first, None, F32), near_mix(0, first, None, F32)
    second, far, near = lax.optimization_barrier((second, far, near))
    far = far_mix(1, second, far, BF16)
    far, far_twin = far[:, :width], far[:, LANES : LANES + width]
    far = (far.astype(F32) + to_twin(far_twin).astype(F32)).astype(BF16)
    near, far = lax.optimization_barrier((near, far))
    far = to_cross(far)
    near = near_mix(1, second, near, F32)
    twin = near[:, LANES : LANES + width].astype(BF16)
    twin = to_twin(after(twin, far)).astype(F32)
    mixed = (near[:, :width] + twin + far.astype(F32)).astype(BF16)
    mixed = lax.all_to_all(
        mixed.reshape(size, count, width), "ep", split_axis=0, concat_axis=0, tiled=True
    )
    return mixed.swapaxes(0, 1).reshape(count, size * width)


def solution(mesh):
    size, inner = mesh.shape["ep"], mesh.shape["tp"]

    def body(tokens, expert_ids, gate_weights, w_gate, w_up, w_down):
        rows = size * math.prod(expert_ids.shape)
        sums = rows * w_gate.shape[2]
        experts, width, units = w_gate.shape
        even = (
            size % 4 == 0
            and size > 4
            and mesh.shape["parts"] == 2
            and rows == size // 4 * 2 * BLOCK
            and units == 8 * UNITS
            and 3 * experts <= UNITS
            and size * math.prod(expert_ids.shape[:1]) % 128 == 0
            and width + 4 * expert_ids.shape[1] <= LANES
        )
        args = (tokens, expert_ids, gate_weights, w_gate, w_up, w_down)
        if inner == 1 and even and sums <= 3 * math.prod(w_gate.shape):
            return fixed_weights(size, *args)
        return moved_weights(*args)

    placed = (
        P(("parts", "ep"), "tp"),
        P(("parts", "ep"), None),
        P(("parts", "ep"), None),
        P(None, "ep", "tp"),
        P(None, "ep", "tp"),
        P(None, "tp", "ep"),
    )
    return jax.shard_map(
        body, mesh=mesh, in_specs=placed, out_specs=P(("parts", "ep"), "tp"), check_vma=False
    )
```

```python
import functools
import math

import jax
import jax.numpy as jnp
from jax import lax
from jax.experimental import pallas as pl
from jax.experimental.pallas import tpu as pltpu
from jax.sharding import PartitionSpec as P

BF16 = jnp.bfloat16
F32 = jnp.float32
TILE = 256
BLOCK = 1024
LANES = 256
UNITS = 128


def slots_of(block_ids, experts):
    flat = block_ids.reshape(-1)
    onehot = (flat[:, None] == jnp.arange(experts, dtype=jnp.int32)[None, :]).astype(jnp.int32)
    before = jnp.cumsum(onehot, axis=0) - onehot
    return jnp.sum(before * onehot, axis=1).reshape(block_ids.shape)


def fill_slots(rows, expert_ids, slot, experts, per_expert):
    count, picks = expert_ids.shape
    spread = jnp.broadcast_to(rows[:, None, :], (count, picks, rows.shape[1]))
    empty = jnp.zeros((experts, per_expert, rows.shape[1]), BF16)
    return empty.at[expert_ids, slot].set(spread)


def moved_weights(tokens, expert_ids, gate_weights, w_gate, w_up, w_down):
    tok_rows, picks = expert_ids.shape
    experts = w_gate.shape[0]
    per_expert = min(tok_rows, 3 * tok_rows * picks // (2 * experts))
    slot = slots_of(expert_ids, experts)
    features = lax.all_gather(tokens, "tp", axis=1, tiled=True)
    outgoing = fill_slots(features, expert_ids, slot, experts, per_expert)
    arrived = lax.all_to_all(outgoing, "ep", split_axis=0, concat_axis=1, tiled=True)
    gate_owned, up_owned = (
        lax.all_to_all(w_gate, "ep", split_axis=0, concat_axis=1, tiled=True),
        lax.all_to_all(w_up, "ep", split_axis=0, concat_axis=1, tiled=True),
    )
    gate = jnp.einsum("ecd,edf->ecf", arrived, gate_owned, preferred_element_type=F32)
    up = jnp.einsum("ecd,edf->ecf", arrived, up_owned, preferred_element_type=F32)
    hidden = (jax.nn.silu(gate) * up).astype(BF16)
    down_owned = lax.all_to_all(w_down, "ep", split_axis=0, concat_axis=2, tiled=True)
    partial_value = jnp.einsum("ecf,efd->ecd", hidden, down_owned, preferred_element_type=F32)
    expert_out = lax.psum_scatter(
        partial_value.astype(BF16), "tp", scatter_dimension=2, tiled=True
    )
    returned = lax.all_to_all(expert_out, "ep", split_axis=1, concat_axis=0, tiled=True)
    picked = returned[expert_ids, slot]
    mixed = jnp.sum(gate_weights[:, :, None] * picked.astype(F32), axis=1)
    return mixed.astype(BF16)


def dot(a, b, contract):
    return lax.dot_general(a, b, ((contract[0], contract[1]), ((), ())), preferred_element_type=F32)


def params(mib=48):
    return pltpu.CompilerParams(vmem_limit_bytes=mib << 20)


def cost(flops, moved):
    return pl.CostEstimate(flops=flops, bytes_accessed=moved, transcendentals=0)


def split3(value):
    high = lax.reduce_precision(value, 8, 7)
    middle = lax.reduce_precision(value - high, 8, 7)
    return high, middle, lax.reduce_precision(value - high - middle, 8, 7)


def order_kernel(width, picks, experts, note_ref, place_out, across_out, gates_out, base_out):
    tokens = note_ref.shape[0]
    note = note_ref[...].astype(F32)
    lane = lax.broadcasted_iota(jnp.int32, (tokens, UNITS), 1)
    name = jnp.where(lane < 3 * experts, lane % experts, -1).astype(F32)
    gates = jnp.zeros((tokens, UNITS), F32)
    for k in range(picks):
        one = note[:, width + k : width + k + 1]
        weight = (
            note[:, width + picks + k : width + picks + k + 1]
            + note[:, width + 2 * picks + k : width + 2 * picks + k + 1]
            + note[:, width + 3 * picks + k : width + 3 * picks + k + 1]
        )
        gates = jnp.where(name == one, weight, gates)
    mask = jnp.where((gates != 0.0) & (lane < experts), 1.0, 0.0)
    high = gates.astype(BF16)
    middle = (gates - high.astype(F32)).astype(BF16)
    rest = (gates - high.astype(F32) - middle.astype(F32)).astype(BF16)
    gates_out[...] = jnp.where(
        lane < experts,
        high.astype(F32),
        jnp.where(lane < 2 * experts, middle.astype(F32), rest.astype(F32)),
    ).astype(BF16)
    row = lax.broadcasted_iota(jnp.int32, (tokens, tokens), 0)
    column = lax.broadcasted_iota(jnp.int32, (tokens, tokens), 1)
    upto = jnp.where(column <= row, 1.0, 0.0).astype(BF16)
    count = dot(upto, mask.astype(BF16), ((1,), (0,)))
    total = jnp.broadcast_to(count[tokens - 1 : tokens, :], (8, UNITS))
    large = jnp.floor(total * (1.0 / 128.0))
    row = lax.broadcasted_iota(jnp.int32, (UNITS, UNITS), 0)
    column = lax.broadcasted_iota(jnp.int32, (UNITS, UNITS), 1)
    before = jnp.where(row < column, 1.0, 0.0).astype(BF16)
    base = 128.0 * dot(large.astype(BF16), before, ((1,), (0,)))
    base += dot((total - 128.0 * large).astype(BF16), before, ((1,), (0,)))
    base_out[...] = base.astype(jnp.int32)
    place = jnp.where(mask > 0.0, count - 1.0 + base[0:1, :], -1.0)
    place_out[...] = place.astype(jnp.int32)
    across_out[...] = place.T.astype(jnp.int32)


def order_of(note, width, picks, experts):
    tokens = note.shape[0]
    return pl.pallas_call(
        functools.partial(order_kernel, width, picks, experts),
        out_shape=[
            jax.ShapeDtypeStruct((tokens, UNITS), jnp.int32),
            jax.ShapeDtypeStruct((UNITS, tokens), jnp.int32),
            jax.ShapeDtypeStruct((tokens, UNITS), BF16),
            jax.ShapeDtypeStruct((8, UNITS), jnp.int32),
        ],
        compiler_params=params(),
        cost_estimate=cost(2 * tokens * tokens * UNITS, 4 * tokens * tokens),
        name="order",
    )(note)


def spans_of(base, rows):
    low = jnp.arange(rows // TILE, dtype=jnp.int32)[:, None] * TILE
    return (
        jnp.sum((base[None, 1:] <= low).astype(jnp.int32), axis=1),
        jnp.sum((base[None, :-1] < low + TILE).astype(jnp.int32), axis=1),
    )


def mine_of(base, e, row0):
    row = row0 + lax.broadcasted_iota(jnp.int32, (TILE, 1), 0)
    return (row >= base[e]) & (row < base[e + 1])


def sort_kernel(experts, low, high, base, across_ref, gates_ref, *refs):
    slices, (out, scale_out, onehot_ref, name_ref) = refs[:-4], refs[-4:]
    tokens = onehot_ref.shape[1]
    number = lax.broadcasted_iota(jnp.int32, (TILE, 128), 0).astype(F32).astype(BF16)
    onehot_ref[...] = jnp.zeros_like(onehot_ref)

    @pl.loop(0, BLOCK // TILE)
    def _(part):
        i = pl.program_id(0) * (BLOCK // TILE) + part
        row0 = i * TILE
        here = pl.ds(pl.multiple_of(part * TILE, TILE), TILE)

        @pl.loop(low[i], high[i])
        def _(e):
            away = across_ref[e] - row0
            away = jnp.where((away >= 0) & (away < TILE), away, -1).astype(F32)
            for c in range(tokens // 128):
                at = slice(c * 128, (c + 1) * 128)
                hit = number == away[c : c + 1, :].astype(BF16)
                onehot_ref[here, at] = jnp.where(hit, jnp.ones((), BF16), onehot_ref[here, at])
            name_ref[here, :] = jnp.where(mine_of(base, e, row0), e, name_ref[here, :])

    onehot = onehot_ref[...]
    for k, ref in enumerate(slices):
        out[:, k * LANES : (k + 1) * LANES] = dot(onehot, ref[...], ((1,), (0,))).astype(BF16)
    gates = dot(onehot, gates_ref[...], ((1,), (0,)))
    lane = lax.broadcasted_iota(jnp.int32, (BLOCK, UNITS), 1)
    name = name_ref[...]
    kept = (lane == name) | (lane == name + experts) | (lane == name + 2 * experts)
    scale = jnp.sum(jnp.where(kept, gates, 0.0), axis=1, keepdims=True)
    scale_out[...] = jnp.broadcast_to(scale, lane.shape)


def sort_rows(spans, base, across, gates, slices, rows, experts):
    tokens = gates.shape[0]
    across = across[:experts].reshape(experts, tokens // 128, 128)
    whole = lambda i, *_: (0, 0)
    width = len(slices) * LANES
    return pl.pallas_call(
        functools.partial(sort_kernel, experts),
        grid_spec=pltpu.PrefetchScalarGridSpec(
            num_scalar_prefetch=3,
            grid=(rows // BLOCK,),
            in_specs=[
                pl.BlockSpec(across.shape, lambda i, *_: (0, 0, 0)),
                pl.BlockSpec((tokens, UNITS), whole),
            ]
            + [pl.BlockSpec((tokens, LANES), whole)] * len(slices),
            out_specs=[
                pl.BlockSpec((BLOCK, width), lambda i, *_: (i, 0)),
                pl.BlockSpec((BLOCK, UNITS), lambda i, *_: (i, 0)),
                pl.BlockSpec((BLOCK, tokens), lambda i, *_: (i, 0)),
            ],
            scratch_shapes=[pltpu.VMEM((BLOCK, UNITS), jnp.int32)],
        ),
        out_shape=[
            jax.ShapeDtypeStruct((rows, width), BF16),
            jax.ShapeDtypeStruct((rows, UNITS), F32),
            jax.ShapeDtypeStruct((rows, tokens), BF16),
        ],
        compiler_params=params(),
        cost_estimate=cost(2 * rows * tokens * width, 8 * rows * width),
        name="sort_rows",
    )(*spans, base, across, gates, *slices)


def sort_more_kernel(onehot_ref, *refs):
    for k, ref in enumerate(refs[:-1]):
        at = slice(k * LANES, (k + 1) * LANES)
        refs[-1][:, at] = dot(onehot_ref[...], ref[...], ((1,), (0,))).astype(BF16)


def sort_more(onehot, slices):
    rows, tokens = onehot.shape
    width = len(slices) * LANES
    return pl.pallas_call(
        sort_more_kernel,
        grid=(rows // BLOCK,),
        in_specs=[pl.BlockSpec((BLOCK, tokens), lambda i: (i, 0))]
        + [pl.BlockSpec((tokens, LANES), lambda i: (0, 0))] * len(slices),
        out_specs=pl.BlockSpec((BLOCK, width), lambda i: (i, 0)),
        out_shape=jax.ShapeDtypeStruct((rows, width), BF16),
        compiler_params=params(),
        cost_estimate=cost(2 * rows * tokens * width, 8 * rows * width),
        name="sort_more",
    )(onehot, *slices)


def scatter_kernel(low, high, place_ref, onehot_ref):
    tokens = place_ref.shape[1]
    lane = lax.broadcasted_iota(jnp.int32, (tokens, 128), 1)
    onehot_ref[...] = jnp.zeros_like(onehot_ref)
    for part in range(BLOCK // TILE):
        i = pl.program_id(0) * (BLOCK // TILE) + part

        @pl.loop(low[i], high[i])
        def _(e):
            place = place_ref[e] - i * TILE
            for c in range(TILE // 128):
                at = slice(part * TILE + c * 128, part * TILE + (c + 1) * 128)
                onehot_ref[:, at] += jnp.where(place == lane + c * 128, 1.0, 0.0).astype(BF16)


def scatter_rows(spans, place, rows):
    tokens = place.shape[1]
    return pl.pallas_call(
        scatter_kernel,
        grid_spec=pltpu.PrefetchScalarGridSpec(
            num_scalar_prefetch=2,
            grid=(rows // BLOCK,),
            in_specs=[pl.BlockSpec(place.shape, lambda i, *_: (0, 0, 0))],
            out_specs=pl.BlockSpec((tokens, BLOCK), lambda i, *_: (0, i)),
        ),
        out_shape=jax.ShapeDtypeStruct((tokens, rows), BF16),
        compiler_params=params(),
        cost_estimate=cost(rows * tokens, 2 * rows * tokens),
        name="scatter_rows",
    )(*spans, place)


def partial_kernel(low, high, base, quarter, near_ref, far_ref, *refs):
    pairs, out = [refs[j : j + 2] for j in range(0, 8, 2)], refs[-1]
    width = pairs[0][0].shape[1]

    @pl.loop(0, BLOCK // TILE)
    def _(part):
        i = pl.program_id(0) * (BLOCK // TILE) + part
        here = pl.ds(pl.multiple_of(part * TILE, TILE), TILE)

        def add(e, kept):
            total = 0.0
            for k, pair in enumerate(pairs):
                weight = jnp.concatenate([pair[0][e], pair[1][e]], axis=1)
                rows_ref, at = (near_ref, far_ref)[k // 2], k % 2 * LANES
                rows = rows_ref[here, at : at + width]
                total += dot(rows, weight, ((1,), (0,)))
            return jnp.where(mine_of(base, e, i * TILE), total, kept)

        out[here, :] = lax.fori_loop(
            low[i], high[i], add, jnp.zeros((TILE, out.shape[1]), F32)
        ).astype(BF16)


def partial_sums(f, spans, base, quarter, near, far, w_gate, w_up, pieces):
    rows = near.shape[0]
    experts, width, _ = w_gate.shape
    own = pl.BlockSpec((experts, width, UNITS), lambda i, lo, hi, b, q: (0, 0, 2 * q[0] + f))
    block = pl.BlockSpec((experts, width, UNITS), lambda i, *_: (0, 0, 0))
    return pl.pallas_call(
        partial_kernel,
        grid_spec=pltpu.PrefetchScalarGridSpec(
            num_scalar_prefetch=4,
            grid=(rows // BLOCK,),
            in_specs=[pl.BlockSpec((BLOCK, 2 * LANES), lambda i, *_: (i, 0))] * 2 + [own] * 2
            + [block] * len(pieces),
            out_specs=pl.BlockSpec((BLOCK, 2 * UNITS), lambda i, *_: (i, 0)),
        ),
        out_shape=jax.ShapeDtypeStruct((rows, 2 * UNITS), BF16),
        compiler_params=params(),
        cost_estimate=cost(16 * rows * LANES * UNITS, 8 * rows * LANES),
        name="partial_sums",
    )(*spans, base, quarter, near, far, w_gate, w_up, *pieces)


def down_kernel(low, high, base, block, onehot_ref, up_ref, down_ref, start, *refs):
    weights, (out, total_ref, value_ref) = refs[:-3], refs[-3:]
    width = weights[0].shape[1]
    j = pl.program_id(0)

    @pl.when(j == 0)
    def _():
        total_ref[...] = jnp.zeros_like(total_ref) if start is None else start[...]
        value_ref[...] = jnp.zeros_like(value_ref)

    @pl.when(block[2] != 0)
    def _():
        for part in range(BLOCK // TILE):
            i = (2 * block[0] + j) * (BLOCK // TILE) + part
            here = slice(part * TILE, (part + 1) * TILE)
            units = jnp.where(block[1] != 0, up_ref[here, :], down_ref[here, :])

            @pl.loop(low[i], high[i])
            def _(e):
                mine = mine_of(base, e, i * TILE)
                for k, weight in enumerate(weights):
                    value = dot(units, weight[e], ((1,), (1,)))
                    at = slice(k * LANES, k * LANES + width)
                    value_ref[here, at] = jnp.where(
                        mine, value, value_ref[here, at].astype(F32)
                    ).astype(BF16)

        total_ref[...] += dot(onehot_ref[...], value_ref[...], ((1,), (0,)))

    @pl.when(j == pl.num_programs(0) - 1)
    def _():
        out[...] = total_ref[...].astype(out.dtype)


def down_and_mix(spans, base, block, onehot, hidden, start, at, weights, dtype):
    rows, units = hidden[0].shape
    count, tokens = len(weights), onehot.shape[0]
    some = pl.BlockSpec((BLOCK, units), lambda j, *_: (j, 0))
    whole = pl.BlockSpec((tokens, count * LANES), lambda j, *_: (0, 0))
    kernel = down_kernel
    if start is None:
        kernel = lambda *refs: down_kernel(*refs[:7], None, *refs[7:])
    return pl.pallas_call(
        kernel,
        grid_spec=pltpu.PrefetchScalarGridSpec(
            num_scalar_prefetch=4,
            grid=(rows // BLOCK,),
            in_specs=[
                pl.BlockSpec((tokens, BLOCK), lambda j, lo, hi, b, k: (0, 2 * k[0] + j)),
                some,
                some,
            ]
            + [pl.BlockSpec((tokens, count * LANES), lambda j, *_: (0, at // count))]
            * (start is not None)
            + [pl.BlockSpec(w.shape, lambda j, *_: (0, 0, 0)) for w in weights],
            out_specs=whole,
            scratch_shapes=[
                pltpu.VMEM((tokens, count * LANES), F32),
                pltpu.VMEM((BLOCK, count * LANES), BF16),
            ],
        ),
        out_shape=jax.ShapeDtypeStruct((tokens, count * LANES), dtype),
        compiler_params=params(56),
        cost_estimate=cost(2 * rows * tokens * LANES * count, 2 * rows * tokens),
        name="down_and_mix",
    )(*spans, base, block, onehot, *hidden, *([] if start is None else [start]), *weights)


def fixed_weights(size, tokens, expert_ids, gate_weights, w_gate, w_up, w_down):
    count, picks = expert_ids.shape
    experts, width, hidden_units = w_gate.shape
    quarter = hidden_units // 4
    rows = size * count * picks
    places = size // 4
    me, plane = lax.axis_index("ep"), lax.axis_index("parts")
    w_down = jnp.swapaxes(w_down, 1, 2)

    twins = [(i, i ^ 1) for i in range(size)]
    cross = [(p * size + i, p * size + (i ^ 2 ^ p)) for p in range(2) for i in range(size)]
    to_twin = lambda value: lax.ppermute(value, "ep", twins)
    to_cross = lambda value: lax.ppermute(value, ("parts", "ep"), cross)
    to_plane = lambda value: lax.ppermute(value, "parts", [(0, 1), (1, 0)])
    line = [[4 * p + k for p in range(places)] for k in range(4)]
    my_quarter = me % 4
    twin_quarter = my_quarter ^ 1
    cross_quarter = my_quarter ^ 2 ^ plane

    note = jnp.concatenate([expert_ids.astype(F32), *split3(gate_weights)], axis=1).astype(BF16)
    fill = LANES - width - note.shape[1]
    parcels = jnp.concatenate(
        [
            tokens.reshape(count, size, width).swapaxes(0, 1),
            jnp.broadcast_to(jnp.pad(note, ((0, 0), (0, fill)))[None], (size, count, LANES - width)),
        ],
        axis=2,
    )
    own = lax.all_to_all(parcels, "ep", split_axis=0, concat_axis=0, tiled=True)
    own = own.reshape(size * count, LANES)
    far, near = to_cross(own), [own, to_twin(own)]
    place, across, gates, base = order_of(own, width, picks, experts)
    base = base[0, : experts + 1]
    spans = spans_of(base, rows)
    which = my_quarter.astype(jnp.int32).reshape(1)

    def cut(n, q):
        if n == 4:
            return lax.dynamic_slice_in_dim(w_down, q * quarter, quarter, 2)
        at = q * quarter + n // 2 * UNITS
        return lax.dynamic_slice_in_dim((w_gate, w_up)[n % 2], at, UNITS, 2)

    def after(value, *others):
        return lax.optimization_barrier((value, *others))[0]

    near_rows, scale, onehot = sort_rows(spans, base, across, gates, near, rows, experts)
    far = after(far, near_rows)
    far_rows = sort_more(onehot, [far, to_twin(far)])
    scale = lax.dynamic_slice_in_dim(scale, (me // 4) * (rows // places), rows // places, 0)

    crossed = [to_cross(cut(0, cross_quarter)), to_cross(cut(1, cross_quarter))]
    for n in range(2, 5):
        crossed.append(to_cross(after(cut(n, cross_quarter), far, *crossed[2:n])))
    twin_of = lambda n: to_twin(cut(n, twin_quarter))

    def sums_of(f, *first):
        rows_in = after(far_rows, *first)
        across_x = crossed[2 * f : 2 * f + 2]
        beside = [to_plane(after(piece, near_rows)) for piece in across_x]
        held = [twin_of(2 * f), twin_of(2 * f + 1), *across_x, *beside]
        return partial_sums(f, spans, base, which, near_rows, rows_in, w_gate, w_up, held)

    def units_of(sums):
        sums = lax.psum_scatter(
            sums, "ep", scatter_dimension=0, axis_index_groups=line, tiled=True
        ).astype(F32)
        return (jax.nn.silu(sums[:, :UNITS]) * sums[:, UNITS:] * scale).astype(BF16)

    sums = sums_of(0, crossed[2])
    later = sums_of(1, sums)
    units = [units_of(sums), units_of(later)]
    held = [twin_of(4), crossed[4], to_plane(crossed[4])]

    place = jnp.broadcast_to(
        after(across[:experts], later)[:, :, None], (experts, size * count, 128)
    )
    columns = scatter_rows(spans, place, rows)
    pieces = [after(cut(4, my_quarter), later), *held]
    units, columns, pieces = lax.optimization_barrier((units, columns, pieces))
    units = jnp.concatenate(units, axis=1)

    spot = me // 4

    def steps(value, step, up):
        links = [
            (4 * p + k, 4 * (p + 1 if up else p - 1) + k)
            for p in (range(step - 1, places - 1) if up else range(1, places - step + 1))
            for k in range(4)
        ]
        return lax.ppermute(value, "ep", links)

    def mix(flags, hidden, start, at=0, count=4, dtype=F32):
        block = jnp.stack([jnp.asarray(flag, jnp.int32) for flag in flags])
        return down_and_mix(
            spans, base, block, columns, hidden, start, at, pieces[at : at + count], dtype
        )

    moving = [steps(units, 1, True), steps(units, 1, False)]
    total, waiting = mix((spot, 1, 1), [units, units], None), []
    for step in range(1, places):
        if step == places - 1:
            for flags, hidden in waiting:
                total = mix(flags, hidden, total)
        *hidden, total = lax.optimization_barrier((*moving, total))
        came_up, came_down = spot >= step, spot < places - step
        above = jnp.minimum(spot + step, places - 1)
        flags = (jnp.where(came_up, spot - step, above), came_up, came_up | came_down)
        if step == places - 1:
            break
        moving = [steps(hidden[0], step + 1, True), steps(hidden[1], step + 1, False)]
        waiting.append((flags, hidden))
        if 2 * step < places:
            waiting.append(((above, 0, came_up & came_down), hidden))
        total = mix(*waiting.pop(0), total)
    far = mix(flags, hidden, total, 2, 2, BF16)
    near = after(total, far)
    far, far_twin = far[:, :width], far[:, LANES : LANES + width]
    far = (far.astype(F32) + to_twin(far_twin).astype(F32)).astype(BF16)
    near, far = lax.optimization_barrier((near, far))
    far = to_cross(far)
    near = mix(flags, hidden, near, 0, 2)
    twin = near[:, LANES : LANES + width].astype(BF16)
    twin = to_twin(after(twin, far)).astype(F32)
    mixed = (near[:, :width] + twin + far.astype(F32)).astype(BF16)
    mixed = lax.all_to_all(
        mixed.reshape(size, count, width), "ep", split_axis=0, concat_axis=0, tiled=True
    )
    return mixed.swapaxes(0, 1).reshape(count, size * width)


def solution(mesh):
    size, inner = mesh.shape["ep"], mesh.shape["tp"]

    def body(tokens, expert_ids, gate_weights, w_gate, w_up, w_down):
        rows = size * math.prod(expert_ids.shape)
        sums = rows * w_gate.shape[2]
        experts, width, units = w_gate.shape
        even = (
            size % 4 == 0
            and size > 4
            and mesh.shape["parts"] == 2
            and rows == size // 4 * 2 * BLOCK
            and units == 8 * UNITS
            and 3 * experts <= UNITS
            and size * math.prod(expert_ids.shape[:1]) % 128 == 0
            and width + 4 * expert_ids.shape[1] <= LANES
        )
        args = (tokens, expert_ids, gate_weights, w_gate, w_up, w_down)
        if inner == 1 and even and sums <= 3 * math.prod(w_gate.shape):
            return fixed_weights(size, *args)
        return moved_weights(*args)

    placed = (
        P(("parts", "ep"), "tp"),
        P(("parts", "ep"), None),
        P(("parts", "ep"), None),
        P(None, "ep", "tp"),
        P(None, "ep", "tp"),
        P(None, "tp", "ep"),
    )
    return jax.shard_map(
        body, mesh=mesh, in_specs=placed, out_specs=P(("parts", "ep"), "tp"), check_vma=False
    )
```

```python
import functools
import math

import jax
import jax.numpy as jnp
from jax import lax
from jax.experimental import pallas as pl
from jax.experimental.pallas import tpu as pltpu
from jax.sharding import PartitionSpec as P

BF16 = jnp.bfloat16
F32 = jnp.float32
TILE = 256
BLOCK = 1024
LANES = 256
UNITS = 128


def slots_of(block_ids, experts):
    flat = block_ids.reshape(-1)
    onehot = (flat[:, None] == jnp.arange(experts, dtype=jnp.int32)[None, :]).astype(jnp.int32)
    before = jnp.cumsum(onehot, axis=0) - onehot
    return jnp.sum(before * onehot, axis=1).reshape(block_ids.shape)


def fill_slots(rows, expert_ids, slot, experts, per_expert):
    count, picks = expert_ids.shape
    spread = jnp.broadcast_to(rows[:, None, :], (count, picks, rows.shape[1]))
    empty = jnp.zeros((experts, per_expert, rows.shape[1]), BF16)
    return empty.at[expert_ids, slot].set(spread)


def moved_weights(tokens, expert_ids, gate_weights, w_gate, w_up, w_down):
    tok_rows, picks = expert_ids.shape
    experts = w_gate.shape[0]
    per_expert = min(tok_rows, 3 * tok_rows * picks // (2 * experts))
    slot = slots_of(expert_ids, experts)
    features = lax.all_gather(tokens, "tp", axis=1, tiled=True)
    outgoing = fill_slots(features, expert_ids, slot, experts, per_expert)
    arrived = lax.all_to_all(outgoing, "ep", split_axis=0, concat_axis=1, tiled=True)
    gate_owned, up_owned = (
        lax.all_to_all(w_gate, "ep", split_axis=0, concat_axis=1, tiled=True),
        lax.all_to_all(w_up, "ep", split_axis=0, concat_axis=1, tiled=True),
    )
    gate = jnp.einsum("ecd,edf->ecf", arrived, gate_owned, preferred_element_type=F32)
    up = jnp.einsum("ecd,edf->ecf", arrived, up_owned, preferred_element_type=F32)
    hidden = (jax.nn.silu(gate) * up).astype(BF16)
    down_owned = lax.all_to_all(w_down, "ep", split_axis=0, concat_axis=2, tiled=True)
    partial_value = jnp.einsum("ecf,efd->ecd", hidden, down_owned, preferred_element_type=F32)
    expert_out = lax.psum_scatter(
        partial_value.astype(BF16), "tp", scatter_dimension=2, tiled=True
    )
    returned = lax.all_to_all(expert_out, "ep", split_axis=1, concat_axis=0, tiled=True)
    picked = returned[expert_ids, slot]
    mixed = jnp.sum(gate_weights[:, :, None] * picked.astype(F32), axis=1)
    return mixed.astype(BF16)


def dot(a, b, contract):
    return lax.dot_general(a, b, ((contract[0], contract[1]), ((), ())), preferred_element_type=F32)


def params(mib=48):
    return pltpu.CompilerParams(vmem_limit_bytes=mib << 20)


def cost(flops, moved):
    return pl.CostEstimate(flops=flops, bytes_accessed=moved, transcendentals=0)


def split3(value):
    high = lax.reduce_precision(value, 8, 7)
    middle = lax.reduce_precision(value - high, 8, 7)
    return high, middle, lax.reduce_precision(value - high - middle, 8, 7)


def order_kernel(width, picks, experts, note_ref, place_out, across_out, gates_out, base_out):
    tokens = note_ref.shape[0]
    note = note_ref[...].astype(F32)
    lane = lax.broadcasted_iota(jnp.int32, (tokens, UNITS), 1)
    name = jnp.where(lane < 3 * experts, lane % experts, -1).astype(F32)
    gates = jnp.zeros((tokens, UNITS), F32)
    for k in range(picks):
        one = note[:, width + k : width + k + 1]
        weight = (
            note[:, width + picks + k : width + picks + k + 1]
            + note[:, width + 2 * picks + k : width + 2 * picks + k + 1]
            + note[:, width + 3 * picks + k : width + 3 * picks + k + 1]
        )
        gates = jnp.where(name == one, weight, gates)
    mask = jnp.where((gates != 0.0) & (lane < experts), 1.0, 0.0)
    high = gates.astype(BF16)
    middle = (gates - high.astype(F32)).astype(BF16)
    rest = (gates - high.astype(F32) - middle.astype(F32)).astype(BF16)
    gates_out[...] = jnp.where(
        lane < experts,
        high.astype(F32),
        jnp.where(lane < 2 * experts, middle.astype(F32), rest.astype(F32)),
    ).astype(BF16)
    row = lax.broadcasted_iota(jnp.int32, (tokens, tokens), 0)
    column = lax.broadcasted_iota(jnp.int32, (tokens, tokens), 1)
    upto = jnp.where(column <= row, 1.0, 0.0).astype(BF16)
    count = dot(upto, mask.astype(BF16), ((1,), (0,)))
    total = jnp.broadcast_to(count[tokens - 1 : tokens, :], (8, UNITS))
    large = jnp.floor(total * (1.0 / 128.0))
    row = lax.broadcasted_iota(jnp.int32, (UNITS, UNITS), 0)
    column = lax.broadcasted_iota(jnp.int32, (UNITS, UNITS), 1)
    before = jnp.where(row < column, 1.0, 0.0).astype(BF16)
    base = 128.0 * dot(large.astype(BF16), before, ((1,), (0,)))
    base += dot((total - 128.0 * large).astype(BF16), before, ((1,), (0,)))
    base_out[...] = base.astype(jnp.int32)
    place = jnp.where(mask > 0.0, count - 1.0 + base[0:1, :], -1.0)
    place_out[...] = place.astype(jnp.int32)
    across_out[...] = place.T.astype(jnp.int32)


def order_of(note, width, picks, experts):
    tokens = note.shape[0]
    return pl.pallas_call(
        functools.partial(order_kernel, width, picks, experts),
        out_shape=[
            jax.ShapeDtypeStruct((tokens, UNITS), jnp.int32),
            jax.ShapeDtypeStruct((UNITS, tokens), jnp.int32),
            jax.ShapeDtypeStruct((tokens, UNITS), BF16),
            jax.ShapeDtypeStruct((8, UNITS), jnp.int32),
        ],
        compiler_params=params(),
        cost_estimate=cost(2 * tokens * tokens * UNITS, 4 * tokens * tokens),
        name="order",
    )(note)


def spans_of(base, rows):
    low = jnp.arange(rows // TILE, dtype=jnp.int32)[:, None] * TILE
    return (
        jnp.sum((base[None, 1:] <= low).astype(jnp.int32), axis=1),
        jnp.sum((base[None, :-1] < low + TILE).astype(jnp.int32), axis=1),
    )


def mine_of(base, e, row0):
    row = row0 + lax.broadcasted_iota(jnp.int32, (TILE, 1), 0)
    return (row >= base[e]) & (row < base[e + 1])


def sort_kernel(experts, low, high, base, across_ref, gates_ref, *refs):
    slices, (out, scale_out, onehot_ref, name_ref) = refs[:-4], refs[-4:]
    tokens = onehot_ref.shape[1]
    number = lax.broadcasted_iota(jnp.int32, (TILE, 128), 0).astype(F32).astype(BF16)
    onehot_ref[...] = jnp.zeros_like(onehot_ref)

    @pl.loop(0, BLOCK // TILE)
    def _(part):
        i = pl.program_id(0) * (BLOCK // TILE) + part
        row0 = i * TILE
        here = pl.ds(pl.multiple_of(part * TILE, TILE), TILE)

        @pl.loop(low[i], high[i])
        def _(e):
            away = across_ref[e] - row0
            away = jnp.where((away >= 0) & (away < TILE), away, -1).astype(F32)
            for c in range(tokens // 128):
                at = slice(c * 128, (c + 1) * 128)
                hit = number == away[c : c + 1, :].astype(BF16)
                onehot_ref[here, at] = jnp.where(hit, jnp.ones((), BF16), onehot_ref[here, at])
            name_ref[here, :] = jnp.where(mine_of(base, e, row0), e, name_ref[here, :])

    onehot = onehot_ref[...]
    for k, ref in enumerate(slices):
        out[:, k * LANES : (k + 1) * LANES] = dot(onehot, ref[...], ((1,), (0,))).astype(BF16)
    gates = dot(onehot, gates_ref[...], ((1,), (0,)))
    lane = lax.broadcasted_iota(jnp.int32, (BLOCK, UNITS), 1)
    name = name_ref[...]
    kept = (lane == name) | (lane == name + experts) | (lane == name + 2 * experts)
    scale = jnp.sum(jnp.where(kept, gates, 0.0), axis=1, keepdims=True)
    scale_out[...] = jnp.broadcast_to(scale, lane.shape)


def sort_rows(spans, base, across, gates, slices, rows, experts):
    tokens = gates.shape[0]
    across = across[:experts].reshape(experts, tokens // 128, 128)
    whole = lambda i, *_: (0, 0)
    width = len(slices) * LANES
    return pl.pallas_call(
        functools.partial(sort_kernel, experts),
        grid_spec=pltpu.PrefetchScalarGridSpec(
            num_scalar_prefetch=3,
            grid=(rows // BLOCK,),
            in_specs=[
                pl.BlockSpec(across.shape, lambda i, *_: (0, 0, 0)),
                pl.BlockSpec((tokens, UNITS), whole),
            ]
            + [pl.BlockSpec((tokens, LANES), whole)] * len(slices),
            out_specs=[
                pl.BlockSpec((BLOCK, width), lambda i, *_: (i, 0)),
                pl.BlockSpec((BLOCK, UNITS), lambda i, *_: (i, 0)),
                pl.BlockSpec((BLOCK, tokens), lambda i, *_: (i, 0)),
            ],
            scratch_shapes=[pltpu.VMEM((BLOCK, UNITS), jnp.int32)],
        ),
        out_shape=[
            jax.ShapeDtypeStruct((rows, width), BF16),
            jax.ShapeDtypeStruct((rows, UNITS), F32),
            jax.ShapeDtypeStruct((rows, tokens), BF16),
        ],
        compiler_params=params(),
        cost_estimate=cost(2 * rows * tokens * width, 8 * rows * width),
        name="sort_rows",
    )(*spans, base, across, gates, *slices)


def sort_more_kernel(onehot_ref, *refs):
    for k, ref in enumerate(refs[:-1]):
        at = slice(k * LANES, (k + 1) * LANES)
        refs[-1][:, at] = dot(onehot_ref[...], ref[...], ((1,), (0,))).astype(BF16)


def sort_more(onehot, slices):
    rows, tokens = onehot.shape
    width = len(slices) * LANES
    return pl.pallas_call(
        sort_more_kernel,
        grid=(rows // BLOCK,),
        in_specs=[pl.BlockSpec((BLOCK, tokens), lambda i: (i, 0))]
        + [pl.BlockSpec((tokens, LANES), lambda i: (0, 0))] * len(slices),
        out_specs=pl.BlockSpec((BLOCK, width), lambda i: (i, 0)),
        out_shape=jax.ShapeDtypeStruct((rows, width), BF16),
        compiler_params=params(),
        cost_estimate=cost(2 * rows * tokens * width, 8 * rows * width),
        name="sort_more",
    )(onehot, *slices)


def scatter_kernel(low, high, place_ref, onehot_ref):
    tokens = place_ref.shape[1]
    lane = lax.broadcasted_iota(jnp.int32, (tokens, 128), 1)
    onehot_ref[...] = jnp.zeros_like(onehot_ref)
    for part in range(BLOCK // TILE):
        i = pl.program_id(0) * (BLOCK // TILE) + part

        @pl.loop(low[i], high[i])
        def _(e):
            place = place_ref[e] - i * TILE
            for c in range(TILE // 128):
                at = slice(part * TILE + c * 128, part * TILE + (c + 1) * 128)
                onehot_ref[:, at] += jnp.where(place == lane + c * 128, 1.0, 0.0).astype(BF16)


def scatter_rows(spans, place, rows):
    tokens = place.shape[1]
    return pl.pallas_call(
        scatter_kernel,
        grid_spec=pltpu.PrefetchScalarGridSpec(
            num_scalar_prefetch=2,
            grid=(rows // BLOCK,),
            in_specs=[pl.BlockSpec(place.shape, lambda i, *_: (0, 0, 0))],
            out_specs=pl.BlockSpec((tokens, BLOCK), lambda i, *_: (0, i)),
        ),
        out_shape=jax.ShapeDtypeStruct((tokens, rows), BF16),
        compiler_params=params(),
        cost_estimate=cost(rows * tokens, 2 * rows * tokens),
        name="scatter_rows",
    )(*spans, place)


def partial_kernel(low, high, base, quarter, near_ref, far_ref, *refs):
    pairs, out = [refs[j : j + 2] for j in range(0, 8, 2)], refs[-1]
    width = pairs[0][0].shape[1]

    @pl.loop(0, BLOCK // TILE)
    def _(part):
        i = pl.program_id(0) * (BLOCK // TILE) + part
        here = pl.ds(pl.multiple_of(part * TILE, TILE), TILE)

        def add(e, kept):
            total = 0.0
            for k, pair in enumerate(pairs):
                weight = jnp.concatenate([pair[0][e], pair[1][e]], axis=1)
                rows_ref, at = (near_ref, far_ref)[k // 2], k % 2 * LANES
                rows = rows_ref[here, at : at + width]
                total += dot(rows, weight, ((1,), (0,)))
            return jnp.where(mine_of(base, e, i * TILE), total, kept)

        out[here, :] = lax.fori_loop(
            low[i], high[i], add, jnp.zeros((TILE, out.shape[1]), F32)
        ).astype(BF16)


def partial_sums(f, spans, base, quarter, near, far, w_gate, w_up, pieces):
    rows = near.shape[0]
    experts, width, _ = w_gate.shape
    own = pl.BlockSpec((experts, width, UNITS), lambda i, lo, hi, b, q: (0, 0, 2 * q[0] + f))
    block = pl.BlockSpec((experts, width, UNITS), lambda i, *_: (0, 0, 0))
    return pl.pallas_call(
        partial_kernel,
        grid_spec=pltpu.PrefetchScalarGridSpec(
            num_scalar_prefetch=4,
            grid=(rows // BLOCK,),
            in_specs=[pl.BlockSpec((BLOCK, 2 * LANES), lambda i, *_: (i, 0))] * 2 + [own] * 2
            + [block] * len(pieces),
            out_specs=pl.BlockSpec((BLOCK, 2 * UNITS), lambda i, *_: (i, 0)),
        ),
        out_shape=jax.ShapeDtypeStruct((rows, 2 * UNITS), BF16),
        compiler_params=params(),
        cost_estimate=cost(16 * rows * LANES * UNITS, 8 * rows * LANES),
        name="partial_sums",
    )(*spans, base, quarter, near, far, w_gate, w_up, *pieces)


def down_kernel(low, high, base, block, onehot_ref, up_ref, down_ref, start, *refs):
    weights, (out, total_ref, value_ref) = refs[:-3], refs[-3:]
    width = weights[0].shape[1]
    j = pl.program_id(0)

    @pl.when(j == 0)
    def _():
        total_ref[...] = jnp.zeros_like(total_ref) if start is None else start[...]
        value_ref[...] = jnp.zeros_like(value_ref)

    @pl.when(block[2] != 0)
    def _():
        for part in range(BLOCK // TILE):
            i = (2 * block[0] + j) * (BLOCK // TILE) + part
            here = slice(part * TILE, (part + 1) * TILE)
            units = jnp.where(block[1] != 0, up_ref[here, :], down_ref[here, :])

            @pl.loop(low[i], high[i])
            def _(e):
                mine = mine_of(base, e, i * TILE)
                for k, weight in enumerate(weights):
                    value = dot(units, weight[e], ((1,), (1,)))
                    at = slice(k * LANES, k * LANES + width)
                    value_ref[here, at] = jnp.where(
                        mine, value, value_ref[here, at].astype(F32)
                    ).astype(BF16)

        total_ref[...] += dot(onehot_ref[...], value_ref[...], ((1,), (0,)))

    @pl.when(j == pl.num_programs(0) - 1)
    def _():
        out[...] = total_ref[...].astype(out.dtype)


def down_and_mix(spans, base, block, onehot, hidden, start, at, weights, dtype):
    rows, units = hidden[0].shape
    count, tokens = len(weights), onehot.shape[0]
    some = pl.BlockSpec((BLOCK, units), lambda j, *_: (j, 0))
    whole = pl.BlockSpec((tokens, count * LANES), lambda j, *_: (0, 0))
    kernel = down_kernel
    if start is None:
        kernel = lambda *refs: down_kernel(*refs[:7], None, *refs[7:])
    return pl.pallas_call(
        kernel,
        grid_spec=pltpu.PrefetchScalarGridSpec(
            num_scalar_prefetch=4,
            grid=(rows // BLOCK,),
            in_specs=[
                pl.BlockSpec((tokens, BLOCK), lambda j, lo, hi, b, k: (0, 2 * k[0] + j)),
                some,
                some,
            ]
            + [pl.BlockSpec((tokens, count * LANES), lambda j, *_: (0, at // count))]
            * (start is not None)
            + [pl.BlockSpec(w.shape, lambda j, *_: (0, 0, 0)) for w in weights],
            out_specs=whole,
            scratch_shapes=[
                pltpu.VMEM((tokens, count * LANES), F32),
                pltpu.VMEM((BLOCK, count * LANES), BF16),
            ],
        ),
        out_shape=jax.ShapeDtypeStruct((tokens, count * LANES), dtype),
        compiler_params=params(56),
        cost_estimate=cost(2 * rows * tokens * LANES * count, 2 * rows * tokens),
        name="down_and_mix",
    )(*spans, base, block, onehot, *hidden, *([] if start is None else [start]), *weights)


def fixed_weights(size, tokens, expert_ids, gate_weights, w_gate, w_up, w_down):
    count, picks = expert_ids.shape
    experts, width, hidden_units = w_gate.shape
    quarter = hidden_units // 4
    rows = size * count * picks
    places = size // 4
    me, plane = lax.axis_index("ep"), lax.axis_index("parts")
    w_down = jnp.swapaxes(w_down, 1, 2)

    twins = [(i, i ^ 1) for i in range(size)]
    cross = [(p * size + i, p * size + (i ^ 2 ^ p)) for p in range(2) for i in range(size)]
    to_twin = lambda value: lax.ppermute(value, "ep", twins)
    to_cross = lambda value: lax.ppermute(value, ("parts", "ep"), cross)
    to_plane = lambda value: lax.ppermute(value, "parts", [(0, 1), (1, 0)])
    line = [[4 * p + k for p in range(places)] for k in range(4)]
    my_quarter = me % 4
    twin_quarter = my_quarter ^ 1
    cross_quarter = my_quarter ^ 2 ^ plane

    note = jnp.concatenate([expert_ids.astype(F32), *split3(gate_weights)], axis=1).astype(BF16)
    fill = LANES - width - note.shape[1]
    parcels = jnp.concatenate(
        [
            tokens.reshape(count, size, width).swapaxes(0, 1),
            jnp.broadcast_to(jnp.pad(note, ((0, 0), (0, fill)))[None], (size, count, LANES - width)),
        ],
        axis=2,
    )
    own = lax.all_to_all(parcels, "ep", split_axis=0, concat_axis=0, tiled=True)
    own = own.reshape(size * count, LANES)
    far, near = to_cross(own), [own, to_twin(own)]
    place, across, gates, base = order_of(own, width, picks, experts)
    base = base[0, : experts + 1]
    spans = spans_of(base, rows)
    which = my_quarter.astype(jnp.int32).reshape(1)

    def cut(n, q):
        if n == 4:
            return lax.dynamic_slice_in_dim(w_down, q * quarter, quarter, 2)
        at = q * quarter + n // 2 * UNITS
        return lax.dynamic_slice_in_dim((w_gate, w_up)[n % 2], at, UNITS, 2)

    def after(value, *others):
        return lax.optimization_barrier((value, *others))[0]

    near_rows, scale, onehot = sort_rows(spans, base, across, gates, near, rows, experts)
    far = after(far, near_rows)
    far_rows = sort_more(onehot, [far, to_twin(far)])
    scale = lax.dynamic_slice_in_dim(scale, (me // 4) * (rows // places), rows // places, 0)

    crossed = [to_cross(cut(0, cross_quarter)), to_cross(after(cut(1, cross_quarter), near[1], base))]
    for n in range(2, 5):
        crossed.append(to_cross(after(cut(n, cross_quarter), far, *crossed[2:n])))
    twin_of = lambda n: to_twin(cut(n, twin_quarter))

    def sums_of(f, *first):
        rows_in = after(far_rows, *first)
        across_x = crossed[2 * f : 2 * f + 2]
        beside = [to_plane(after(across_x[0], near_rows))]
        beside.append(to_plane(after(across_x[1], *beside)))
        held = [twin_of(2 * f), twin_of(2 * f + 1), *across_x, *beside]
        return partial_sums(f, spans, base, which, near_rows, rows_in, w_gate, w_up, held)

    def units_of(sums):
        sums = lax.psum_scatter(
            sums, "ep", scatter_dimension=0, axis_index_groups=line, tiled=True
        ).astype(F32)
        return (jax.nn.silu(sums[:, :UNITS]) * sums[:, UNITS:] * scale).astype(BF16)

    sums = sums_of(0, crossed[2])
    later = sums_of(1, sums)
    units = [units_of(sums), units_of(later)]
    held = [twin_of(4), crossed[4], to_plane(crossed[4])]

    place = jnp.broadcast_to(
        after(across[:experts], later)[:, :, None], (experts, size * count, 128)
    )
    columns = scatter_rows(spans, place, rows)
    pieces = [after(cut(4, my_quarter), later), *held]
    units, columns, pieces = lax.optimization_barrier((units, columns, pieces))
    units = jnp.concatenate(units, axis=1)

    spot = me // 4

    def steps(value, step, up):
        links = [
            (4 * p + k, 4 * (p + 1 if up else p - 1) + k)
            for p in (range(step - 1, places - 1) if up else range(1, places - step + 1))
            for k in range(4)
        ]
        return lax.ppermute(value, "ep", links)

    def mix(flags, hidden, start, at=0, count=4, dtype=F32):
        block = jnp.stack([jnp.asarray(flag, jnp.int32) for flag in flags])
        return down_and_mix(
            spans, base, block, columns, hidden, start, at, pieces[at : at + count], dtype
        )

    moving = [steps(units, 1, True), steps(units, 1, False)]
    total, waiting = mix((spot, 1, 1), [units, units], None), []
    for step in range(1, places):
        if step == places - 1:
            for flags, hidden in waiting:
                total = mix(flags, hidden, total)
        *hidden, total = lax.optimization_barrier((*moving, total))
        came_up, came_down = spot >= step, spot < places - step
        above = jnp.minimum(spot + step, places - 1)
        flags = (jnp.where(came_up, spot - step, above), came_up, came_up | came_down)
        if step == places - 1:
            break
        moving = [steps(hidden[0], step + 1, True), steps(hidden[1], step + 1, False)]
        waiting.append((flags, hidden))
        if 2 * step < places:
            waiting.append(((above, 0, came_up & came_down), hidden))
        total = mix(*waiting.pop(0), total)
    far = mix(flags, hidden, total, 2, 2, BF16)
    near = after(total, far)
    far, far_twin = far[:, :width], far[:, LANES : LANES + width]
    far = (far.astype(F32) + to_twin(far_twin).astype(F32)).astype(BF16)
    near, far = lax.optimization_barrier((near, far))
    far = to_cross(far)
    near = mix(flags, hidden, near, 0, 2)
    twin = near[:, LANES : LANES + width].astype(BF16)
    twin = to_twin(after(twin, far)).astype(F32)
    mixed = (near[:, :width] + twin + far.astype(F32)).astype(BF16)
    mixed = lax.all_to_all(
        mixed.reshape(size, count, width), "ep", split_axis=0, concat_axis=0, tiled=True
    )
    return mixed.swapaxes(0, 1).reshape(count, size * width)


def solution(mesh):
    size, inner = mesh.shape["ep"], mesh.shape["tp"]

    def body(tokens, expert_ids, gate_weights, w_gate, w_up, w_down):
        rows = size * math.prod(expert_ids.shape)
        sums = rows * w_gate.shape[2]
        experts, width, units = w_gate.shape
        even = (
            size % 4 == 0
            and size > 4
            and mesh.shape["parts"] == 2
            and rows == size // 4 * 2 * BLOCK
            and units == 8 * UNITS
            and 3 * experts <= UNITS
            and size * math.prod(expert_ids.shape[:1]) % 128 == 0
            and width + 4 * expert_ids.shape[1] <= LANES
        )
        args = (tokens, expert_ids, gate_weights, w_gate, w_up, w_down)
        if inner == 1 and even and sums <= 3 * math.prod(w_gate.shape):
            return fixed_weights(size, *args)
        return moved_weights(*args)

    placed = (
        P(("parts", "ep"), "tp"),
        P(("parts", "ep"), None),
        P(("parts", "ep"), None),
        P(None, "ep", "tp"),
        P(None, "ep", "tp"),
        P(None, "tp", "ep"),
    )
    return jax.shard_map(
        body, mesh=mesh, in_specs=placed, out_specs=P(("parts", "ep"), "tp"), check_vma=False
    )
```

```python
import functools
import math

import jax
import jax.numpy as jnp
from jax import lax
from jax.experimental import pallas as pl
from jax.experimental.pallas import tpu as pltpu
from jax.sharding import PartitionSpec as P

BF16 = jnp.bfloat16
F32 = jnp.float32
TILE = 256
BLOCK = 1024
LANES = 256
UNITS = 128


def slots_of(block_ids, experts):
    flat = block_ids.reshape(-1)
    onehot = (flat[:, None] == jnp.arange(experts, dtype=jnp.int32)[None, :]).astype(jnp.int32)
    before = jnp.cumsum(onehot, axis=0) - onehot
    return jnp.sum(before * onehot, axis=1).reshape(block_ids.shape)


def fill_slots(rows, expert_ids, slot, experts, per_expert):
    count, picks = expert_ids.shape
    spread = jnp.broadcast_to(rows[:, None, :], (count, picks, rows.shape[1]))
    empty = jnp.zeros((experts, per_expert, rows.shape[1]), BF16)
    return empty.at[expert_ids, slot].set(spread)


def moved_weights(tokens, expert_ids, gate_weights, w_gate, w_up, w_down):
    tok_rows, picks = expert_ids.shape
    experts = w_gate.shape[0]
    per_expert = min(tok_rows, 3 * tok_rows * picks // (2 * experts))
    slot = slots_of(expert_ids, experts)
    features = lax.all_gather(tokens, "tp", axis=1, tiled=True)
    outgoing = fill_slots(features, expert_ids, slot, experts, per_expert)
    arrived = lax.all_to_all(outgoing, "ep", split_axis=0, concat_axis=1, tiled=True)
    gate_owned, up_owned = (
        lax.all_to_all(w_gate, "ep", split_axis=0, concat_axis=1, tiled=True),
        lax.all_to_all(w_up, "ep", split_axis=0, concat_axis=1, tiled=True),
    )
    gate = jnp.einsum("ecd,edf->ecf", arrived, gate_owned, preferred_element_type=F32)
    up = jnp.einsum("ecd,edf->ecf", arrived, up_owned, preferred_element_type=F32)
    hidden = (jax.nn.silu(gate) * up).astype(BF16)
    down_owned = lax.all_to_all(w_down, "ep", split_axis=0, concat_axis=2, tiled=True)
    partial_value = jnp.einsum("ecf,efd->ecd", hidden, down_owned, preferred_element_type=F32)
    expert_out = lax.psum_scatter(
        partial_value.astype(BF16), "tp", scatter_dimension=2, tiled=True
    )
    returned = lax.all_to_all(expert_out, "ep", split_axis=1, concat_axis=0, tiled=True)
    picked = returned[expert_ids, slot]
    mixed = jnp.sum(gate_weights[:, :, None] * picked.astype(F32), axis=1)
    return mixed.astype(BF16)


def dot(a, b, contract):
    return lax.dot_general(a, b, ((contract[0], contract[1]), ((), ())), preferred_element_type=F32)


def params(mib=48):
    return pltpu.CompilerParams(vmem_limit_bytes=mib << 20)


def cost(flops, moved):
    return pl.CostEstimate(flops=flops, bytes_accessed=moved, transcendentals=0)


def split3(value):
    high = lax.reduce_precision(value, 8, 7)
    middle = lax.reduce_precision(value - high, 8, 7)
    return high, middle, lax.reduce_precision(value - high - middle, 8, 7)


def order_kernel(width, picks, experts, note_ref, place_out, across_out, gates_out, base_out):
    tokens = note_ref.shape[0]
    note = note_ref[...].astype(F32)
    lane = lax.broadcasted_iota(jnp.int32, (tokens, UNITS), 1)
    name = jnp.where(lane < 3 * experts, lane % experts, -1).astype(F32)
    gates = jnp.zeros((tokens, UNITS), F32)
    for k in range(picks):
        one = note[:, width + k : width + k + 1]
        weight = (
            note[:, width + picks + k : width + picks + k + 1]
            + note[:, width + 2 * picks + k : width + 2 * picks + k + 1]
            + note[:, width + 3 * picks + k : width + 3 * picks + k + 1]
        )
        gates = jnp.where(name == one, weight, gates)
    mask = jnp.where((gates != 0.0) & (lane < experts), 1.0, 0.0)
    high = gates.astype(BF16)
    middle = (gates - high.astype(F32)).astype(BF16)
    rest = (gates - high.astype(F32) - middle.astype(F32)).astype(BF16)
    gates_out[...] = jnp.where(
        lane < experts,
        high.astype(F32),
        jnp.where(lane < 2 * experts, middle.astype(F32), rest.astype(F32)),
    ).astype(BF16)
    row = lax.broadcasted_iota(jnp.int32, (tokens, tokens), 0)
    column = lax.broadcasted_iota(jnp.int32, (tokens, tokens), 1)
    upto = jnp.where(column <= row, 1.0, 0.0).astype(BF16)
    count = dot(upto, mask.astype(BF16), ((1,), (0,)))
    total = jnp.broadcast_to(count[tokens - 1 : tokens, :], (8, UNITS))
    large = jnp.floor(total * (1.0 / 128.0))
    row = lax.broadcasted_iota(jnp.int32, (UNITS, UNITS), 0)
    column = lax.broadcasted_iota(jnp.int32, (UNITS, UNITS), 1)
    before = jnp.where(row < column, 1.0, 0.0).astype(BF16)
    base = 128.0 * dot(large.astype(BF16), before, ((1,), (0,)))
    base += dot((total - 128.0 * large).astype(BF16), before, ((1,), (0,)))
    base_out[...] = base.astype(jnp.int32)
    place = jnp.where(mask > 0.0, count - 1.0 + base[0:1, :], -1.0)
    place_out[...] = place.astype(jnp.int32)
    across_out[...] = place.T.astype(jnp.int32)


def order_of(note, width, picks, experts):
    tokens = note.shape[0]
    return pl.pallas_call(
        functools.partial(order_kernel, width, picks, experts),
        out_shape=[
            jax.ShapeDtypeStruct((tokens, UNITS), jnp.int32),
            jax.ShapeDtypeStruct((UNITS, tokens), jnp.int32),
            jax.ShapeDtypeStruct((tokens, UNITS), BF16),
            jax.ShapeDtypeStruct((8, UNITS), jnp.int32),
        ],
        compiler_params=params(),
        cost_estimate=cost(2 * tokens * tokens * UNITS, 4 * tokens * tokens),
        name="order",
    )(note)


def spans_of(base, rows):
    low = jnp.arange(rows // TILE, dtype=jnp.int32)[:, None] * TILE
    return (
        jnp.sum((base[None, 1:] <= low).astype(jnp.int32), axis=1),
        jnp.sum((base[None, :-1] < low + TILE).astype(jnp.int32), axis=1),
    )


def mine_of(base, e, row0):
    row = row0 + lax.broadcasted_iota(jnp.int32, (TILE, 1), 0)
    return (row >= base[e]) & (row < base[e + 1])


def sort_kernel(experts, first, low, high, base, across_ref, gates_ref, *refs):
    slices, (out, scale_out, onehot_ref, name_ref) = refs[:-4], refs[-4:]
    tokens = onehot_ref.shape[1]
    number = lax.broadcasted_iota(jnp.int32, (TILE, 128), 0).astype(F32).astype(BF16)
    onehot_ref[...] = jnp.zeros_like(onehot_ref)

    @pl.loop(0, BLOCK // TILE)
    def _(part):
        i = (first + pl.program_id(0)) * (BLOCK // TILE) + part
        row0 = i * TILE
        here = pl.ds(pl.multiple_of(part * TILE, TILE), TILE)

        @pl.loop(low[i], high[i])
        def _(e):
            away = across_ref[e] - row0
            away = jnp.where((away >= 0) & (away < TILE), away, -1).astype(F32)
            for c in range(tokens // 128):
                at = slice(c * 128, (c + 1) * 128)
                hit = number == away[c : c + 1, :].astype(BF16)
                onehot_ref[here, at] = jnp.where(hit, jnp.ones((), BF16), onehot_ref[here, at])
            name_ref[here, :] = jnp.where(mine_of(base, e, row0), e, name_ref[here, :])

    onehot = onehot_ref[...]
    for k, ref in enumerate(slices):
        out[:, k * LANES : (k + 1) * LANES] = dot(onehot, ref[...], ((1,), (0,))).astype(BF16)
    gates = dot(onehot, gates_ref[...], ((1,), (0,)))
    lane = lax.broadcasted_iota(jnp.int32, (BLOCK, UNITS), 1)
    name = name_ref[...]
    kept = (lane == name) | (lane == name + experts) | (lane == name + 2 * experts)
    scale = jnp.sum(jnp.where(kept, gates, 0.0), axis=1, keepdims=True)
    scale_out[...] = jnp.broadcast_to(scale, lane.shape)


def sort_rows(spans, base, across, gates, slices, rows, experts, begun=()):
    first = rows // BLOCK // 2 * bool(begun)
    kernel = functools.partial(sort_kernel, experts, first)
    if begun:
        kernel = lambda *refs: sort_kernel(experts, first, *refs[:-7], *refs[-4:])
    tokens = gates.shape[0]
    across = across[:experts].reshape(experts, tokens // 128, 128)
    whole = lambda i, *_: (0, 0)
    width = len(slices) * LANES
    return pl.pallas_call(
        kernel,
        grid_spec=pltpu.PrefetchScalarGridSpec(
            num_scalar_prefetch=3,
            grid=(rows // BLOCK // 2,),
            in_specs=[
                pl.BlockSpec(across.shape, lambda i, *_: (0, 0, 0)),
                pl.BlockSpec((tokens, UNITS), whole),
            ]
            + [pl.BlockSpec((tokens, LANES), whole)] * len(slices)
            + [pl.BlockSpec(memory_space=pl.ANY)] * len(begun),
            out_specs=[
                pl.BlockSpec((BLOCK, width), lambda i, *_: (first + i, 0)),
                pl.BlockSpec((BLOCK, UNITS), lambda i, *_: (first + i, 0)),
                pl.BlockSpec((BLOCK, tokens), lambda i, *_: (first + i, 0)),
            ],
            scratch_shapes=[pltpu.VMEM((BLOCK, UNITS), jnp.int32)],
        ),
        out_shape=[
            jax.ShapeDtypeStruct((rows, width), BF16),
            jax.ShapeDtypeStruct((rows, UNITS), F32),
            jax.ShapeDtypeStruct((rows, tokens), BF16),
        ],
        input_output_aliases={5 + len(slices) + k: k for k in range(len(begun))},
        compiler_params=params(),
        cost_estimate=cost(rows * tokens * width, 4 * rows * width),
        name="sort_rows",
    )(*spans, base, across, gates, *slices, *begun)


def sort_more_kernel(onehot_ref, *refs):
    for k, ref in enumerate(refs[:-1]):
        at = slice(k * LANES, (k + 1) * LANES)
        refs[-1][:, at] = dot(onehot_ref[...], ref[...], ((1,), (0,))).astype(BF16)


def sort_more(onehot, slices):
    rows, tokens = onehot.shape
    width = len(slices) * LANES
    return pl.pallas_call(
        sort_more_kernel,
        grid=(rows // BLOCK,),
        in_specs=[pl.BlockSpec((BLOCK, tokens), lambda i: (i, 0))]
        + [pl.BlockSpec((tokens, LANES), lambda i: (0, 0))] * len(slices),
        out_specs=pl.BlockSpec((BLOCK, width), lambda i: (i, 0)),
        out_shape=jax.ShapeDtypeStruct((rows, width), BF16),
        compiler_params=params(),
        cost_estimate=cost(2 * rows * tokens * width, 8 * rows * width),
        name="sort_more",
    )(onehot, *slices)


def scatter_kernel(low, high, place_ref, onehot_ref):
    tokens = place_ref.shape[1]
    lane = lax.broadcasted_iota(jnp.int32, (tokens, 128), 1)
    onehot_ref[...] = jnp.zeros_like(onehot_ref)
    for part in range(BLOCK // TILE):
        i = pl.program_id(0) * (BLOCK // TILE) + part

        @pl.loop(low[i], high[i])
        def _(e):
            place = place_ref[e] - i * TILE
            for c in range(TILE // 128):
                at = slice(part * TILE + c * 128, part * TILE + (c + 1) * 128)
                onehot_ref[:, at] += jnp.where(place == lane + c * 128, 1.0, 0.0).astype(BF16)


def scatter_rows(spans, place, rows):
    tokens = place.shape[1]
    return pl.pallas_call(
        scatter_kernel,
        grid_spec=pltpu.PrefetchScalarGridSpec(
            num_scalar_prefetch=2,
            grid=(rows // BLOCK,),
            in_specs=[pl.BlockSpec(place.shape, lambda i, *_: (0, 0, 0))],
            out_specs=pl.BlockSpec((tokens, BLOCK), lambda i, *_: (0, i)),
        ),
        out_shape=jax.ShapeDtypeStruct((tokens, rows), BF16),
        compiler_params=params(),
        cost_estimate=cost(rows * tokens, 2 * rows * tokens),
        name="scatter_rows",
    )(*spans, place)


def partial_kernel(low, high, base, quarter, near_ref, far_ref, *refs):
    pairs, out = [refs[j : j + 2] for j in range(0, 8, 2)], refs[-1]
    width = pairs[0][0].shape[1]

    @pl.loop(0, BLOCK // TILE)
    def _(part):
        i = pl.program_id(0) * (BLOCK // TILE) + part
        here = pl.ds(pl.multiple_of(part * TILE, TILE), TILE)

        def add(e, kept):
            total = 0.0
            for k, pair in enumerate(pairs):
                weight = jnp.concatenate([pair[0][e], pair[1][e]], axis=1)
                rows_ref, at = (near_ref, far_ref)[k // 2], k % 2 * LANES
                rows = rows_ref[here, at : at + width]
                total += dot(rows, weight, ((1,), (0,)))
            return jnp.where(mine_of(base, e, i * TILE), total, kept)

        out[here, :] = lax.fori_loop(
            low[i], high[i], add, jnp.zeros((TILE, out.shape[1]), F32)
        ).astype(BF16)


def partial_sums(f, spans, base, quarter, near, far, w_gate, w_up, pieces):
    rows = near.shape[0]
    experts, width, _ = w_gate.shape
    own = pl.BlockSpec((experts, width, UNITS), lambda i, lo, hi, b, q: (0, 0, 2 * q[0] + f))
    block = pl.BlockSpec((experts, width, UNITS), lambda i, *_: (0, 0, 0))
    return pl.pallas_call(
        partial_kernel,
        grid_spec=pltpu.PrefetchScalarGridSpec(
            num_scalar_prefetch=4,
            grid=(rows // BLOCK,),
            in_specs=[pl.BlockSpec((BLOCK, 2 * LANES), lambda i, *_: (i, 0))] * 2 + [own] * 2
            + [block] * len(pieces),
            out_specs=pl.BlockSpec((BLOCK, 2 * UNITS), lambda i, *_: (i, 0)),
        ),
        out_shape=jax.ShapeDtypeStruct((rows, 2 * UNITS), BF16),
        compiler_params=params(),
        cost_estimate=cost(16 * rows * LANES * UNITS, 8 * rows * LANES),
        name="partial_sums",
    )(*spans, base, quarter, near, far, w_gate, w_up, *pieces)


def down_kernel(slots, low, high, base, block, onehot_ref, *refs):
    hidden, start, refs = refs[: 2 * slots], refs[2 * slots], refs[2 * slots + 1 :]
    weights, (out, total_ref, value_ref) = refs[:-3], refs[-3:]
    width = weights[0].shape[1]
    j = pl.program_id(0)
    slot = j // 2

    @pl.when(j == 0)
    def _():
        total_ref[...] = jnp.zeros_like(total_ref) if start is None else start[...]
        value_ref[...] = jnp.zeros_like(value_ref)

    @pl.when(block[3 * slot + 2] != 0)
    def _():
        for part in range(BLOCK // TILE):
            i = (2 * block[3 * slot] + j % 2) * (BLOCK // TILE) + part
            here = slice(part * TILE, (part + 1) * TILE)
            source = 2 * slot + 1 - block[3 * slot + 1]
            units = hidden[0][here, :]
            for k in range(1, 2 * slots):
                units = jnp.where(source == k, hidden[k][here, :], units)

            @pl.loop(low[i], high[i])
            def _(e):
                mine = mine_of(base, e, i * TILE)
                for k, weight in enumerate(weights):
                    value = dot(units, weight[e], ((1,), (1,)))
                    at = slice(k * LANES, k * LANES + width)
                    value_ref[here, at] = jnp.where(
                        mine, value, value_ref[here, at].astype(F32)
                    ).astype(BF16)

        total_ref[...] += dot(onehot_ref[...], value_ref[...], ((1,), (0,)))

    @pl.when(j == pl.num_programs(0) - 1)
    def _():
        out[...] = total_ref[...].astype(out.dtype)


def down_and_mix(spans, base, block, onehot, hidden, start, at, weights, dtype):
    rows, units = hidden[0].shape
    slots = len(hidden) // 2
    count, tokens = len(weights), onehot.shape[0]
    some = [
        pl.BlockSpec((BLOCK, units), lambda j, *_, s=k // 2: (jnp.clip(j - 2 * s, 0, 1), 0))
        for k in range(2 * slots)
    ]
    whole = pl.BlockSpec((tokens, count * LANES), lambda j, *_: (0, 0))
    kernel = functools.partial(down_kernel, slots)
    if start is None:
        kernel = lambda *refs: down_kernel(slots, *refs[: 5 + 2 * slots], None, *refs[5 + 2 * slots :])
    return pl.pallas_call(
        kernel,
        grid_spec=pltpu.PrefetchScalarGridSpec(
            num_scalar_prefetch=4,
            grid=(2 * slots,),
            in_specs=[
                pl.BlockSpec(
                    (tokens, BLOCK), lambda j, lo, hi, b, k: (0, 2 * k[3 * (j // 2)] + j % 2)
                )
            ]
            + some
            + [pl.BlockSpec((tokens, count * LANES), lambda j, *_: (0, at // count))]
            * (start is not None)
            + [pl.BlockSpec(w.shape, lambda j, *_: (0, 0, 0)) for w in weights],
            out_specs=whole,
            scratch_shapes=[
                pltpu.VMEM((tokens, count * LANES), F32),
                pltpu.VMEM((BLOCK, count * LANES), BF16),
            ],
        ),
        out_shape=jax.ShapeDtypeStruct((tokens, count * LANES), dtype),
        compiler_params=params(56),
        cost_estimate=cost(2 * slots * rows * tokens * LANES * count, 2 * slots * rows * tokens),
        name="down_and_mix",
    )(*spans, base, block, onehot, *hidden, *([] if start is None else [start]), *weights)


def fixed_weights(size, tokens, expert_ids, gate_weights, w_gate, w_up, w_down):
    count, picks = expert_ids.shape
    experts, width, hidden_units = w_gate.shape
    quarter = hidden_units // 4
    rows = size * count * picks
    places = size // 4
    me, plane = lax.axis_index("ep"), lax.axis_index("parts")
    w_down = jnp.swapaxes(w_down, 1, 2)

    twins = [(i, i ^ 1) for i in range(size)]
    cross = [(p * size + i, p * size + (i ^ 2 ^ p)) for p in range(2) for i in range(size)]
    to_twin = lambda value: lax.ppermute(value, "ep", twins)
    to_cross = lambda value: lax.ppermute(value, ("parts", "ep"), cross)
    to_plane = lambda value: lax.ppermute(value, "parts", [(0, 1), (1, 0)])
    line = [[4 * p + k for p in range(places)] for k in range(4)]
    my_quarter = me % 4
    twin_quarter = my_quarter ^ 1
    cross_quarter = my_quarter ^ 2 ^ plane

    note = jnp.concatenate([expert_ids.astype(F32), *split3(gate_weights)], axis=1).astype(BF16)
    fill = LANES - width - note.shape[1]
    parcels = jnp.concatenate(
        [
            tokens.reshape(count, size, width).swapaxes(0, 1),
            jnp.broadcast_to(jnp.pad(note, ((0, 0), (0, fill)))[None], (size, count, LANES - width)),
        ],
        axis=2,
    )
    own = lax.all_to_all(parcels, "ep", split_axis=0, concat_axis=0, tiled=True)
    own = own.reshape(size * count, LANES)
    far, near = to_cross(own), [own, to_twin(own)]
    place, across, gates, base = order_of(own, width, picks, experts)
    base = base[0, : experts + 1]
    spans = spans_of(base, rows)
    which = my_quarter.astype(jnp.int32).reshape(1)

    def cut(n, q):
        if n == 4:
            return lax.dynamic_slice_in_dim(w_down, q * quarter, quarter, 2)
        at = q * quarter + n // 2 * UNITS
        return lax.dynamic_slice_in_dim((w_gate, w_up)[n % 2], at, UNITS, 2)

    def after(value, *others):
        return lax.optimization_barrier((value, *others))[0]

    crossed = [to_cross(cut(0, cross_quarter)), to_cross(after(cut(1, cross_quarter), near[1], base))]
    begun = sort_rows(spans, base, across, gates, near, rows, experts)
    beside = [to_plane(after(crossed[0], begun[0]))]
    rest = after(gates, crossed[0])
    near_rows, scale, onehot = sort_rows(spans, base, across, rest, near, rows, experts, begun)
    far = after(far, near_rows)
    far_rows = sort_more(onehot, [far, to_twin(far)])
    scale = lax.dynamic_slice_in_dim(scale, (me // 4) * (rows // places), rows // places, 0)

    for n in range(2, 5):
        crossed.append(to_cross(after(cut(n, cross_quarter), far, *crossed[2:n])))
    twin_of = lambda n: to_twin(cut(n, twin_quarter))

    for n in range(1, 4):
        beside.append(to_plane(after(crossed[n], near_rows, beside[n - 1])))

    def sums_of(f, *first):
        rows_in = after(far_rows, *first)
        pair = slice(2 * f, 2 * f + 2)
        held = [twin_of(2 * f), twin_of(2 * f + 1), *crossed[pair], *beside[pair]]
        return partial_sums(f, spans, base, which, near_rows, rows_in, w_gate, w_up, held)

    def units_of(sums):
        sums = lax.psum_scatter(
            sums, "ep", scatter_dimension=0, axis_index_groups=line, tiled=True
        )
        gate, up = sums[:, :UNITS].astype(F32), sums[:, UNITS:].astype(F32)
        return (jax.nn.silu(gate) * up * scale).astype(BF16)

    sums = sums_of(0, crossed[2])
    later = sums_of(1, sums)
    units = [units_of(sums), units_of(later)]
    held = [twin_of(4), crossed[4], to_plane(crossed[4])]

    place = jnp.broadcast_to(
        after(across[:experts], later)[:, :, None], (experts, size * count, 128)
    )
    columns = scatter_rows(spans, place, rows)
    pieces = [after(cut(4, my_quarter), later), *held]
    units, columns, pieces = lax.optimization_barrier((units, columns, pieces))
    units = jnp.concatenate(units, axis=1)

    spot = me // 4

    def steps(value, step, up):
        links = [
            (4 * p + k, 4 * (p + 1 if up else p - 1) + k)
            for p in (range(step - 1, places - 1) if up else range(1, places - step + 1))
            for k in range(4)
        ]
        return lax.ppermute(value, "ep", links)

    def mix(flags, hidden, start, at=0, count=4, dtype=F32):
        block = jnp.stack([jnp.asarray(flag, jnp.int32) for flag in flags])
        hidden = list(hidden)
        return down_and_mix(
            spans, base, block, columns, hidden, start, at, pieces[at : at + count], dtype
        )

    moving = [steps(units, 1, True), steps(units, 1, False)]
    total, waiting = mix((spot, 1, 1), [units, units], None), []
    for step in range(1, places):
        if step == places - 1:
            if waiting:
                both = [sum(map(tuple, parts), ()) for parts in zip(*waiting)]
                total = mix(*both, total)
        *hidden, total = lax.optimization_barrier((*moving, total))
        came_up, came_down = spot >= step, spot < places - step
        above = jnp.minimum(spot + step, places - 1)
        flags = (jnp.where(came_up, spot - step, above), came_up, came_up | came_down)
        if step == places - 1:
            break
        moving = [steps(hidden[0], step + 1, True), steps(hidden[1], step + 1, False)]
        waiting.append((flags, hidden))
        if 2 * step < places:
            waiting.append(((above, 0, came_up & came_down), hidden))
        if step == 1:
            total = mix(*waiting.pop(0), total)
    far = mix(flags, hidden, total, 2, 2, BF16)
    near = after(total, far)
    far, far_twin = far[:, :width], far[:, LANES : LANES + width]
    far = (far.astype(F32) + to_twin(far_twin).astype(F32)).astype(BF16)
    near, far = lax.optimization_barrier((near, far))
    far = to_cross(far)
    near = mix(flags, hidden, near, 0, 2)
    twin = near[:, LANES : LANES + width].astype(BF16)
    twin = to_twin(after(twin, far)).astype(F32)
    mixed = (near[:, :width] + twin + far.astype(F32)).astype(BF16)
    mixed = lax.all_to_all(
        mixed.reshape(size, count, width), "ep", split_axis=0, concat_axis=0, tiled=True
    )
    return mixed.swapaxes(0, 1).reshape(count, size * width)


def solution(mesh):
    size, inner = mesh.shape["ep"], mesh.shape["tp"]

    def body(tokens, expert_ids, gate_weights, w_gate, w_up, w_down):
        rows = size * math.prod(expert_ids.shape)
        sums = rows * w_gate.shape[2]
        experts, width, units = w_gate.shape
        even = (
            size % 4 == 0
            and size > 4
            and mesh.shape["parts"] == 2
            and rows == size // 4 * 2 * BLOCK
            and units == 8 * UNITS
            and 3 * experts <= UNITS
            and size * math.prod(expert_ids.shape[:1]) % 128 == 0
            and width + 4 * expert_ids.shape[1] <= LANES
        )
        args = (tokens, expert_ids, gate_weights, w_gate, w_up, w_down)
        if inner == 1 and even and sums <= 3 * math.prod(w_gate.shape):
            return fixed_weights(size, *args)
        return moved_weights(*args)

    placed = (
        P(("parts", "ep"), "tp"),
        P(("parts", "ep"), None),
        P(("parts", "ep"), None),
        P(None, "ep", "tp"),
        P(None, "ep", "tp"),
        P(None, "tp", "ep"),
    )
    return jax.shard_map(
        body, mesh=mesh, in_specs=placed, out_specs=P(("parts", "ep"), "tp"), check_vma=False
    )
```

```python
import functools
import math

import jax
import jax.numpy as jnp
from jax import lax
from jax.experimental import pallas as pl
from jax.experimental.pallas import tpu as pltpu
from jax.sharding import PartitionSpec as P

BF16 = jnp.bfloat16
F32 = jnp.float32
TILE = 256
STEP = 512
BLOCK = 1024
LANES = 256
UNITS = 128


def slots_of(block_ids, experts):
    flat = block_ids.reshape(-1)
    onehot = (flat[:, None] == jnp.arange(experts, dtype=jnp.int32)[None, :]).astype(jnp.int32)
    before = jnp.cumsum(onehot, axis=0) - onehot
    return jnp.sum(before * onehot, axis=1).reshape(block_ids.shape)


def fill_slots(rows, expert_ids, slot, experts, per_expert):
    count, picks = expert_ids.shape
    spread = jnp.broadcast_to(rows[:, None, :], (count, picks, rows.shape[1]))
    empty = jnp.zeros((experts, per_expert, rows.shape[1]), BF16)
    return empty.at[expert_ids, slot].set(spread)


def moved_weights(tokens, expert_ids, gate_weights, w_gate, w_up, w_down):
    tok_rows, picks = expert_ids.shape
    experts = w_gate.shape[0]
    per_expert = min(tok_rows, 3 * tok_rows * picks // (2 * experts))
    slot = slots_of(expert_ids, experts)
    features = lax.all_gather(tokens, "tp", axis=1, tiled=True)
    outgoing = fill_slots(features, expert_ids, slot, experts, per_expert)
    arrived = lax.all_to_all(outgoing, "ep", split_axis=0, concat_axis=1, tiled=True)
    gate_owned, up_owned = (
        lax.all_to_all(w_gate, "ep", split_axis=0, concat_axis=1, tiled=True),
        lax.all_to_all(w_up, "ep", split_axis=0, concat_axis=1, tiled=True),
    )
    gate = jnp.einsum("ecd,edf->ecf", arrived, gate_owned, preferred_element_type=F32)
    up = jnp.einsum("ecd,edf->ecf", arrived, up_owned, preferred_element_type=F32)
    hidden = (jax.nn.silu(gate) * up).astype(BF16)
    down_owned = lax.all_to_all(w_down, "ep", split_axis=0, concat_axis=2, tiled=True)
    partial_value = jnp.einsum("ecf,efd->ecd", hidden, down_owned, preferred_element_type=F32)
    expert_out = lax.psum_scatter(
        partial_value.astype(BF16), "tp", scatter_dimension=2, tiled=True
    )
    returned = lax.all_to_all(expert_out, "ep", split_axis=1, concat_axis=0, tiled=True)
    picked = returned[expert_ids, slot]
    mixed = jnp.sum(gate_weights[:, :, None] * picked.astype(F32), axis=1)
    return mixed.astype(BF16)


def dot(a, b, contract):
    return lax.dot_general(a, b, ((contract[0], contract[1]), ((), ())), preferred_element_type=F32)


def params(mib=48):
    return pltpu.CompilerParams(vmem_limit_bytes=mib << 20)


def cost(flops, moved):
    return pl.CostEstimate(flops=flops, bytes_accessed=moved, transcendentals=0)


def split3(value):
    high = lax.reduce_precision(value, 8, 7)
    middle = lax.reduce_precision(value - high, 8, 7)
    return high, middle, lax.reduce_precision(value - high - middle, 8, 7)


def order_kernel(width, picks, experts, note_ref, place_out, across_out, gates_out, base_out):
    tokens = note_ref.shape[0]
    note = note_ref[...].astype(F32)
    lane = lax.broadcasted_iota(jnp.int32, (tokens, UNITS), 1)
    name = jnp.where(lane < 3 * experts, lane % experts, -1).astype(F32)
    gates = jnp.zeros((tokens, UNITS), F32)
    for k in range(picks):
        one = note[:, width + k : width + k + 1]
        weight = (
            note[:, width + picks + k : width + picks + k + 1]
            + note[:, width + 2 * picks + k : width + 2 * picks + k + 1]
            + note[:, width + 3 * picks + k : width + 3 * picks + k + 1]
        )
        gates = jnp.where(name == one, weight, gates)
    mask = jnp.where((gates != 0.0) & (lane < experts), 1.0, 0.0)
    high = gates.astype(BF16)
    middle = (gates - high.astype(F32)).astype(BF16)
    rest = (gates - high.astype(F32) - middle.astype(F32)).astype(BF16)
    gates_out[...] = jnp.where(
        lane < experts,
        high.astype(F32),
        jnp.where(lane < 2 * experts, middle.astype(F32), rest.astype(F32)),
    ).astype(BF16)
    row = lax.broadcasted_iota(jnp.int32, (tokens, tokens), 0)
    column = lax.broadcasted_iota(jnp.int32, (tokens, tokens), 1)
    upto = jnp.where(column <= row, 1.0, 0.0).astype(BF16)
    count = dot(upto, mask.astype(BF16), ((1,), (0,)))
    total = jnp.broadcast_to(count[tokens - 1 : tokens, :], (8, UNITS))
    large = jnp.floor(total * (1.0 / 128.0))
    row = lax.broadcasted_iota(jnp.int32, (UNITS, UNITS), 0)
    column = lax.broadcasted_iota(jnp.int32, (UNITS, UNITS), 1)
    before = jnp.where(row < column, 1.0, 0.0).astype(BF16)
    base = 128.0 * dot(large.astype(BF16), before, ((1,), (0,)))
    base += dot((total - 128.0 * large).astype(BF16), before, ((1,), (0,)))
    base_out[...] = base.astype(jnp.int32)
    place = jnp.where(mask > 0.0, count - 1.0 + base[0:1, :], -1.0)
    place_out[...] = place.astype(jnp.int32)
    across_out[...] = place.T.astype(jnp.int32)


def order_of(note, width, picks, experts):
    tokens = note.shape[0]
    return pl.pallas_call(
        functools.partial(order_kernel, width, picks, experts),
        out_shape=[
            jax.ShapeDtypeStruct((tokens, UNITS), jnp.int32),
            jax.ShapeDtypeStruct((UNITS, tokens), jnp.int32),
            jax.ShapeDtypeStruct((tokens, UNITS), BF16),
            jax.ShapeDtypeStruct((8, UNITS), jnp.int32),
        ],
        compiler_params=params(),
        cost_estimate=cost(2 * tokens * tokens * UNITS, 4 * tokens * tokens),
        name="order",
    )(note)


def spans_of(base, rows):
    low = jnp.arange(rows // TILE, dtype=jnp.int32)[:, None] * TILE
    return (
        jnp.sum((base[None, 1:] <= low).astype(jnp.int32), axis=1),
        jnp.sum((base[None, :-1] < low + TILE).astype(jnp.int32), axis=1),
    )


def mine_of(base, e, row0, rows=TILE):
    row = row0 + lax.broadcasted_iota(jnp.int32, (rows, 1), 0)
    return (row >= base[e]) & (row < base[e + 1])


def sort_kernel(experts, first, low, high, base, across_ref, gates_ref, *refs):
    slices, (out, scale_out, onehot_ref, name_ref) = refs[:-4], refs[-4:]
    tokens = onehot_ref.shape[1]
    number = lax.broadcasted_iota(jnp.int32, (TILE, 128), 0).astype(F32).astype(BF16)
    onehot_ref[...] = jnp.zeros_like(onehot_ref)

    @pl.loop(0, BLOCK // TILE)
    def _(part):
        i = (first + pl.program_id(0)) * (BLOCK // TILE) + part
        row0 = i * TILE
        here = pl.ds(pl.multiple_of(part * TILE, TILE), TILE)

        @pl.loop(low[i], high[i])
        def _(e):
            away = across_ref[e] - row0
            away = jnp.where((away >= 0) & (away < TILE), away, -1).astype(F32)
            for c in range(tokens // 128):
                at = slice(c * 128, (c + 1) * 128)
                hit = number == away[c : c + 1, :].astype(BF16)
                onehot_ref[here, at] = jnp.where(hit, jnp.ones((), BF16), onehot_ref[here, at])
            name_ref[here, :] = jnp.where(mine_of(base, e, row0), e, name_ref[here, :])

    onehot = onehot_ref[...]
    for k, ref in enumerate(slices):
        out[:, k * LANES : (k + 1) * LANES] = dot(onehot, ref[...], ((1,), (0,))).astype(BF16)
    gates = dot(onehot, gates_ref[...], ((1,), (0,)))
    lane = lax.broadcasted_iota(jnp.int32, (BLOCK, UNITS), 1)
    name = name_ref[...]
    kept = (lane == name) | (lane == name + experts) | (lane == name + 2 * experts)
    scale = jnp.sum(jnp.where(kept, gates, 0.0), axis=1, keepdims=True)
    scale_out[...] = jnp.broadcast_to(scale, lane.shape)


def sort_rows(spans, base, across, gates, slices, rows, experts, begun=()):
    first = rows // BLOCK // 2 * bool(begun)
    kernel = functools.partial(sort_kernel, experts, first)
    if begun:
        kernel = lambda *refs: sort_kernel(experts, first, *refs[:-7], *refs[-4:])
    tokens = gates.shape[0]
    across = across[:experts].reshape(experts, tokens // 128, 128)
    whole = lambda i, *_: (0, 0)
    width = len(slices) * LANES
    return pl.pallas_call(
        kernel,
        grid_spec=pltpu.PrefetchScalarGridSpec(
            num_scalar_prefetch=3,
            grid=(rows // BLOCK // 2,),
            in_specs=[
                pl.BlockSpec(across.shape, lambda i, *_: (0, 0, 0)),
                pl.BlockSpec((tokens, UNITS), whole),
            ]
            + [pl.BlockSpec((tokens, LANES), whole)] * len(slices)
            + [pl.BlockSpec(memory_space=pl.ANY)] * len(begun),
            out_specs=[
                pl.BlockSpec((BLOCK, width), lambda i, *_: (first + i, 0)),
                pl.BlockSpec((BLOCK, UNITS), lambda i, *_: (first + i, 0)),
                pl.BlockSpec((BLOCK, tokens), lambda i, *_: (first + i, 0)),
            ],
            scratch_shapes=[pltpu.VMEM((BLOCK, UNITS), jnp.int32)],
        ),
        out_shape=[
            jax.ShapeDtypeStruct((rows, width), BF16),
            jax.ShapeDtypeStruct((rows, UNITS), F32),
            jax.ShapeDtypeStruct((rows, tokens), BF16),
        ],
        input_output_aliases={5 + len(slices) + k: k for k in range(len(begun))},
        compiler_params=params(),
        cost_estimate=cost(rows * tokens * width, 4 * rows * width),
        name="sort_rows",
    )(*spans, base, across, gates, *slices, *begun)


def sort_more_kernel(onehot_ref, *refs):
    for k, ref in enumerate(refs[:-1]):
        at = slice(k * LANES, (k + 1) * LANES)
        refs[-1][:, at] = dot(onehot_ref[...], ref[...], ((1,), (0,))).astype(BF16)


def sort_more(onehot, slices):
    rows, tokens = onehot.shape
    width = len(slices) * LANES
    return pl.pallas_call(
        sort_more_kernel,
        grid=(rows // BLOCK,),
        in_specs=[pl.BlockSpec((BLOCK, tokens), lambda i: (i, 0))]
        + [pl.BlockSpec((tokens, LANES), lambda i: (0, 0))] * len(slices),
        out_specs=pl.BlockSpec((BLOCK, width), lambda i: (i, 0)),
        out_shape=jax.ShapeDtypeStruct((rows, width), BF16),
        compiler_params=params(),
        cost_estimate=cost(2 * rows * tokens * width, 8 * rows * width),
        name="sort_more",
    )(onehot, *slices)


def scatter_kernel(low, high, place_ref, onehot_ref):
    tokens = place_ref.shape[1]
    lane = lax.broadcasted_iota(jnp.int32, (tokens, 128), 1)
    onehot_ref[...] = jnp.zeros_like(onehot_ref)
    for part in range(BLOCK // TILE):
        i = pl.program_id(0) * (BLOCK // TILE) + part

        @pl.loop(low[i], high[i])
        def _(e):
            place = place_ref[e] - i * TILE
            for c in range(TILE // 128):
                at = slice(part * TILE + c * 128, part * TILE + (c + 1) * 128)
                onehot_ref[:, at] += jnp.where(place == lane + c * 128, 1.0, 0.0).astype(BF16)


def scatter_rows(spans, place, rows):
    tokens = place.shape[1]
    return pl.pallas_call(
        scatter_kernel,
        grid_spec=pltpu.PrefetchScalarGridSpec(
            num_scalar_prefetch=2,
            grid=(rows // BLOCK,),
            in_specs=[pl.BlockSpec(place.shape, lambda i, *_: (0, 0, 0))],
            out_specs=pl.BlockSpec((tokens, BLOCK), lambda i, *_: (0, i)),
        ),
        out_shape=jax.ShapeDtypeStruct((tokens, rows), BF16),
        compiler_params=params(),
        cost_estimate=cost(rows * tokens, 2 * rows * tokens),
        name="scatter_rows",
    )(*spans, place)


def partial_kernel(low, high, base, quarter, near_ref, far_ref, *refs):
    pairs, out = [refs[j : j + 2] for j in range(0, 8, 2)], refs[-1]
    width = pairs[0][0].shape[1]

    @pl.loop(0, BLOCK // STEP)
    def _(part):
        i = pl.program_id(0) * (BLOCK // STEP) + part
        here = pl.ds(pl.multiple_of(part * STEP, STEP), STEP)

        def add(e, kept):
            total = 0.0
            for k, pair in enumerate(pairs):
                weight = jnp.concatenate([pair[0][e], pair[1][e]], axis=1)
                rows_ref, at = (near_ref, far_ref)[k // 2], k % 2 * LANES
                rows = rows_ref[here, at : at + width]
                total += dot(rows, weight, ((1,), (0,)))
            return jnp.where(mine_of(base, e, i * STEP, STEP), total, kept)

        out[here, :] = lax.fori_loop(
            low[STEP // TILE * i],
            high[STEP // TILE * (i + 1) - 1],
            add,
            jnp.zeros((STEP, out.shape[1]), F32),
        ).astype(BF16)


def partial_sums(f, spans, base, quarter, near, far, w_gate, w_up, pieces):
    rows = near.shape[0]
    experts, width, _ = w_gate.shape
    own = pl.BlockSpec((experts, width, UNITS), lambda i, lo, hi, b, q: (0, 0, 2 * q[0] + f))
    block = pl.BlockSpec((experts, width, UNITS), lambda i, *_: (0, 0, 0))
    return pl.pallas_call(
        partial_kernel,
        grid_spec=pltpu.PrefetchScalarGridSpec(
            num_scalar_prefetch=4,
            grid=(rows // BLOCK,),
            in_specs=[pl.BlockSpec((BLOCK, 2 * LANES), lambda i, *_: (i, 0))] * 2 + [own] * 2
            + [block] * len(pieces),
            out_specs=pl.BlockSpec((BLOCK, 2 * UNITS), lambda i, *_: (i, 0)),
        ),
        out_shape=jax.ShapeDtypeStruct((rows, 2 * UNITS), BF16),
        compiler_params=params(),
        cost_estimate=cost(16 * rows * LANES * UNITS, 8 * rows * LANES),
        name="partial_sums",
    )(*spans, base, quarter, near, far, w_gate, w_up, *pieces)


def down_kernel(slots, low, high, base, block, onehot_ref, *refs):
    hidden, start, refs = refs[: 2 * slots], refs[2 * slots], refs[2 * slots + 1 :]
    weights, (out, total_ref, value_ref) = refs[:-3], refs[-3:]
    width = weights[0].shape[1]
    j = pl.program_id(0)
    slot = j // 2

    @pl.when(j == 0)
    def _():
        total_ref[...] = jnp.zeros_like(total_ref) if start is None else start[...]
        value_ref[...] = jnp.zeros_like(value_ref)

    @pl.when(block[3 * slot + 2] != 0)
    def _():
        for part in range(BLOCK // STEP):
            i = (2 * block[3 * slot] + j % 2) * (BLOCK // STEP) + part
            here = slice(part * STEP, (part + 1) * STEP)
            source = 2 * slot + 1 - block[3 * slot + 1]
            units = hidden[0][here, :]
            for k in range(1, 2 * slots):
                units = jnp.where(source == k, hidden[k][here, :], units)

            @pl.loop(low[STEP // TILE * i], high[STEP // TILE * (i + 1) - 1])
            def _(e):
                mine = mine_of(base, e, i * STEP, STEP)
                for k, weight in enumerate(weights):
                    value = dot(units, weight[e], ((1,), (1,)))
                    at = slice(k * LANES, k * LANES + width)
                    value_ref[here, at] = jnp.where(
                        mine, value, value_ref[here, at].astype(F32)
                    ).astype(BF16)

        total_ref[...] += dot(onehot_ref[...], value_ref[...], ((1,), (0,)))

    @pl.when(j == pl.num_programs(0) - 1)
    def _():
        out[...] = total_ref[...].astype(out.dtype)


def down_and_mix(spans, base, block, onehot, hidden, start, at, weights, dtype):
    rows, units = hidden[0].shape
    slots = len(hidden) // 2
    count, tokens = len(weights), onehot.shape[0]
    some = [
        pl.BlockSpec((BLOCK, units), lambda j, *_, s=k // 2: (jnp.clip(j - 2 * s, 0, 1), 0))
        for k in range(2 * slots)
    ]
    whole = pl.BlockSpec((tokens, count * LANES), lambda j, *_: (0, 0))
    kernel = functools.partial(down_kernel, slots)
    if start is None:
        kernel = lambda *refs: down_kernel(slots, *refs[: 5 + 2 * slots], None, *refs[5 + 2 * slots :])
    return pl.pallas_call(
        kernel,
        grid_spec=pltpu.PrefetchScalarGridSpec(
            num_scalar_prefetch=4,
            grid=(2 * slots,),
            in_specs=[
                pl.BlockSpec(
                    (tokens, BLOCK), lambda j, lo, hi, b, k: (0, 2 * k[3 * (j // 2)] + j % 2)
                )
            ]
            + some
            + [pl.BlockSpec((tokens, count * LANES), lambda j, *_: (0, at // count))]
            * (start is not None)
            + [pl.BlockSpec(w.shape, lambda j, *_: (0, 0, 0)) for w in weights],
            out_specs=whole,
            scratch_shapes=[
                pltpu.VMEM((tokens, count * LANES), F32),
                pltpu.VMEM((BLOCK, count * LANES), BF16),
            ],
        ),
        out_shape=jax.ShapeDtypeStruct((tokens, count * LANES), dtype),
        compiler_params=params(56),
        cost_estimate=cost(2 * slots * rows * tokens * LANES * count, 2 * slots * rows * tokens),
        name="down_and_mix",
    )(*spans, base, block, onehot, *hidden, *([] if start is None else [start]), *weights)


def fixed_weights(size, tokens, expert_ids, gate_weights, w_gate, w_up, w_down):
    count, picks = expert_ids.shape
    experts, width, hidden_units = w_gate.shape
    quarter = hidden_units // 4
    rows = size * count * picks
    places = size // 4
    me, plane = lax.axis_index("ep"), lax.axis_index("parts")
    w_down = jnp.swapaxes(w_down, 1, 2)

    twins = [(i, i ^ 1) for i in range(size)]
    cross = [(p * size + i, p * size + (i ^ 2 ^ p)) for p in range(2) for i in range(size)]
    to_twin = lambda value: lax.ppermute(value, "ep", twins)
    to_cross = lambda value: lax.ppermute(value, ("parts", "ep"), cross)
    to_plane = lambda value: lax.ppermute(value, "parts", [(0, 1), (1, 0)])
    line = [[4 * p + k for p in range(places)] for k in range(4)]
    my_quarter = me % 4
    twin_quarter = my_quarter ^ 1
    cross_quarter = my_quarter ^ 2 ^ plane

    note = jnp.concatenate([expert_ids.astype(F32), *split3(gate_weights)], axis=1).astype(BF16)
    fill = LANES - width - note.shape[1]
    parcels = jnp.concatenate(
        [
            tokens.reshape(count, size, width).swapaxes(0, 1),
            jnp.broadcast_to(jnp.pad(note, ((0, 0), (0, fill)))[None], (size, count, LANES - width)),
        ],
        axis=2,
    )
    own = lax.all_to_all(parcels, "ep", split_axis=0, concat_axis=0, tiled=True)
    own = own.reshape(size * count, LANES)
    far, near = to_cross(own), [own, to_twin(own)]
    place, across, gates, base = order_of(own, width, picks, experts)
    base = base[0, : experts + 1]
    spans = spans_of(base, rows)
    which = my_quarter.astype(jnp.int32).reshape(1)

    def cut(n, q):
        if n == 4:
            return lax.dynamic_slice_in_dim(w_down, q * quarter, quarter, 2)
        at = q * quarter + n // 2 * UNITS
        return lax.dynamic_slice_in_dim((w_gate, w_up)[n % 2], at, UNITS, 2)

    def after(value, *others):
        return lax.optimization_barrier((value, *others))[0]

    crossed = [to_cross(cut(0, cross_quarter)), to_cross(after(cut(1, cross_quarter), near[1], base))]
    begun = sort_rows(spans, base, across, gates, near, rows, experts)
    beside = [to_plane(after(crossed[0], begun[0]))]
    rest = after(gates, crossed[0])
    near_rows, scale, onehot = sort_rows(spans, base, across, rest, near, rows, experts, begun)
    far = after(far, near_rows)
    far_rows = sort_more(onehot, [far, to_twin(far)])
    scale = lax.dynamic_slice_in_dim(scale, (me // 4) * (rows // places), rows // places, 0)

    for n in range(2, 5):
        crossed.append(to_cross(after(cut(n, cross_quarter), far, *crossed[2:n])))
    twin_of = lambda n: to_twin(cut(n, twin_quarter))

    for n in range(1, 4):
        beside.append(to_plane(after(crossed[n], near_rows, beside[n - 1])))

    def sums_of(f, *first):
        rows_in = after(far_rows, *first)
        pair = slice(2 * f, 2 * f + 2)
        held = [twin_of(2 * f), twin_of(2 * f + 1), *crossed[pair], *beside[pair]]
        return partial_sums(f, spans, base, which, near_rows, rows_in, w_gate, w_up, held)

    def units_of(sums):
        sums = lax.psum_scatter(
            sums, "ep", scatter_dimension=0, axis_index_groups=line, tiled=True
        )
        gate, up = sums[:, :UNITS].astype(F32), sums[:, UNITS:].astype(F32)
        return (jax.nn.silu(gate) * up * scale).astype(BF16)

    sums = sums_of(0, crossed[2])
    later = sums_of(1, sums)
    units = [units_of(sums), units_of(later)]
    held = [twin_of(4), crossed[4], to_plane(crossed[4])]

    place = jnp.broadcast_to(
        after(across[:experts], later)[:, :, None], (experts, size * count, 128)
    )
    columns = scatter_rows(spans, place, rows)
    pieces = [after(cut(4, my_quarter), later), *held]
    units, columns, pieces = lax.optimization_barrier((units, columns, pieces))
    units = jnp.concatenate(units, axis=1)

    spot = me // 4

    def steps(value, step, up):
        links = [
            (4 * p + k, 4 * (p + 1 if up else p - 1) + k)
            for p in (range(step - 1, places - 1) if up else range(1, places - step + 1))
            for k in range(4)
        ]
        return lax.ppermute(value, "ep", links)

    def mix(flags, hidden, start, at=0, count=4, dtype=F32):
        block = jnp.stack([jnp.asarray(flag, jnp.int32) for flag in flags])
        hidden = list(hidden)
        return down_and_mix(
            spans, base, block, columns, hidden, start, at, pieces[at : at + count], dtype
        )

    moving = [steps(units, 1, True), steps(units, 1, False)]
    total, waiting = mix((spot, 1, 1), [units, units], None), []
    for step in range(1, places):
        if step == places - 1:
            if waiting:
                both = [sum(map(tuple, parts), ()) for parts in zip(*waiting)]
                total = mix(*both, total)
        *hidden, total = lax.optimization_barrier((*moving, total))
        came_up, came_down = spot >= step, spot < places - step
        above = jnp.minimum(spot + step, places - 1)
        flags = (jnp.where(came_up, spot - step, above), came_up, came_up | came_down)
        if step == places - 1:
            break
        moving = [steps(hidden[0], step + 1, True), steps(hidden[1], step + 1, False)]
        waiting.append((flags, hidden))
        if 2 * step < places:
            waiting.append(((above, 0, came_up & came_down), hidden))
        if step == 1:
            total = mix(*waiting.pop(0), total)
    far = mix(flags, hidden, total, 2, 2, BF16)
    near = after(total, far)
    far, far_twin = far[:, :width], far[:, LANES : LANES + width]
    far = (far.astype(F32) + to_twin(far_twin).astype(F32)).astype(BF16)
    near, far = lax.optimization_barrier((near, far))
    far = to_cross(far)
    near = mix(flags, hidden, near, 0, 2)
    twin = near[:, LANES : LANES + width].astype(BF16)
    twin = to_twin(after(twin, far)).astype(F32)
    mixed = (near[:, :width] + twin + far.astype(F32)).astype(BF16)
    mixed = lax.all_to_all(
        mixed.reshape(size, count, width), "ep", split_axis=0, concat_axis=0, tiled=True
    )
    return mixed.swapaxes(0, 1).reshape(count, size * width)


def solution(mesh):
    size, inner = mesh.shape["ep"], mesh.shape["tp"]

    def body(tokens, expert_ids, gate_weights, w_gate, w_up, w_down):
        rows = size * math.prod(expert_ids.shape)
        sums = rows * w_gate.shape[2]
        experts, width, units = w_gate.shape
        even = (
            size % 4 == 0
            and size > 4
            and mesh.shape["parts"] == 2
            and rows == size // 4 * 2 * BLOCK
            and units == 8 * UNITS
            and 3 * experts <= UNITS
            and size * math.prod(expert_ids.shape[:1]) % 128 == 0
            and width + 4 * expert_ids.shape[1] <= LANES
        )
        args = (tokens, expert_ids, gate_weights, w_gate, w_up, w_down)
        if inner == 1 and even and sums <= 3 * math.prod(w_gate.shape):
            return fixed_weights(size, *args)
        return moved_weights(*args)

    placed = (
        P(("parts", "ep"), "tp"),
        P(("parts", "ep"), None),
        P(("parts", "ep"), None),
        P(None, "ep", "tp"),
        P(None, "ep", "tp"),
        P(None, "tp", "ep"),
    )
    return jax.shard_map(
        body, mesh=mesh, in_specs=placed, out_specs=P(("parts", "ep"), "tp"), check_vma=False
    )
```

```python
import functools
import math

import jax
import jax.numpy as jnp
from jax import lax
from jax.experimental import pallas as pl
from jax.experimental.pallas import tpu as pltpu
from jax.sharding import PartitionSpec as P

BF16 = jnp.bfloat16
F32 = jnp.float32
TILE = 256
BLOCK = 1024
LANES = 256
UNITS = 128


def slots_of(block_ids, experts):
    flat = block_ids.reshape(-1)
    onehot = (flat[:, None] == jnp.arange(experts, dtype=jnp.int32)[None, :]).astype(jnp.int32)
    before = jnp.cumsum(onehot, axis=0) - onehot
    return jnp.sum(before * onehot, axis=1).reshape(block_ids.shape)


def fill_slots(rows, expert_ids, slot, experts, per_expert):
    count, picks = expert_ids.shape
    spread = jnp.broadcast_to(rows[:, None, :], (count, picks, rows.shape[1]))
    empty = jnp.zeros((experts, per_expert, rows.shape[1]), BF16)
    return empty.at[expert_ids, slot].set(spread)


def moved_weights(tokens, expert_ids, gate_weights, w_gate, w_up, w_down):
    tok_rows, picks = expert_ids.shape
    experts = w_gate.shape[0]
    per_expert = min(tok_rows, 3 * tok_rows * picks // (2 * experts))
    slot = slots_of(expert_ids, experts)
    features = lax.all_gather(tokens, "tp", axis=1, tiled=True)
    outgoing = fill_slots(features, expert_ids, slot, experts, per_expert)
    arrived = lax.all_to_all(outgoing, "ep", split_axis=0, concat_axis=1, tiled=True)
    gate_owned, up_owned = (
        lax.all_to_all(w_gate, "ep", split_axis=0, concat_axis=1, tiled=True),
        lax.all_to_all(w_up, "ep", split_axis=0, concat_axis=1, tiled=True),
    )
    gate = jnp.einsum("ecd,edf->ecf", arrived, gate_owned, preferred_element_type=F32)
    up = jnp.einsum("ecd,edf->ecf", arrived, up_owned, preferred_element_type=F32)
    hidden = (jax.nn.silu(gate) * up).astype(BF16)
    down_owned = lax.all_to_all(w_down, "ep", split_axis=0, concat_axis=2, tiled=True)
    partial_value = jnp.einsum("ecf,efd->ecd", hidden, down_owned, preferred_element_type=F32)
    expert_out = lax.psum_scatter(
        partial_value.astype(BF16), "tp", scatter_dimension=2, tiled=True
    )
    returned = lax.all_to_all(expert_out, "ep", split_axis=1, concat_axis=0, tiled=True)
    picked = returned[expert_ids, slot]
    mixed = jnp.sum(gate_weights[:, :, None] * picked.astype(F32), axis=1)
    return mixed.astype(BF16)


def dot(a, b, contract):
    return lax.dot_general(a, b, ((contract[0], contract[1]), ((), ())), preferred_element_type=F32)


def params(mib=48):
    return pltpu.CompilerParams(vmem_limit_bytes=mib << 20)


def cost(flops, moved):
    return pl.CostEstimate(flops=flops, bytes_accessed=moved, transcendentals=0)


def split3(value):
    high = lax.reduce_precision(value, 8, 7)
    middle = lax.reduce_precision(value - high, 8, 7)
    return high, middle, lax.reduce_precision(value - high - middle, 8, 7)


def order_kernel(width, picks, experts, note_ref, place_out, across_out, gates_out, base_out):
    tokens = note_ref.shape[0]
    note = note_ref[...].astype(F32)
    lane = lax.broadcasted_iota(jnp.int32, (tokens, UNITS), 1)
    name = jnp.where(lane < 3 * experts, lane % experts, -1).astype(F32)
    gates = jnp.zeros((tokens, UNITS), F32)
    for k in range(picks):
        one = note[:, width + k : width + k + 1]
        weight = (
            note[:, width + picks + k : width + picks + k + 1]
            + note[:, width + 2 * picks + k : width + 2 * picks + k + 1]
            + note[:, width + 3 * picks + k : width + 3 * picks + k + 1]
        )
        gates = jnp.where(name == one, weight, gates)
    mask = jnp.where((gates != 0.0) & (lane < experts), 1.0, 0.0)
    high = gates.astype(BF16)
    middle = (gates - high.astype(F32)).astype(BF16)
    rest = (gates - high.astype(F32) - middle.astype(F32)).astype(BF16)
    gates_out[...] = jnp.where(
        lane < experts,
        high.astype(F32),
        jnp.where(lane < 2 * experts, middle.astype(F32), rest.astype(F32)),
    ).astype(BF16)
    row = lax.broadcasted_iota(jnp.int32, (tokens, tokens), 0)
    column = lax.broadcasted_iota(jnp.int32, (tokens, tokens), 1)
    upto = jnp.where(column <= row, 1.0, 0.0).astype(BF16)
    count = dot(upto, mask.astype(BF16), ((1,), (0,)))
    total = jnp.broadcast_to(count[tokens - 1 : tokens, :], (8, UNITS))
    large = jnp.floor(total * (1.0 / 128.0))
    row = lax.broadcasted_iota(jnp.int32, (UNITS, UNITS), 0)
    column = lax.broadcasted_iota(jnp.int32, (UNITS, UNITS), 1)
    before = jnp.where(row < column, 1.0, 0.0).astype(BF16)
    base = 128.0 * dot(large.astype(BF16), before, ((1,), (0,)))
    base += dot((total - 128.0 * large).astype(BF16), before, ((1,), (0,)))
    base_out[...] = base.astype(jnp.int32)
    place = jnp.where(mask > 0.0, count - 1.0 + base[0:1, :], -1.0)
    place_out[...] = place.astype(jnp.int32)
    across_out[...] = place.T.astype(jnp.int32)


def order_of(note, width, picks, experts):
    tokens = note.shape[0]
    return pl.pallas_call(
        functools.partial(order_kernel, width, picks, experts),
        out_shape=[
            jax.ShapeDtypeStruct((tokens, UNITS), jnp.int32),
            jax.ShapeDtypeStruct((UNITS, tokens), jnp.int32),
            jax.ShapeDtypeStruct((tokens, UNITS), BF16),
            jax.ShapeDtypeStruct((8, UNITS), jnp.int32),
        ],
        compiler_params=params(),
        cost_estimate=cost(2 * tokens * tokens * UNITS, 4 * tokens * tokens),
        name="order",
    )(note)


def spans_of(base, rows):
    low = jnp.arange(rows // TILE, dtype=jnp.int32)[:, None] * TILE
    return (
        jnp.sum((base[None, 1:] <= low).astype(jnp.int32), axis=1),
        jnp.sum((base[None, :-1] < low + TILE).astype(jnp.int32), axis=1),
    )


def mine_of(base, e, row0):
    row = row0 + lax.broadcasted_iota(jnp.int32, (TILE, 1), 0)
    return (row >= base[e]) & (row < base[e + 1])


def sort_kernel(experts, first, low, high, base, across_ref, gates_ref, *refs):
    slices, (out, scale_out, onehot_ref, name_ref) = refs[:-4], refs[-4:]
    tokens = onehot_ref.shape[1]
    number = lax.broadcasted_iota(jnp.int32, (TILE, 128), 0).astype(F32).astype(BF16)
    onehot_ref[...] = jnp.zeros_like(onehot_ref)

    @pl.loop(0, BLOCK // TILE)
    def _(part):
        i = (first + pl.program_id(0)) * (BLOCK // TILE) + part
        row0 = i * TILE
        here = pl.ds(pl.multiple_of(part * TILE, TILE), TILE)

        @pl.loop(low[i], high[i])
        def _(e):
            away = across_ref[e] - row0
            away = jnp.where((away >= 0) & (away < TILE), away, -1).astype(F32)
            for c in range(tokens // 128):
                at = slice(c * 128, (c + 1) * 128)
                hit = number == away[c : c + 1, :].astype(BF16)
                onehot_ref[here, at] = jnp.where(hit, jnp.ones((), BF16), onehot_ref[here, at])
            name_ref[here, :] = jnp.where(mine_of(base, e, row0), e, name_ref[here, :])

    onehot = onehot_ref[...]
    for k, ref in enumerate(slices):
        out[:, k * LANES : (k + 1) * LANES] = dot(onehot, ref[...], ((1,), (0,))).astype(BF16)
    gates = dot(onehot, gates_ref[...], ((1,), (0,)))
    lane = lax.broadcasted_iota(jnp.int32, (BLOCK, UNITS), 1)
    name = name_ref[...]
    kept = (lane == name) | (lane == name + experts) | (lane == name + 2 * experts)
    scale = jnp.sum(jnp.where(kept, gates, 0.0), axis=1, keepdims=True)
    scale_out[...] = jnp.broadcast_to(scale, lane.shape)


def sort_rows(spans, base, across, gates, slices, rows, experts, begun=()):
    first = rows // BLOCK // 2 * bool(begun)
    kernel = functools.partial(sort_kernel, experts, first)
    if begun:
        kernel = lambda *refs: sort_kernel(experts, first, *refs[:-7], *refs[-4:])
    tokens = gates.shape[0]
    across = across[:experts].reshape(experts, tokens // 128, 128)
    whole = lambda i, *_: (0, 0)
    width = len(slices) * LANES
    return pl.pallas_call(
        kernel,
        grid_spec=pltpu.PrefetchScalarGridSpec(
            num_scalar_prefetch=3,
            grid=(rows // BLOCK // 2,),
            in_specs=[
                pl.BlockSpec(across.shape, lambda i, *_: (0, 0, 0)),
                pl.BlockSpec((tokens, UNITS), whole),
            ]
            + [pl.BlockSpec((tokens, LANES), whole)] * len(slices)
            + [pl.BlockSpec(memory_space=pl.ANY)] * len(begun),
            out_specs=[
                pl.BlockSpec((BLOCK, width), lambda i, *_: (first + i, 0)),
                pl.BlockSpec((BLOCK, UNITS), lambda i, *_: (first + i, 0)),
                pl.BlockSpec((BLOCK, tokens), lambda i, *_: (first + i, 0)),
            ],
            scratch_shapes=[pltpu.VMEM((BLOCK, UNITS), jnp.int32)],
        ),
        out_shape=[
            jax.ShapeDtypeStruct((rows, width), BF16),
            jax.ShapeDtypeStruct((rows, UNITS), F32),
            jax.ShapeDtypeStruct((rows, tokens), BF16),
        ],
        input_output_aliases={5 + len(slices) + k: k for k in range(len(begun))},
        compiler_params=params(),
        cost_estimate=cost(rows * tokens * width, 4 * rows * width),
        name="sort_rows",
    )(*spans, base, across, gates, *slices, *begun)


def sort_more_kernel(onehot_ref, *refs):
    for k, ref in enumerate(refs[:-1]):
        at = slice(k * LANES, (k + 1) * LANES)
        refs[-1][:, at] = dot(onehot_ref[...], ref[...], ((1,), (0,))).astype(BF16)


def sort_more(onehot, slices):
    rows, tokens = onehot.shape
    width = len(slices) * LANES
    return pl.pallas_call(
        sort_more_kernel,
        grid=(rows // BLOCK,),
        in_specs=[pl.BlockSpec((BLOCK, tokens), lambda i: (i, 0))]
        + [pl.BlockSpec((tokens, LANES), lambda i: (0, 0))] * len(slices),
        out_specs=pl.BlockSpec((BLOCK, width), lambda i: (i, 0)),
        out_shape=jax.ShapeDtypeStruct((rows, width), BF16),
        compiler_params=params(),
        cost_estimate=cost(2 * rows * tokens * width, 8 * rows * width),
        name="sort_more",
    )(onehot, *slices)


def scatter_kernel(low, high, place_ref, onehot_ref):
    tokens = place_ref.shape[1]
    lane = lax.broadcasted_iota(jnp.int32, (tokens, 128), 1)
    onehot_ref[...] = jnp.zeros_like(onehot_ref)
    for part in range(BLOCK // TILE):
        i = pl.program_id(0) * (BLOCK // TILE) + part

        @pl.loop(low[i], high[i])
        def _(e):
            place = place_ref[e] - i * TILE
            for c in range(TILE // 128):
                at = slice(part * TILE + c * 128, part * TILE + (c + 1) * 128)
                onehot_ref[:, at] += jnp.where(place == lane + c * 128, 1.0, 0.0).astype(BF16)


def scatter_rows(spans, place, rows):
    tokens = place.shape[1]
    return pl.pallas_call(
        scatter_kernel,
        grid_spec=pltpu.PrefetchScalarGridSpec(
            num_scalar_prefetch=2,
            grid=(rows // BLOCK,),
            in_specs=[pl.BlockSpec(place.shape, lambda i, *_: (0, 0, 0))],
            out_specs=pl.BlockSpec((tokens, BLOCK), lambda i, *_: (0, i)),
        ),
        out_shape=jax.ShapeDtypeStruct((tokens, rows), BF16),
        compiler_params=params(),
        cost_estimate=cost(rows * tokens, 2 * rows * tokens),
        name="scatter_rows",
    )(*spans, place)


def partial_kernel(low, high, base, quarter, near_ref, far_ref, *refs):
    pairs, out = [refs[j : j + 2] for j in range(0, 8, 2)], refs[-1]
    width = pairs[0][0].shape[1]

    @pl.loop(0, BLOCK // TILE)
    def _(part):
        i = pl.program_id(0) * (BLOCK // TILE) + part
        here = pl.ds(pl.multiple_of(part * TILE, TILE), TILE)

        def add(e, kept):
            total = 0.0
            for k, pair in enumerate(pairs):
                weight = jnp.concatenate([pair[0][e], pair[1][e]], axis=1)
                rows_ref, at = (near_ref, far_ref)[k // 2], k % 2 * LANES
                rows = rows_ref[here, at : at + width]
                total += dot(rows, weight, ((1,), (0,)))
            return jnp.where(mine_of(base, e, i * TILE), total, kept)

        out[here, :] = lax.fori_loop(
            low[i], high[i], add, jnp.zeros((TILE, out.shape[1]), F32)
        ).astype(BF16)


def partial_sums(f, spans, base, quarter, near, far, w_gate, w_up, pieces):
    rows = near.shape[0]
    experts, width, _ = w_gate.shape
    own = pl.BlockSpec((experts, width, UNITS), lambda i, lo, hi, b, q: (0, 0, 2 * q[0] + f))
    block = pl.BlockSpec((experts, width, UNITS), lambda i, *_: (0, 0, 0))
    return pl.pallas_call(
        partial_kernel,
        grid_spec=pltpu.PrefetchScalarGridSpec(
            num_scalar_prefetch=4,
            grid=(rows // BLOCK,),
            in_specs=[pl.BlockSpec((BLOCK, 2 * LANES), lambda i, *_: (i, 0))] * 2 + [own] * 2
            + [block] * len(pieces),
            out_specs=pl.BlockSpec((BLOCK, 2 * UNITS), lambda i, *_: (i, 0)),
        ),
        out_shape=jax.ShapeDtypeStruct((rows, 2 * UNITS), BF16),
        compiler_params=params(),
        cost_estimate=cost(16 * rows * LANES * UNITS, 8 * rows * LANES),
        name="partial_sums",
    )(*spans, base, quarter, near, far, w_gate, w_up, *pieces)


def down_kernel(slots, low, high, base, block, onehot_ref, *refs):
    hidden, start, refs = refs[: 4 * slots], refs[4 * slots], refs[4 * slots + 1 :]
    weights, (out, total_ref, value_ref) = refs[:-3], refs[-3:]
    width = weights[0].shape[1]
    j = pl.program_id(0)
    slot = j // 2

    @pl.when(j == 0)
    def _():
        total_ref[...] = jnp.zeros_like(total_ref) if start is None else start[...]
        value_ref[...] = jnp.zeros_like(value_ref)

    @pl.when(block[3 * slot + 2] != 0)
    def _():
        for part in range(BLOCK // TILE):
            i = (2 * block[3 * slot] + j % 2) * (BLOCK // TILE) + part
            here = slice(part * TILE, (part + 1) * TILE)
            source = 4 * slot + 2 - 2 * block[3 * slot + 1] + j % 2
            units = hidden[0][here, :]
            for k in range(1, 4 * slots):
                units = jnp.where(source == k, hidden[k][here, :], units)

            @pl.loop(low[i], high[i])
            def _(e):
                mine = mine_of(base, e, i * TILE)
                for k, weight in enumerate(weights):
                    value = dot(units, weight[e], ((1,), (1,)))
                    at = slice(k * LANES, k * LANES + width)
                    value_ref[here, at] = jnp.where(
                        mine, value, value_ref[here, at].astype(F32)
                    ).astype(BF16)

        total_ref[...] += dot(onehot_ref[...], value_ref[...], ((1,), (0,)))

    @pl.when(j == pl.num_programs(0) - 1)
    def _():
        out[...] = total_ref[...].astype(out.dtype)


def down_and_mix(spans, base, block, onehot, hidden, start, at, weights, dtype):
    rows, units = hidden[0].shape
    slots = len(hidden) // 4
    count, tokens = len(weights), onehot.shape[0]
    some = [pl.BlockSpec((rows, units), lambda j, *_: (0, 0))] * (4 * slots)
    whole = pl.BlockSpec((tokens, count * LANES), lambda j, *_: (0, 0))
    kernel = functools.partial(down_kernel, slots)
    if start is None:
        kernel = lambda *refs: down_kernel(slots, *refs[: 5 + 4 * slots], None, *refs[5 + 4 * slots :])
    return pl.pallas_call(
        kernel,
        grid_spec=pltpu.PrefetchScalarGridSpec(
            num_scalar_prefetch=4,
            grid=(2 * slots,),
            in_specs=[
                pl.BlockSpec(
                    (tokens, BLOCK), lambda j, lo, hi, b, k: (0, 2 * k[3 * (j // 2)] + j % 2)
                )
            ]
            + some
            + [pl.BlockSpec((tokens, count * LANES), lambda j, *_: (0, at // count))]
            * (start is not None)
            + [pl.BlockSpec(w.shape, lambda j, *_: (0, 0, 0)) for w in weights],
            out_specs=whole,
            scratch_shapes=[
                pltpu.VMEM((tokens, count * LANES), F32),
                pltpu.VMEM((BLOCK, count * LANES), BF16),
            ],
        ),
        out_shape=jax.ShapeDtypeStruct((tokens, count * LANES), dtype),
        compiler_params=params(56),
        cost_estimate=cost(4 * slots * rows * tokens * LANES * count, 4 * slots * rows * tokens),
        name="down_and_mix",
    )(*spans, base, block, onehot, *hidden, *([] if start is None else [start]), *weights)


def fixed_weights(size, tokens, expert_ids, gate_weights, w_gate, w_up, w_down):
    count, picks = expert_ids.shape
    experts, width, hidden_units = w_gate.shape
    quarter = hidden_units // 4
    rows = size * count * picks
    places = size // 4
    me, plane = lax.axis_index("ep"), lax.axis_index("parts")
    w_down = jnp.swapaxes(w_down, 1, 2)

    twins = [(i, i ^ 1) for i in range(size)]
    cross = [(p * size + i, p * size + (i ^ 2 ^ p)) for p in range(2) for i in range(size)]
    to_twin = lambda value: lax.ppermute(value, "ep", twins)
    to_cross = lambda value: lax.ppermute(value, ("parts", "ep"), cross)
    to_plane = lambda value: lax.ppermute(value, "parts", [(0, 1), (1, 0)])
    line = [[4 * p + k for p in range(places)] for k in range(4)]
    my_quarter = me % 4
    twin_quarter = my_quarter ^ 1
    cross_quarter = my_quarter ^ 2 ^ plane

    note = jnp.concatenate([expert_ids.astype(F32), *split3(gate_weights)], axis=1).astype(BF16)
    fill = LANES - width - note.shape[1]
    parcels = jnp.concatenate(
        [
            tokens.reshape(count, size, width).swapaxes(0, 1),
            jnp.broadcast_to(jnp.pad(note, ((0, 0), (0, fill)))[None], (size, count, LANES - width)),
        ],
        axis=2,
    )
    own = lax.all_to_all(parcels, "ep", split_axis=0, concat_axis=0, tiled=True)
    own = own.reshape(size * count, LANES)
    far, near = to_cross(own), [own, to_twin(own)]
    place, across, gates, base = order_of(own, width, picks, experts)
    base = base[0, : experts + 1]
    spans = spans_of(base, rows)
    which = my_quarter.astype(jnp.int32).reshape(1)

    def cut(n, q):
        if n == 4:
            return lax.dynamic_slice_in_dim(w_down, q * quarter, quarter, 2)
        at = q * quarter + n // 2 * UNITS
        return lax.dynamic_slice_in_dim((w_gate, w_up)[n % 2], at, UNITS, 2)

    def after(value, *others):
        return lax.optimization_barrier((value, *others))[0]

    crossed = [to_cross(cut(0, cross_quarter)), to_cross(after(cut(1, cross_quarter), near[1], base))]
    begun = sort_rows(spans, base, across, gates, near, rows, experts)
    beside = [to_plane(after(crossed[0], begun[0]))]
    rest = after(gates, crossed[0])
    near_rows, scale, onehot = sort_rows(spans, base, across, rest, near, rows, experts, begun)
    far = after(far, near_rows)
    far_rows = sort_more(onehot, [far, to_twin(far)])
    scale = lax.dynamic_slice_in_dim(scale, (me // 4) * (rows // places), rows // places, 0)

    for n in range(2, 5):
        crossed.append(to_cross(after(cut(n, cross_quarter), far, *crossed[2:n])))
    twin_of = lambda n: to_twin(cut(n, twin_quarter))

    for n in range(1, 4):
        beside.append(to_plane(after(crossed[n], near_rows, beside[n - 1])))

    def sums_of(f, *first):
        rows_in = after(far_rows, *first)
        pair = slice(2 * f, 2 * f + 2)
        held = [twin_of(2 * f), twin_of(2 * f + 1), *crossed[pair], *beside[pair]]
        return partial_sums(f, spans, base, which, near_rows, rows_in, w_gate, w_up, held)

    def units_of(sums):
        sums = lax.psum_scatter(
            sums, "ep", scatter_dimension=0, axis_index_groups=line, tiled=True
        )
        gate, up = sums[:, :UNITS].astype(F32), sums[:, UNITS:].astype(F32)
        return (jax.nn.silu(gate) * up * scale).astype(BF16)

    sums = sums_of(0, crossed[2])
    later = sums_of(1, sums)
    units = [units_of(sums), units_of(later)]
    held = [twin_of(4), crossed[4], to_plane(crossed[4])]

    place = jnp.broadcast_to(
        after(across[:experts], later)[:, :, None], (experts, size * count, 128)
    )
    columns = scatter_rows(spans, place, rows)
    pieces = [after(cut(4, my_quarter), later), *held]
    units, columns, pieces = lax.optimization_barrier((units, columns, pieces))
    units = jnp.concatenate(units, axis=1)

    spot = me // 4

    def steps(value, step, up):
        links = [
            (4 * p + k, 4 * (p + 1 if up else p - 1) + k)
            for p in (range(step - 1, places - 1) if up else range(1, places - step + 1))
            for k in range(4)
        ]
        return lax.ppermute(value, "ep", links)

    def mix(flags, hidden, start, at=0, count=4, dtype=F32):
        block = jnp.stack([jnp.asarray(flag, jnp.int32) for flag in flags])
        hidden = list(hidden)
        return down_and_mix(
            spans, base, block, columns, hidden, start, at, pieces[at : at + count], dtype
        )

    halves = [units[:BLOCK], units[BLOCK:]]
    moving = [[steps(half, 1, up) for up in (True, False)] for half in halves]
    total, waiting = mix((spot, 1, 1), halves + halves, None), []
    for step in range(1, places):
        if step == places - 1 and waiting:
            both = [sum(map(tuple, parts), ()) for parts in zip(*waiting)]
            total = mix(*both, total)
        arrived = []
        for n in range(2):
            *half, total = lax.optimization_barrier((*moving[n], total))
            arrived.append(half)
            if step < places - 1:
                moving[n] = [steps(half[k], step + 1, k == 0) for k in range(2)]
        hidden = [arrived[n][k] for k in range(2) for n in range(2)]
        came_up, came_down = spot >= step, spot < places - step
        above = jnp.minimum(spot + step, places - 1)
        flags = (jnp.where(came_up, spot - step, above), came_up, came_up | came_down)
        if step == places - 1:
            break
        waiting.append((flags, hidden))
        if 2 * step < places:
            waiting.append(((above, 0, came_up & came_down), hidden))
        if step == 1:
            total = mix(*waiting.pop(0), total)
    far = mix(flags, hidden, total, 2, 2, BF16)
    near = after(total, far)
    far, far_twin = far[:, :width], far[:, LANES : LANES + width]
    far = (far.astype(F32) + to_twin(far_twin).astype(F32)).astype(BF16)
    near, far = lax.optimization_barrier((near, far))
    far = to_cross(far)
    near = mix(flags, hidden, near, 0, 2)
    twin = near[:, LANES : LANES + width].astype(BF16)
    twin = to_twin(after(twin, far)).astype(F32)
    mixed = (near[:, :width] + twin + far.astype(F32)).astype(BF16)
    mixed = lax.all_to_all(
        mixed.reshape(size, count, width), "ep", split_axis=0, concat_axis=0, tiled=True
    )
    return mixed.swapaxes(0, 1).reshape(count, size * width)


def solution(mesh):
    size, inner = mesh.shape["ep"], mesh.shape["tp"]

    def body(tokens, expert_ids, gate_weights, w_gate, w_up, w_down):
        rows = size * math.prod(expert_ids.shape)
        sums = rows * w_gate.shape[2]
        experts, width, units = w_gate.shape
        even = (
            size % 4 == 0
            and size > 4
            and mesh.shape["parts"] == 2
            and rows == size // 4 * 2 * BLOCK
            and units == 8 * UNITS
            and 3 * experts <= UNITS
            and size * math.prod(expert_ids.shape[:1]) % 128 == 0
            and width + 4 * expert_ids.shape[1] <= LANES
        )
        args = (tokens, expert_ids, gate_weights, w_gate, w_up, w_down)
        if inner == 1 and even and sums <= 3 * math.prod(w_gate.shape):
            return fixed_weights(size, *args)
        return moved_weights(*args)

    placed = (
        P(("parts", "ep"), "tp"),
        P(("parts", "ep"), None),
        P(("parts", "ep"), None),
        P(None, "ep", "tp"),
        P(None, "ep", "tp"),
        P(None, "tp", "ep"),
    )
    return jax.shard_map(
        body, mesh=mesh, in_specs=placed, out_specs=P(("parts", "ep"), "tp"), check_vma=False
    )
```

```python
import functools
import math

import jax
import jax.numpy as jnp
from jax import lax
from jax.experimental import pallas as pl
from jax.experimental.pallas import tpu as pltpu
from jax.sharding import PartitionSpec as P

BF16 = jnp.bfloat16
F32 = jnp.float32
TILE = 256
BLOCK = 1024
LANES = 256
UNITS = 128


def slots_of(block_ids, experts):
    flat = block_ids.reshape(-1)
    onehot = (flat[:, None] == jnp.arange(experts, dtype=jnp.int32)[None, :]).astype(jnp.int32)
    before = jnp.cumsum(onehot, axis=0) - onehot
    return jnp.sum(before * onehot, axis=1).reshape(block_ids.shape)


def fill_slots(rows, expert_ids, slot, experts, per_expert):
    count, picks = expert_ids.shape
    spread = jnp.broadcast_to(rows[:, None, :], (count, picks, rows.shape[1]))
    empty = jnp.zeros((experts, per_expert, rows.shape[1]), BF16)
    return empty.at[expert_ids, slot].set(spread)


def moved_weights(tokens, expert_ids, gate_weights, w_gate, w_up, w_down):
    tok_rows, picks = expert_ids.shape
    experts = w_gate.shape[0]
    per_expert = min(tok_rows, 3 * tok_rows * picks // (2 * experts))
    slot = slots_of(expert_ids, experts)
    features = lax.all_gather(tokens, "tp", axis=1, tiled=True)
    outgoing = fill_slots(features, expert_ids, slot, experts, per_expert)
    arrived = lax.all_to_all(outgoing, "ep", split_axis=0, concat_axis=1, tiled=True)
    gate_owned, up_owned = (
        lax.all_to_all(w_gate, "ep", split_axis=0, concat_axis=1, tiled=True),
        lax.all_to_all(w_up, "ep", split_axis=0, concat_axis=1, tiled=True),
    )
    gate = jnp.einsum("ecd,edf->ecf", arrived, gate_owned, preferred_element_type=F32)
    up = jnp.einsum("ecd,edf->ecf", arrived, up_owned, preferred_element_type=F32)
    hidden = (jax.nn.silu(gate) * up).astype(BF16)
    down_owned = lax.all_to_all(w_down, "ep", split_axis=0, concat_axis=2, tiled=True)
    partial_value = jnp.einsum("ecf,efd->ecd", hidden, down_owned, preferred_element_type=F32)
    expert_out = lax.psum_scatter(
        partial_value.astype(BF16), "tp", scatter_dimension=2, tiled=True
    )
    returned = lax.all_to_all(expert_out, "ep", split_axis=1, concat_axis=0, tiled=True)
    picked = returned[expert_ids, slot]
    mixed = jnp.sum(gate_weights[:, :, None] * picked.astype(F32), axis=1)
    return mixed.astype(BF16)


def dot(a, b, contract):
    return lax.dot_general(a, b, ((contract[0], contract[1]), ((), ())), preferred_element_type=F32)


def params(mib=48):
    return pltpu.CompilerParams(vmem_limit_bytes=mib << 20)


def cost(flops, moved):
    return pl.CostEstimate(flops=flops, bytes_accessed=moved, transcendentals=0)


def split3(value):
    high = lax.reduce_precision(value, 8, 7)
    middle = lax.reduce_precision(value - high, 8, 7)
    return high, middle, lax.reduce_precision(value - high - middle, 8, 7)


def order_kernel(width, picks, experts, note_ref, place_out, across_out, gates_out, base_out):
    tokens = note_ref.shape[0]
    note = note_ref[...].astype(F32)
    lane = lax.broadcasted_iota(jnp.int32, (tokens, UNITS), 1)
    name = jnp.where(lane < 3 * experts, lane % experts, -1).astype(F32)
    gates = jnp.zeros((tokens, UNITS), F32)
    for k in range(picks):
        one = note[:, width + k : width + k + 1]
        weight = (
            note[:, width + picks + k : width + picks + k + 1]
            + note[:, width + 2 * picks + k : width + 2 * picks + k + 1]
            + note[:, width + 3 * picks + k : width + 3 * picks + k + 1]
        )
        gates = jnp.where(name == one, weight, gates)
    mask = jnp.where((gates != 0.0) & (lane < experts), 1.0, 0.0)
    high = gates.astype(BF16)
    middle = (gates - high.astype(F32)).astype(BF16)
    rest = (gates - high.astype(F32) - middle.astype(F32)).astype(BF16)
    gates_out[...] = jnp.where(
        lane < experts,
        high.astype(F32),
        jnp.where(lane < 2 * experts, middle.astype(F32), rest.astype(F32)),
    ).astype(BF16)
    row = lax.broadcasted_iota(jnp.int32, (tokens, tokens), 0)
    column = lax.broadcasted_iota(jnp.int32, (tokens, tokens), 1)
    upto = jnp.where(column <= row, 1.0, 0.0).astype(BF16)
    count = dot(upto, mask.astype(BF16), ((1,), (0,)))
    total = jnp.broadcast_to(count[tokens - 1 : tokens, :], (8, UNITS))
    large = jnp.floor(total * (1.0 / 128.0))
    row = lax.broadcasted_iota(jnp.int32, (UNITS, UNITS), 0)
    column = lax.broadcasted_iota(jnp.int32, (UNITS, UNITS), 1)
    before = jnp.where(row < column, 1.0, 0.0).astype(BF16)
    base = 128.0 * dot(large.astype(BF16), before, ((1,), (0,)))
    base += dot((total - 128.0 * large).astype(BF16), before, ((1,), (0,)))
    base_out[...] = base.astype(jnp.int32)
    place = jnp.where(mask > 0.0, count - 1.0 + base[0:1, :], -1.0)
    place_out[...] = place.astype(jnp.int32)
    across_out[...] = place.T.astype(jnp.int32)


def order_of(note, width, picks, experts):
    tokens = note.shape[0]
    return pl.pallas_call(
        functools.partial(order_kernel, width, picks, experts),
        out_shape=[
            jax.ShapeDtypeStruct((tokens, UNITS), jnp.int32),
            jax.ShapeDtypeStruct((UNITS, tokens), jnp.int32),
            jax.ShapeDtypeStruct((tokens, UNITS), BF16),
            jax.ShapeDtypeStruct((8, UNITS), jnp.int32),
        ],
        compiler_params=params(),
        cost_estimate=cost(2 * tokens * tokens * UNITS, 4 * tokens * tokens),
        name="order",
    )(note)


def spans_of(base, rows):
    low = jnp.arange(rows // TILE, dtype=jnp.int32)[:, None] * TILE
    return (
        jnp.sum((base[None, 1:] <= low).astype(jnp.int32), axis=1),
        jnp.sum((base[None, :-1] < low + TILE).astype(jnp.int32), axis=1),
    )


def mine_of(base, e, row0):
    row = row0 + lax.broadcasted_iota(jnp.int32, (TILE, 1), 0)
    return (row >= base[e]) & (row < base[e + 1])


def sort_kernel(experts, first, low, high, base, across_ref, gates_ref, *refs):
    slices, (out, scale_out, onehot_ref, name_ref) = refs[:-4], refs[-4:]
    tokens = onehot_ref.shape[1]
    number = lax.broadcasted_iota(jnp.int32, (TILE, 128), 0).astype(F32).astype(BF16)
    onehot_ref[...] = jnp.zeros_like(onehot_ref)

    @pl.loop(0, BLOCK // TILE)
    def _(part):
        i = (first + pl.program_id(0)) * (BLOCK // TILE) + part
        row0 = i * TILE
        here = pl.ds(pl.multiple_of(part * TILE, TILE), TILE)

        @pl.loop(low[i], high[i])
        def _(e):
            away = across_ref[e] - row0
            away = jnp.where((away >= 0) & (away < TILE), away, -1).astype(F32)
            for c in range(tokens // 128):
                at = slice(c * 128, (c + 1) * 128)
                hit = number == away[c : c + 1, :].astype(BF16)
                onehot_ref[here, at] = jnp.where(hit, jnp.ones((), BF16), onehot_ref[here, at])
            name_ref[here, :] = jnp.where(mine_of(base, e, row0), e, name_ref[here, :])

    onehot = onehot_ref[...]
    for k, ref in enumerate(slices):
        out[:, k * LANES : (k + 1) * LANES] = dot(onehot, ref[...], ((1,), (0,))).astype(BF16)
    gates = dot(onehot, gates_ref[...], ((1,), (0,)))
    lane = lax.broadcasted_iota(jnp.int32, (BLOCK, UNITS), 1)
    name = name_ref[...]
    kept = (lane == name) | (lane == name + experts) | (lane == name + 2 * experts)
    scale = jnp.sum(jnp.where(kept, gates, 0.0), axis=1, keepdims=True)
    scale_out[...] = jnp.broadcast_to(scale, lane.shape)


def sort_rows(spans, base, across, gates, slices, rows, experts, begun=()):
    first = rows // BLOCK // 2 * bool(begun)
    kernel = functools.partial(sort_kernel, experts, first)
    if begun:
        kernel = lambda *refs: sort_kernel(experts, first, *refs[:-7], *refs[-4:])
    tokens = gates.shape[0]
    across = across[:experts].reshape(experts, tokens // 128, 128)
    whole = lambda i, *_: (0, 0)
    width = len(slices) * LANES
    return pl.pallas_call(
        kernel,
        grid_spec=pltpu.PrefetchScalarGridSpec(
            num_scalar_prefetch=3,
            grid=(rows // BLOCK // 2,),
            in_specs=[
                pl.BlockSpec(across.shape, lambda i, *_: (0, 0, 0)),
                pl.BlockSpec((tokens, UNITS), whole),
            ]
            + [pl.BlockSpec((tokens, LANES), whole)] * len(slices)
            + [pl.BlockSpec(memory_space=pl.ANY)] * len(begun),
            out_specs=[
                pl.BlockSpec((BLOCK, width), lambda i, *_: (first + i, 0)),
                pl.BlockSpec((BLOCK, UNITS), lambda i, *_: (first + i, 0)),
                pl.BlockSpec((BLOCK, tokens), lambda i, *_: (first + i, 0)),
            ],
            scratch_shapes=[pltpu.VMEM((BLOCK, UNITS), jnp.int32)],
        ),
        out_shape=[
            jax.ShapeDtypeStruct((rows, width), BF16),
            jax.ShapeDtypeStruct((rows, UNITS), F32),
            jax.ShapeDtypeStruct((rows, tokens), BF16),
        ],
        input_output_aliases={5 + len(slices) + k: k for k in range(len(begun))},
        compiler_params=params(),
        cost_estimate=cost(rows * tokens * width, 4 * rows * width),
        name="sort_rows",
    )(*spans, base, across, gates, *slices, *begun)


def sort_more_kernel(onehot_ref, *refs):
    for k, ref in enumerate(refs[:-1]):
        at = slice(k * LANES, (k + 1) * LANES)
        refs[-1][:, at] = dot(onehot_ref[...], ref[...], ((1,), (0,))).astype(BF16)


def sort_more(onehot, slices):
    rows, tokens = onehot.shape
    width = len(slices) * LANES
    return pl.pallas_call(
        sort_more_kernel,
        grid=(rows // BLOCK,),
        in_specs=[pl.BlockSpec((BLOCK, tokens), lambda i: (i, 0))]
        + [pl.BlockSpec((tokens, LANES), lambda i: (0, 0))] * len(slices),
        out_specs=pl.BlockSpec((BLOCK, width), lambda i: (i, 0)),
        out_shape=jax.ShapeDtypeStruct((rows, width), BF16),
        compiler_params=params(),
        cost_estimate=cost(2 * rows * tokens * width, 8 * rows * width),
        name="sort_more",
    )(onehot, *slices)


def scatter_kernel(low, high, place_ref, onehot_ref):
    tokens = place_ref.shape[1]
    lane = lax.broadcasted_iota(jnp.int32, (tokens, 128), 1)
    onehot_ref[...] = jnp.zeros_like(onehot_ref)
    for part in range(BLOCK // TILE):
        i = pl.program_id(0) * (BLOCK // TILE) + part

        @pl.loop(low[i], high[i])
        def _(e):
            place = place_ref[e] - i * TILE
            for c in range(TILE // 128):
                at = slice(part * TILE + c * 128, part * TILE + (c + 1) * 128)
                onehot_ref[:, at] += jnp.where(place == lane + c * 128, 1.0, 0.0).astype(BF16)


def scatter_rows(spans, place, rows):
    tokens = place.shape[1]
    return pl.pallas_call(
        scatter_kernel,
        grid_spec=pltpu.PrefetchScalarGridSpec(
            num_scalar_prefetch=2,
            grid=(rows // BLOCK,),
            in_specs=[pl.BlockSpec(place.shape, lambda i, *_: (0, 0, 0))],
            out_specs=pl.BlockSpec((tokens, BLOCK), lambda i, *_: (0, i)),
        ),
        out_shape=jax.ShapeDtypeStruct((tokens, rows), BF16),
        compiler_params=params(),
        cost_estimate=cost(rows * tokens, 2 * rows * tokens),
        name="scatter_rows",
    )(*spans, place)


def partial_kernel(low, high, base, quarter, near_ref, far_ref, *refs):
    pairs, out = [refs[j : j + 2] for j in range(0, 8, 2)], refs[-1]
    width = pairs[0][0].shape[1]

    @pl.loop(0, BLOCK // TILE)
    def _(part):
        i = pl.program_id(0) * (BLOCK // TILE) + part
        here = pl.ds(pl.multiple_of(part * TILE, TILE), TILE)

        def add(e, kept):
            total = 0.0
            for k, pair in enumerate(pairs):
                weight = jnp.concatenate([pair[0][e], pair[1][e]], axis=1)
                rows_ref, at = (near_ref, far_ref)[k // 2], k % 2 * LANES
                rows = rows_ref[here, at : at + width]
                total += dot(rows, weight, ((1,), (0,)))
            return jnp.where(mine_of(base, e, i * TILE), total, kept)

        out[here, :] = lax.fori_loop(
            low[i], high[i], add, jnp.zeros((TILE, out.shape[1]), F32)
        ).astype(BF16)


def partial_sums(f, spans, base, quarter, near, far, w_gate, w_up, pieces):
    rows = near.shape[0]
    experts, width, _ = w_gate.shape
    own = pl.BlockSpec((experts, width, UNITS), lambda i, lo, hi, b, q: (0, 0, 2 * q[0] + f))
    block = pl.BlockSpec((experts, width, UNITS), lambda i, *_: (0, 0, 0))
    return pl.pallas_call(
        partial_kernel,
        grid_spec=pltpu.PrefetchScalarGridSpec(
            num_scalar_prefetch=4,
            grid=(rows // BLOCK,),
            in_specs=[pl.BlockSpec((BLOCK, 2 * LANES), lambda i, *_: (i, 0))] * 2 + [own] * 2
            + [block] * len(pieces),
            out_specs=pl.BlockSpec((BLOCK, 2 * UNITS), lambda i, *_: (i, 0)),
        ),
        out_shape=jax.ShapeDtypeStruct((rows, 2 * UNITS), BF16),
        compiler_params=params(),
        cost_estimate=cost(16 * rows * LANES * UNITS, 8 * rows * LANES),
        name="partial_sums",
    )(*spans, base, quarter, near, far, w_gate, w_up, *pieces)


def down_kernel(slots, low, high, base, block, onehot_ref, *refs):
    hidden, start, refs = refs[: 2 * slots], refs[2 * slots], refs[2 * slots + 1 :]
    weights, (out, total_ref, value_ref) = refs[:-3], refs[-3:]
    width = weights[0].shape[1]
    j = pl.program_id(0)
    slot = j // 2

    @pl.when(j == 0)
    def _():
        total_ref[...] = jnp.zeros_like(total_ref) if start is None else start[...]
        value_ref[...] = jnp.zeros_like(value_ref)

    @pl.when(block[3 * slot + 2] != 0)
    def _():
        for part in range(BLOCK // TILE):
            i = (2 * block[3 * slot] + j % 2) * (BLOCK // TILE) + part
            here = slice(part * TILE, (part + 1) * TILE)
            source = 2 * slot + 1 - block[3 * slot + 1]
            units = hidden[0][here, :]
            for k in range(1, 2 * slots):
                units = jnp.where(source == k, hidden[k][here, :], units)

            @pl.loop(low[i], high[i])
            def _(e):
                mine = mine_of(base, e, i * TILE)
                for k, weight in enumerate(weights):
                    value = dot(units, weight[e], ((1,), (1,)))
                    at = slice(k * LANES, k * LANES + width)
                    value_ref[here, at] = jnp.where(
                        mine, value, value_ref[here, at].astype(F32)
                    ).astype(BF16)

        total_ref[...] += dot(onehot_ref[...], value_ref[...], ((1,), (0,)))

    @pl.when(j == pl.num_programs(0) - 1)
    def _():
        out[...] = total_ref[...].astype(out.dtype)


def down_and_mix(spans, base, block, onehot, hidden, start, at, weights, dtype):
    rows, units = hidden[0].shape
    slots = len(hidden) // 2
    count, tokens = len(weights), onehot.shape[0]
    some = [
        pl.BlockSpec((BLOCK, units), lambda j, *_, s=k // 2: (jnp.clip(j - 2 * s, 0, 1), 0))
        for k in range(2 * slots)
    ]
    whole = pl.BlockSpec((tokens, count * LANES), lambda j, *_: (0, 0))
    kernel = functools.partial(down_kernel, slots)
    if start is None:
        kernel = lambda *refs: down_kernel(slots, *refs[: 5 + 2 * slots], None, *refs[5 + 2 * slots :])
    return pl.pallas_call(
        kernel,
        grid_spec=pltpu.PrefetchScalarGridSpec(
            num_scalar_prefetch=4,
            grid=(2 * slots,),
            in_specs=[
                pl.BlockSpec(
                    (tokens, BLOCK), lambda j, lo, hi, b, k: (0, 2 * k[3 * (j // 2)] + j % 2)
                )
            ]
            + some
            + [pl.BlockSpec((tokens, count * LANES), lambda j, *_: (0, at // count))]
            * (start is not None)
            + [pl.BlockSpec(w.shape, lambda j, *_: (0, 0, 0)) for w in weights],
            out_specs=whole,
            scratch_shapes=[
                pltpu.VMEM((tokens, count * LANES), F32),
                pltpu.VMEM((BLOCK, count * LANES), BF16),
            ],
        ),
        out_shape=jax.ShapeDtypeStruct((tokens, count * LANES), dtype),
        compiler_params=params(32),
        cost_estimate=cost(2 * slots * rows * tokens * LANES * count, 2 * slots * rows * tokens),
        name="down_and_mix",
    )(*spans, base, block, onehot, *hidden, *([] if start is None else [start]), *weights)


def fixed_weights(size, tokens, expert_ids, gate_weights, w_gate, w_up, w_down):
    count, picks = expert_ids.shape
    experts, width, hidden_units = w_gate.shape
    quarter = hidden_units // 4
    rows = size * count * picks
    places = size // 4
    me, plane = lax.axis_index("ep"), lax.axis_index("parts")
    w_down = jnp.swapaxes(w_down, 1, 2)

    twins = [(i, i ^ 1) for i in range(size)]
    cross = [(p * size + i, p * size + (i ^ 2 ^ p)) for p in range(2) for i in range(size)]
    to_twin = lambda value: lax.ppermute(value, "ep", twins)
    to_cross = lambda value: lax.ppermute(value, ("parts", "ep"), cross)
    to_plane = lambda value: lax.ppermute(value, "parts", [(0, 1), (1, 0)])
    line = [[4 * p + k for p in range(places)] for k in range(4)]
    my_quarter = me % 4
    twin_quarter = my_quarter ^ 1
    cross_quarter = my_quarter ^ 2 ^ plane

    note = jnp.concatenate([expert_ids.astype(F32), *split3(gate_weights)], axis=1).astype(BF16)
    fill = LANES - width - note.shape[1]
    parcels = jnp.concatenate(
        [
            tokens.reshape(count, size, width).swapaxes(0, 1),
            jnp.broadcast_to(jnp.pad(note, ((0, 0), (0, fill)))[None], (size, count, LANES - width)),
        ],
        axis=2,
    )
    own = lax.all_to_all(parcels, "ep", split_axis=0, concat_axis=0, tiled=True)
    own = own.reshape(size * count, LANES)
    far, near = to_cross(own), [own, to_twin(own)]
    place, across, gates, base = order_of(own, width, picks, experts)
    base = base[0, : experts + 1]
    spans = spans_of(base, rows)
    which = my_quarter.astype(jnp.int32).reshape(1)

    def cut(n, q):
        if n == 4:
            return lax.dynamic_slice_in_dim(w_down, q * quarter, quarter, 2)
        at = q * quarter + n // 2 * UNITS
        return lax.dynamic_slice_in_dim((w_gate, w_up)[n % 2], at, UNITS, 2)

    def after(value, *others):
        return lax.optimization_barrier((value, *others))[0]

    crossed = [to_cross(cut(0, cross_quarter)), to_cross(after(cut(1, cross_quarter), near[1], base))]
    begun = sort_rows(spans, base, across, gates, near, rows, experts)
    beside = [to_plane(after(crossed[0], begun[0]))]
    rest = after(gates, crossed[0])
    near_rows, scale, onehot = sort_rows(spans, base, across, rest, near, rows, experts, begun)
    far = after(far, near_rows)
    far_rows = sort_more(onehot, [far, to_twin(far)])
    scale = lax.dynamic_slice_in_dim(scale, (me // 4) * (rows // places), rows // places, 0)

    for n in range(2, 5):
        crossed.append(to_cross(after(cut(n, cross_quarter), far, *crossed[2:n])))
    twin_of = lambda n: to_twin(cut(n, twin_quarter))

    for n in range(1, 4):
        beside.append(to_plane(after(crossed[n], near_rows, beside[n - 1])))

    def sums_of(f, *first):
        rows_in = after(far_rows, *first)
        pair = slice(2 * f, 2 * f + 2)
        held = [twin_of(2 * f), twin_of(2 * f + 1), *crossed[pair], *beside[pair]]
        return partial_sums(f, spans, base, which, near_rows, rows_in, w_gate, w_up, held)

    def units_of(sums):
        sums = lax.psum_scatter(
            sums, "ep", scatter_dimension=0, axis_index_groups=line, tiled=True
        )
        gate, up = sums[:, :UNITS].astype(F32), sums[:, UNITS:].astype(F32)
        return (jax.nn.silu(gate) * up * scale).astype(BF16)

    sums = sums_of(0, crossed[2])
    later = sums_of(1, sums)
    units = [units_of(sums), units_of(later)]
    held = [twin_of(4), crossed[4], to_plane(crossed[4])]

    place = jnp.broadcast_to(
        after(across[:experts], later)[:, :, None], (experts, size * count, 128)
    )
    columns = scatter_rows(spans, place, rows)
    pieces = [after(cut(4, my_quarter), later), *held]
    units, columns, pieces = lax.optimization_barrier((units, columns, pieces))
    units = jnp.concatenate(units, axis=1)

    spot = me // 4

    def steps(value, step, up):
        links = [
            (4 * p + k, 4 * (p + 1 if up else p - 1) + k)
            for p in (range(step - 1, places - 1) if up else range(1, places - step + 1))
            for k in range(4)
        ]
        return lax.ppermute(value, "ep", links)

    def mix(flags, hidden, start, at=0, count=4, dtype=F32):
        block = jnp.stack([jnp.asarray(flag, jnp.int32) for flag in flags])
        hidden = list(hidden)
        return down_and_mix(
            spans, base, block, columns, hidden, start, at, pieces[at : at + count], dtype
        )

    moving = [steps(units, 1, True), steps(units, 1, False)]
    total, waiting = mix((spot, 1, 1), [units, units], None), []
    for step in range(1, places):
        if step == places - 1:
            if waiting:
                both = [sum(map(tuple, parts), ()) for parts in zip(*waiting)]
                total = mix(*both, total)
        *hidden, total = lax.optimization_barrier((*moving, total))
        came_up, came_down = spot >= step, spot < places - step
        above = jnp.minimum(spot + step, places - 1)
        flags = (jnp.where(came_up, spot - step, above), came_up, came_up | came_down)
        if step == places - 1:
            break
        moving = [steps(hidden[0], step + 1, True), steps(hidden[1], step + 1, False)]
        waiting.append((flags, hidden))
        if 2 * step < places:
            waiting.append(((above, 0, came_up & came_down), hidden))
        if step == 1:
            total = mix(*waiting.pop(0), total)
    far = mix(flags, hidden, total, 2, 2, BF16)
    near = after(total, far)
    far, far_twin = far[:, :width], far[:, LANES : LANES + width]
    far = (far.astype(F32) + to_twin(far_twin).astype(F32)).astype(BF16)
    near, far = lax.optimization_barrier((near, far))
    far = to_cross(far)
    near = mix(flags, hidden, near, 0, 2)
    twin = near[:, LANES : LANES + width].astype(BF16)
    twin = to_twin(after(twin, far)).astype(F32)
    mixed = (near[:, :width] + twin + far.astype(F32)).astype(BF16)
    mixed = lax.all_to_all(
        mixed.reshape(size, count, width), "ep", split_axis=0, concat_axis=0, tiled=True
    )
    return mixed.swapaxes(0, 1).reshape(count, size * width)


def solution(mesh):
    size, inner = mesh.shape["ep"], mesh.shape["tp"]

    def body(tokens, expert_ids, gate_weights, w_gate, w_up, w_down):
        rows = size * math.prod(expert_ids.shape)
        sums = rows * w_gate.shape[2]
        experts, width, units = w_gate.shape
        even = (
            size % 4 == 0
            and size > 4
            and mesh.shape["parts"] == 2
            and rows == size // 4 * 2 * BLOCK
            and units == 8 * UNITS
            and 3 * experts <= UNITS
            and size * math.prod(expert_ids.shape[:1]) % 128 == 0
            and width + 4 * expert_ids.shape[1] <= LANES
        )
        args = (tokens, expert_ids, gate_weights, w_gate, w_up, w_down)
        if inner == 1 and even and sums <= 3 * math.prod(w_gate.shape):
            return fixed_weights(size, *args)
        return moved_weights(*args)

    placed = (
        P(("parts", "ep"), "tp"),
        P(("parts", "ep"), None),
        P(("parts", "ep"), None),
        P(None, "ep", "tp"),
        P(None, "ep", "tp"),
        P(None, "tp", "ep"),
    )
    return jax.shard_map(
        body, mesh=mesh, in_specs=placed, out_specs=P(("parts", "ep"), "tp"), check_vma=False
    )
```

```python
import functools
import math

import jax
import jax.numpy as jnp
from jax import lax
from jax.experimental import pallas as pl
from jax.experimental.pallas import tpu as pltpu
from jax.sharding import PartitionSpec as P

BF16 = jnp.bfloat16
F32 = jnp.float32
TILE = 256
BLOCK = 1024
LANES = 256
UNITS = 128


def slots_of(block_ids, experts):
    flat = block_ids.reshape(-1)
    onehot = (flat[:, None] == jnp.arange(experts, dtype=jnp.int32)[None, :]).astype(jnp.int32)
    before = jnp.cumsum(onehot, axis=0) - onehot
    return jnp.sum(before * onehot, axis=1).reshape(block_ids.shape)


def fill_slots(rows, expert_ids, slot, experts, per_expert):
    count, picks = expert_ids.shape
    spread = jnp.broadcast_to(rows[:, None, :], (count, picks, rows.shape[1]))
    empty = jnp.zeros((experts, per_expert, rows.shape[1]), BF16)
    return empty.at[expert_ids, slot].set(spread)


def moved_weights(tokens, expert_ids, gate_weights, w_gate, w_up, w_down):
    tok_rows, picks = expert_ids.shape
    experts = w_gate.shape[0]
    per_expert = min(tok_rows, 3 * tok_rows * picks // (2 * experts))
    slot = slots_of(expert_ids, experts)
    features = lax.all_gather(tokens, "tp", axis=1, tiled=True)
    outgoing = fill_slots(features, expert_ids, slot, experts, per_expert)
    arrived = lax.all_to_all(outgoing, "ep", split_axis=0, concat_axis=1, tiled=True)
    gate_owned, up_owned = (
        lax.all_to_all(w_gate, "ep", split_axis=0, concat_axis=1, tiled=True),
        lax.all_to_all(w_up, "ep", split_axis=0, concat_axis=1, tiled=True),
    )
    gate = jnp.einsum("ecd,edf->ecf", arrived, gate_owned, preferred_element_type=F32)
    up = jnp.einsum("ecd,edf->ecf", arrived, up_owned, preferred_element_type=F32)
    hidden = (jax.nn.silu(gate) * up).astype(BF16)
    down_owned = lax.all_to_all(w_down, "ep", split_axis=0, concat_axis=2, tiled=True)
    partial_value = jnp.einsum("ecf,efd->ecd", hidden, down_owned, preferred_element_type=F32)
    expert_out = lax.psum_scatter(
        partial_value.astype(BF16), "tp", scatter_dimension=2, tiled=True
    )
    returned = lax.all_to_all(expert_out, "ep", split_axis=1, concat_axis=0, tiled=True)
    picked = returned[expert_ids, slot]
    mixed = jnp.sum(gate_weights[:, :, None] * picked.astype(F32), axis=1)
    return mixed.astype(BF16)


def dot(a, b, contract):
    return lax.dot_general(a, b, ((contract[0], contract[1]), ((), ())), preferred_element_type=F32)


def params(mib=24):
    return pltpu.CompilerParams(vmem_limit_bytes=mib << 20)


def cost(flops, moved):
    return pl.CostEstimate(flops=flops, bytes_accessed=moved, transcendentals=0)


def split3(value):
    high = lax.reduce_precision(value, 8, 7)
    middle = lax.reduce_precision(value - high, 8, 7)
    return high, middle, lax.reduce_precision(value - high - middle, 8, 7)


def order_kernel(width, picks, experts, note_ref, place_out, across_out, gates_out, base_out):
    tokens = note_ref.shape[0]
    note = note_ref[...].astype(F32)
    lane = lax.broadcasted_iota(jnp.int32, (tokens, UNITS), 1)
    name = jnp.where(lane < 3 * experts, lane % experts, -1).astype(F32)
    gates = jnp.zeros((tokens, UNITS), F32)
    for k in range(picks):
        one = note[:, width + k : width + k + 1]
        weight = (
            note[:, width + picks + k : width + picks + k + 1]
            + note[:, width + 2 * picks + k : width + 2 * picks + k + 1]
            + note[:, width + 3 * picks + k : width + 3 * picks + k + 1]
        )
        gates = jnp.where(name == one, weight, gates)
    mask = jnp.where((gates != 0.0) & (lane < experts), 1.0, 0.0)
    high = gates.astype(BF16)
    middle = (gates - high.astype(F32)).astype(BF16)
    rest = (gates - high.astype(F32) - middle.astype(F32)).astype(BF16)
    gates_out[...] = jnp.where(
        lane < experts,
        high.astype(F32),
        jnp.where(lane < 2 * experts, middle.astype(F32), rest.astype(F32)),
    ).astype(BF16)
    row = lax.broadcasted_iota(jnp.int32, (tokens, tokens), 0)
    column = lax.broadcasted_iota(jnp.int32, (tokens, tokens), 1)
    upto = jnp.where(column <= row, 1.0, 0.0).astype(BF16)
    count = dot(upto, mask.astype(BF16), ((1,), (0,)))
    total = jnp.broadcast_to(count[tokens - 1 : tokens, :], (8, UNITS))
    large = jnp.floor(total * (1.0 / 128.0))
    row = lax.broadcasted_iota(jnp.int32, (UNITS, UNITS), 0)
    column = lax.broadcasted_iota(jnp.int32, (UNITS, UNITS), 1)
    before = jnp.where(row < column, 1.0, 0.0).astype(BF16)
    base = 128.0 * dot(large.astype(BF16), before, ((1,), (0,)))
    base += dot((total - 128.0 * large).astype(BF16), before, ((1,), (0,)))
    base_out[...] = base.astype(jnp.int32)
    place = jnp.where(mask > 0.0, count - 1.0 + base[0:1, :], -1.0)
    place_out[...] = place.astype(jnp.int32)
    across_out[...] = place.T.astype(jnp.int32)


def order_of(note, width, picks, experts):
    tokens = note.shape[0]
    return pl.pallas_call(
        functools.partial(order_kernel, width, picks, experts),
        out_shape=[
            jax.ShapeDtypeStruct((tokens, UNITS), jnp.int32),
            jax.ShapeDtypeStruct((UNITS, tokens), jnp.int32),
            jax.ShapeDtypeStruct((tokens, UNITS), BF16),
            jax.ShapeDtypeStruct((8, UNITS), jnp.int32),
        ],
        compiler_params=params(),
        cost_estimate=cost(2 * tokens * tokens * UNITS, 4 * tokens * tokens),
        name="order",
    )(note)


def spans_of(base, rows):
    low = jnp.arange(rows // TILE, dtype=jnp.int32)[:, None] * TILE
    return (
        jnp.sum((base[None, 1:] <= low).astype(jnp.int32), axis=1),
        jnp.sum((base[None, :-1] < low + TILE).astype(jnp.int32), axis=1),
    )


def mine_of(base, e, row0):
    row = row0 + lax.broadcasted_iota(jnp.int32, (TILE, 1), 0)
    return (row >= base[e]) & (row < base[e + 1])


def sort_kernel(experts, first, low, high, base, across_ref, gates_ref, *refs):
    slices, (out, scale_out, onehot_ref, name_ref) = refs[:-4], refs[-4:]
    tokens = onehot_ref.shape[1]
    number = lax.broadcasted_iota(jnp.int32, (TILE, 128), 0).astype(F32).astype(BF16)
    onehot_ref[...] = jnp.zeros_like(onehot_ref)

    @pl.loop(0, BLOCK // TILE)
    def _(part):
        i = (first + pl.program_id(0)) * (BLOCK // TILE) + part
        row0 = i * TILE
        here = pl.ds(pl.multiple_of(part * TILE, TILE), TILE)

        @pl.loop(low[i], high[i])
        def _(e):
            away = across_ref[e] - row0
            away = jnp.where((away >= 0) & (away < TILE), away, -1).astype(F32)
            for c in range(tokens // 128):
                at = slice(c * 128, (c + 1) * 128)
                hit = number == away[c : c + 1, :].astype(BF16)
                onehot_ref[here, at] = jnp.where(hit, jnp.ones((), BF16), onehot_ref[here, at])
            name_ref[here, :] = jnp.where(mine_of(base, e, row0), e, name_ref[here, :])

    onehot = onehot_ref[...]
    for k, ref in enumerate(slices):
        out[:, k * LANES : (k + 1) * LANES] = dot(onehot, ref[...], ((1,), (0,))).astype(BF16)
    gates = dot(onehot, gates_ref[...], ((1,), (0,)))
    lane = lax.broadcasted_iota(jnp.int32, (BLOCK, UNITS), 1)
    name = name_ref[...]
    kept = (lane == name) | (lane == name + experts) | (lane == name + 2 * experts)
    scale = jnp.sum(jnp.where(kept, gates, 0.0), axis=1, keepdims=True)
    scale_out[...] = jnp.broadcast_to(scale, lane.shape)


def sort_rows(spans, base, across, gates, slices, rows, experts, begun=()):
    first = rows // BLOCK // 2 * bool(begun)
    kernel = functools.partial(sort_kernel, experts, first)
    if begun:
        kernel = lambda *refs: sort_kernel(experts, first, *refs[:-7], *refs[-4:])
    tokens = gates.shape[0]
    across = across[:experts].reshape(experts, tokens // 128, 128)
    whole = lambda i, *_: (0, 0)
    width = len(slices) * LANES
    return pl.pallas_call(
        kernel,
        grid_spec=pltpu.PrefetchScalarGridSpec(
            num_scalar_prefetch=3,
            grid=(rows // BLOCK // 2,),
            in_specs=[
                pl.BlockSpec(across.shape, lambda i, *_: (0, 0, 0)),
                pl.BlockSpec((tokens, UNITS), whole),
            ]
            + [pl.BlockSpec((tokens, LANES), whole)] * len(slices)
            + [pl.BlockSpec(memory_space=pl.ANY)] * len(begun),
            out_specs=[
                pl.BlockSpec((BLOCK, width), lambda i, *_: (first + i, 0)),
                pl.BlockSpec((BLOCK, UNITS), lambda i, *_: (first + i, 0)),
                pl.BlockSpec((BLOCK, tokens), lambda i, *_: (first + i, 0)),
            ],
            scratch_shapes=[pltpu.VMEM((BLOCK, UNITS), jnp.int32)],
        ),
        out_shape=[
            jax.ShapeDtypeStruct((rows, width), BF16),
            jax.ShapeDtypeStruct((rows, UNITS), F32),
            jax.ShapeDtypeStruct((rows, tokens), BF16),
        ],
        input_output_aliases={5 + len(slices) + k: k for k in range(len(begun))},
        compiler_params=params(),
        cost_estimate=cost(rows * tokens * width, 4 * rows * width),
        name="sort_rows",
    )(*spans, base, across, gates, *slices, *begun)


def sort_more_kernel(onehot_ref, *refs):
    for k, ref in enumerate(refs[:-1]):
        at = slice(k * LANES, (k + 1) * LANES)
        refs[-1][:, at] = dot(onehot_ref[...], ref[...], ((1,), (0,))).astype(BF16)


def sort_more(onehot, slices):
    rows, tokens = onehot.shape
    width = len(slices) * LANES
    return pl.pallas_call(
        sort_more_kernel,
        grid=(rows // BLOCK,),
        in_specs=[pl.BlockSpec((BLOCK, tokens), lambda i: (i, 0))]
        + [pl.BlockSpec((tokens, LANES), lambda i: (0, 0))] * len(slices),
        out_specs=pl.BlockSpec((BLOCK, width), lambda i: (i, 0)),
        out_shape=jax.ShapeDtypeStruct((rows, width), BF16),
        compiler_params=params(),
        cost_estimate=cost(2 * rows * tokens * width, 8 * rows * width),
        name="sort_more",
    )(onehot, *slices)


def scatter_kernel(low, high, place_ref, onehot_ref):
    tokens = place_ref.shape[1]
    lane = lax.broadcasted_iota(jnp.int32, (tokens, 128), 1)
    onehot_ref[...] = jnp.zeros_like(onehot_ref)
    for part in range(BLOCK // TILE):
        i = pl.program_id(0) * (BLOCK // TILE) + part

        @pl.loop(low[i], high[i])
        def _(e):
            place = place_ref[e] - i * TILE
            for c in range(TILE // 128):
                at = slice(part * TILE + c * 128, part * TILE + (c + 1) * 128)
                onehot_ref[:, at] += jnp.where(place == lane + c * 128, 1.0, 0.0).astype(BF16)


def scatter_rows(spans, place, rows):
    tokens = place.shape[1]
    return pl.pallas_call(
        scatter_kernel,
        grid_spec=pltpu.PrefetchScalarGridSpec(
            num_scalar_prefetch=2,
            grid=(rows // BLOCK,),
            in_specs=[pl.BlockSpec(place.shape, lambda i, *_: (0, 0, 0))],
            out_specs=pl.BlockSpec((tokens, BLOCK), lambda i, *_: (0, i)),
        ),
        out_shape=jax.ShapeDtypeStruct((tokens, rows), BF16),
        compiler_params=params(),
        cost_estimate=cost(rows * tokens, 2 * rows * tokens),
        name="scatter_rows",
    )(*spans, place)


def partial_kernel(low, high, base, quarter, near_ref, far_ref, *refs):
    pairs, out = [refs[j : j + 2] for j in range(0, 8, 2)], refs[-1]
    width = pairs[0][0].shape[1]

    @pl.loop(0, BLOCK // TILE)
    def _(part):
        i = pl.program_id(0) * (BLOCK // TILE) + part
        here = pl.ds(pl.multiple_of(part * TILE, TILE), TILE)

        def add(e, kept):
            total = 0.0
            for k, pair in enumerate(pairs):
                weight = jnp.concatenate([pair[0][e], pair[1][e]], axis=1)
                rows_ref, at = (near_ref, far_ref)[k // 2], k % 2 * LANES
                rows = rows_ref[here, at : at + width]
                total += dot(rows, weight, ((1,), (0,)))
            return jnp.where(mine_of(base, e, i * TILE), total, kept)

        out[here, :] = lax.fori_loop(
            low[i], high[i], add, jnp.zeros((TILE, out.shape[1]), F32)
        ).astype(BF16)


def partial_sums(f, spans, base, quarter, near, far, w_gate, w_up, pieces):
    rows = near.shape[0]
    experts, width, _ = w_gate.shape
    own = pl.BlockSpec((experts, width, UNITS), lambda i, lo, hi, b, q: (0, 0, 2 * q[0] + f))
    block = pl.BlockSpec((experts, width, UNITS), lambda i, *_: (0, 0, 0))
    return pl.pallas_call(
        partial_kernel,
        grid_spec=pltpu.PrefetchScalarGridSpec(
            num_scalar_prefetch=4,
            grid=(rows // BLOCK,),
            in_specs=[pl.BlockSpec((BLOCK, 2 * LANES), lambda i, *_: (i, 0))] * 2 + [own] * 2
            + [block] * len(pieces),
            out_specs=pl.BlockSpec((BLOCK, 2 * UNITS), lambda i, *_: (i, 0)),
        ),
        out_shape=jax.ShapeDtypeStruct((rows, 2 * UNITS), BF16),
        compiler_params=params(),
        cost_estimate=cost(16 * rows * LANES * UNITS, 8 * rows * LANES),
        name="partial_sums",
    )(*spans, base, quarter, near, far, w_gate, w_up, *pieces)


def down_kernel(slots, low, high, base, block, onehot_ref, *refs):
    hidden, start, refs = refs[: 2 * slots], refs[2 * slots], refs[2 * slots + 1 :]
    weights, (out, total_ref, value_ref) = refs[:-3], refs[-3:]
    width = weights[0].shape[1]
    j = pl.program_id(0)
    slot = j // 2

    @pl.when(j == 0)
    def _():
        total_ref[...] = jnp.zeros_like(total_ref) if start is None else start[...]
        value_ref[...] = jnp.zeros_like(value_ref)

    @pl.when(block[3 * slot + 2] != 0)
    def _():
        for part in range(BLOCK // TILE):
            i = (2 * block[3 * slot] + j % 2) * (BLOCK // TILE) + part
            here = slice(part * TILE, (part + 1) * TILE)
            source = 2 * slot + 1 - block[3 * slot + 1]
            units = hidden[0][here, :]
            for k in range(1, 2 * slots):
                units = jnp.where(source == k, hidden[k][here, :], units)

            @pl.loop(low[i], high[i])
            def _(e):
                mine = mine_of(base, e, i * TILE)
                for k, weight in enumerate(weights):
                    value = dot(units, weight[e], ((1,), (1,)))
                    at = slice(k * LANES, k * LANES + width)
                    value_ref[here, at] = jnp.where(
                        mine, value, value_ref[here, at].astype(F32)
                    ).astype(BF16)

        total_ref[...] += dot(onehot_ref[...], value_ref[...], ((1,), (0,)))

    @pl.when(j == pl.num_programs(0) - 1)
    def _():
        out[...] = total_ref[...].astype(out.dtype)


def down_and_mix(spans, base, block, onehot, hidden, start, at, weights, dtype):
    rows, units = hidden[0].shape
    slots = len(hidden) // 2
    count, tokens = len(weights), onehot.shape[0]
    some = [
        pl.BlockSpec((BLOCK, units), lambda j, *_, s=k // 2: (jnp.clip(j - 2 * s, 0, 1), 0))
        for k in range(2 * slots)
    ]
    whole = pl.BlockSpec((tokens, count * LANES), lambda j, *_: (0, 0))
    kernel = functools.partial(down_kernel, slots)
    if start is None:
        kernel = lambda *refs: down_kernel(slots, *refs[: 5 + 2 * slots], None, *refs[5 + 2 * slots :])
    return pl.pallas_call(
        kernel,
        grid_spec=pltpu.PrefetchScalarGridSpec(
            num_scalar_prefetch=4,
            grid=(2 * slots,),
            in_specs=[
                pl.BlockSpec(
                    (tokens, BLOCK), lambda j, lo, hi, b, k: (0, 2 * k[3 * (j // 2)] + j % 2)
                )
            ]
            + some
            + [pl.BlockSpec((tokens, count * LANES), lambda j, *_: (0, at // count))]
            * (start is not None)
            + [pl.BlockSpec(w.shape, lambda j, *_: (0, 0, 0)) for w in weights],
            out_specs=whole,
            scratch_shapes=[
                pltpu.VMEM((tokens, count * LANES), F32),
                pltpu.VMEM((BLOCK, count * LANES), BF16),
            ],
        ),
        out_shape=jax.ShapeDtypeStruct((tokens, count * LANES), dtype),
        compiler_params=params(32),
        cost_estimate=cost(2 * slots * rows * tokens * LANES * count, 2 * slots * rows * tokens),
        name="down_and_mix",
    )(*spans, base, block, onehot, *hidden, *([] if start is None else [start]), *weights)


def fixed_weights(size, tokens, expert_ids, gate_weights, w_gate, w_up, w_down):
    count, picks = expert_ids.shape
    experts, width, hidden_units = w_gate.shape
    quarter = hidden_units // 4
    rows = size * count * picks
    places = size // 4
    me, plane = lax.axis_index("ep"), lax.axis_index("parts")
    w_down = jnp.swapaxes(w_down, 1, 2)

    twins = [(i, i ^ 1) for i in range(size)]
    cross = [(p * size + i, p * size + (i ^ 2 ^ p)) for p in range(2) for i in range(size)]
    to_twin = lambda value: lax.ppermute(value, "ep", twins)
    to_cross = lambda value: lax.ppermute(value, ("parts", "ep"), cross)
    to_plane = lambda value: lax.ppermute(value, "parts", [(0, 1), (1, 0)])
    line = [[4 * p + k for p in range(places)] for k in range(4)]
    my_quarter = me % 4
    twin_quarter = my_quarter ^ 1
    cross_quarter = my_quarter ^ 2 ^ plane

    note = jnp.concatenate([expert_ids.astype(F32), *split3(gate_weights)], axis=1).astype(BF16)
    fill = LANES - width - note.shape[1]
    parcels = jnp.concatenate(
        [
            tokens.reshape(count, size, width).swapaxes(0, 1),
            jnp.broadcast_to(jnp.pad(note, ((0, 0), (0, fill)))[None], (size, count, LANES - width)),
        ],
        axis=2,
    )
    own = lax.all_to_all(parcels, "ep", split_axis=0, concat_axis=0, tiled=True)
    own = own.reshape(size * count, LANES)
    far, near = to_cross(own), [own, to_twin(own)]
    place, across, gates, base = order_of(own, width, picks, experts)
    base = base[0, : experts + 1]
    spans = spans_of(base, rows)
    which = my_quarter.astype(jnp.int32).reshape(1)

    def cut(n, q):
        if n == 4:
            return lax.dynamic_slice_in_dim(w_down, q * quarter, quarter, 2)
        at = q * quarter + n // 2 * UNITS
        return lax.dynamic_slice_in_dim((w_gate, w_up)[n % 2], at, UNITS, 2)

    def after(value, *others):
        return lax.optimization_barrier((value, *others))[0]

    crossed = [to_cross(cut(0, cross_quarter)), to_cross(after(cut(1, cross_quarter), near[1], base))]
    begun = sort_rows(spans, base, across, gates, near, rows, experts)
    beside = [to_plane(after(crossed[0], begun[0]))]
    rest = after(gates, crossed[0])
    near_rows, scale, onehot = sort_rows(spans, base, across, rest, near, rows, experts, begun)
    far = after(far, near_rows)
    far_rows = sort_more(onehot, [far, to_twin(far)])
    scale = lax.dynamic_slice_in_dim(scale, (me // 4) * (rows // places), rows // places, 0)

    for n in range(2, 5):
        crossed.append(to_cross(after(cut(n, cross_quarter), far, *crossed[2:n])))
    twin_of = lambda n: to_twin(cut(n, twin_quarter))

    for n in range(1, 4):
        beside.append(to_plane(after(crossed[n], near_rows, beside[n - 1])))

    def sums_of(f, *first):
        rows_in = after(far_rows, *first)
        pair = slice(2 * f, 2 * f + 2)
        held = [twin_of(2 * f), twin_of(2 * f + 1), *crossed[pair], *beside[pair]]
        return partial_sums(f, spans, base, which, near_rows, rows_in, w_gate, w_up, held)

    def units_of(sums):
        sums = lax.psum_scatter(
            sums, "ep", scatter_dimension=0, axis_index_groups=line, tiled=True
        )
        gate, up = sums[:, :UNITS].astype(F32), sums[:, UNITS:].astype(F32)
        return (jax.nn.silu(gate) * up * scale).astype(BF16)

    sums = sums_of(0, crossed[2])
    later = sums_of(1, sums)
    units = [units_of(sums), units_of(later)]
    held = [twin_of(4), crossed[4], to_plane(crossed[4])]

    place = jnp.broadcast_to(
        after(across[:experts], later)[:, :, None], (experts, size * count, 128)
    )
    columns = scatter_rows(spans, place, rows)
    pieces = [after(cut(4, my_quarter), later), *held]
    units, columns, pieces = lax.optimization_barrier((units, columns, pieces))
    units = jnp.concatenate(units, axis=1)

    spot = me // 4

    def steps(value, step, up):
        links = [
            (4 * p + k, 4 * (p + 1 if up else p - 1) + k)
            for p in (range(step - 1, places - 1) if up else range(1, places - step + 1))
            for k in range(4)
        ]
        return lax.ppermute(value, "ep", links)

    def mix(flags, hidden, start, at=0, count=4, dtype=F32):
        block = jnp.stack([jnp.asarray(flag, jnp.int32) for flag in flags])
        hidden = list(hidden)
        return down_and_mix(
            spans, base, block, columns, hidden, start, at, pieces[at : at + count], dtype
        )

    moving = [steps(units, 1, True), steps(units, 1, False)]
    total, waiting = mix((spot, 1, 1), [units, units], None), []
    for step in range(1, places):
        if step == places - 1:
            if waiting:
                both = [sum(map(tuple, parts), ()) for parts in zip(*waiting)]
                total = mix(*both, total)
        *hidden, total = lax.optimization_barrier((*moving, total))
        came_up, came_down = spot >= step, spot < places - step
        above = jnp.minimum(spot + step, places - 1)
        flags = (jnp.where(came_up, spot - step, above), came_up, came_up | came_down)
        if step == places - 1:
            break
        moving = [steps(hidden[0], step + 1, True), steps(hidden[1], step + 1, False)]
        waiting.append((flags, hidden))
        if 2 * step < places:
            waiting.append(((above, 0, came_up & came_down), hidden))
        if step == 1:
            total = mix(*waiting.pop(0), total)
    far = mix(flags, hidden, total, 2, 2, BF16)
    near = after(total, far)
    far, far_twin = far[:, :width], far[:, LANES : LANES + width]
    far = (far.astype(F32) + to_twin(far_twin).astype(F32)).astype(BF16)
    near, far = lax.optimization_barrier((near, far))
    far = to_cross(far)
    near = mix(flags, hidden, near, 0, 2)
    twin = near[:, LANES : LANES + width].astype(BF16)
    twin = to_twin(after(twin, far)).astype(F32)
    mixed = (near[:, :width] + twin + far.astype(F32)).astype(BF16)
    mixed = lax.all_to_all(
        mixed.reshape(size, count, width), "ep", split_axis=0, concat_axis=0, tiled=True
    )
    return mixed.swapaxes(0, 1).reshape(count, size * width)


def solution(mesh):
    size, inner = mesh.shape["ep"], mesh.shape["tp"]

    def body(tokens, expert_ids, gate_weights, w_gate, w_up, w_down):
        rows = size * math.prod(expert_ids.shape)
        sums = rows * w_gate.shape[2]
        experts, width, units = w_gate.shape
        even = (
            size % 4 == 0
            and size > 4
            and mesh.shape["parts"] == 2
            and rows == size // 4 * 2 * BLOCK
            and units == 8 * UNITS
            and 3 * experts <= UNITS
            and size * math.prod(expert_ids.shape[:1]) % 128 == 0
            and width + 4 * expert_ids.shape[1] <= LANES
        )
        args = (tokens, expert_ids, gate_weights, w_gate, w_up, w_down)
        if inner == 1 and even and sums <= 3 * math.prod(w_gate.shape):
            return fixed_weights(size, *args)
        return moved_weights(*args)

    placed = (
        P(("parts", "ep"), "tp"),
        P(("parts", "ep"), None),
        P(("parts", "ep"), None),
        P(None, "ep", "tp"),
        P(None, "ep", "tp"),
        P(None, "tp", "ep"),
    )
    return jax.shard_map(
        body, mesh=mesh, in_specs=placed, out_specs=P(("parts", "ep"), "tp"), check_vma=False
    )
```
